32 devices in a mesh: branch: 4 (over y, x), seq: 8 (over z, core).
Axes of the slice: x: 2, y: 2, z: 4, core: 2. Of those that a mesh axis runs over, the one named last changes fastest.
Arguments:
- tile_embeddings: bfloat16 [16384, 768], P(('seq', 'branch')), may hold values from -6 to 6
- tile_valid: int32 [16384], replicated, may hold values from 0 to 1, as said below
- slide_bounds: int32 [4], replicated, may hold values from 0 to 16384, as said below
- norm_gain: float32 [2, 2, 768], replicated, may hold values from 0.5 to 1.5
- norm_bias: float32 [2, 2, 768], replicated, may hold values from -3 to 3
- attention_in: bfloat16 [2, 768, 2304], replicated, may hold values from -0.21875 to 0.21875
- attention_out: bfloat16 [2, 768, 768], replicated, may hold values from -6 to 6
- hidden_up: bfloat16 [2, 768, 3072], replicated, may hold values from -0.21875 to 0.21875
- hidden_down: bfloat16 [2, 3072, 768], replicated, may hold values from -0.109375 to 0.109375
- cotangent: bfloat16 [16384, 768], P(('seq', 'branch')), may hold values from -6 to 6
Outputs:
- layer_outputs: bfloat16 [2, 16384, 768], P(None, ('seq', 'branch'))
- grad_embeddings: float32 [16384, 768], P(('seq', 'branch'))
- grad_norm_gain: float32 [2, 2, 768], replicated
- grad_norm_bias: float32 [2, 2, 768], replicated
- grad_attention_in: float32 [2, 768, 2304], replicated
- grad_attention_out: float32 [2, 768, 768], replicated
- grad_hidden_up: float32 [2, 768, 3072], replicated
- grad_hidden_down: float32 [2, 3072, 768], replicated
The draws below stay inside these ranges and needn't reach their ends.
Inputs may be any that keep to these rules, and one draw needn't show every extreme that they name: `slide_bounds`: rises strictly from 0 to 16384; every entry is a multiple of 4096; one slide holds at least half of the tiles. `tile_valid`: 1 marks a tile that holds tissue, 0 a padding or background tile.
All inputs are finite; a program needn't handle non-finite values.
Results may differ from the reference program's by a relative error of at most 0.0095.
Values may be sent and summed in bfloat16 or wider, within the bound.
A program may use at most 384 MiB of HBM per device.

```python
from functools import partial
import jax
import jax.numpy as jnp
from jax import lax

D = 768
H = 16
HD = 48
FF = 3072
SEG = 1024
PAD = 4096
LAYERS = 2
TILES = 16384


def slide_layout(key):
    units = TILES // PAD
    first_key, second_key, third_key = jax.random.split(key, 3)
    largest = jax.random.randint(first_key, (), (units + 1) // 2, units - 1)
    remainder = units - largest
    cut_point = jax.random.randint(second_key, (), 1, remainder)
    placing = jax.random.randint(third_key, (), 0, 3)
    order = jnp.arange(3, dtype=jnp.int32)
    ranking = jnp.clip(order - (order > placing).astype(jnp.int32), 0, 1)
    others = jnp.stack([cut_point, remainder - cut_point])
    counts = jnp.where(order == placing, largest, jnp.take(others, ranking))
    return jnp.concatenate([jnp.zeros((1,), jnp.int32), jnp.cumsum(counts).astype(jnp.int32)]) * PAD


def draw_slide_bounds(key, part):
    return slide_layout(key).astype(jnp.int32)


def draw_tile_valid(key, part):
    bounds = slide_layout(key)
    key = jax.random.fold_in(key, 7)
    trim_key, hole_key = jax.random.split(key)
    trims = jax.random.randint(trim_key, (3,), 0, PAD // 2)
    places = jnp.arange(TILES, dtype=jnp.int32)
    slide_index = jnp.sum((places[:, None] >= bounds[None, 1:3]).astype(jnp.int32), axis=1)
    ends = jnp.take(bounds[1:], slide_index) - jnp.take(trims, slide_index)
    tissue = jax.random.randint(hole_key, (TILES,), 0, 8) != 0
    return ((places < ends) & tissue).astype(jnp.int32)


def block_scale(stream_key, shape, cuts, smallest, high):
    level = 1.0
    for axis_at, shards_of in cuts:
        steps = jax.random.uniform(jax.random.fold_in(jax.random.fold_in(stream_key, 6), axis_at), (shards_of,), jnp.float32, smallest / len(cuts), high / len(cuts))
        level = level * jnp.repeat(jnp.exp(steps), shape[axis_at] // shards_of).reshape((-1,) + (1,) * (len(shape) - 1 - axis_at))
    return level


def bell_draw(rng, shape, deviation, most, cuts=(), kind=jnp.bfloat16):
    level = block_scale(rng, shape, cuts, -0.22, 0.18) if cuts else 1.0
    array = jax.random.normal(rng, shape, jnp.float32) * deviation * level
    return jnp.minimum(jnp.maximum(array, -most), most).astype(kind)


def setup_inputs(seed: int = 0) -> dict:
    keys = jax.random.split(jax.random.key(seed), 11)
    tile_embeddings = bell_draw(keys[0], (TILES, D), 1.0, 6.0, ((0, 32),))
    tile_valid = draw_tile_valid(jax.random.fold_in(keys[10], 71), 0)
    slide_bounds = draw_slide_bounds(jax.random.fold_in(keys[10], 71), 0)
    norm_gain = jnp.clip(1.0 + 0.1 * jax.random.normal(keys[3], (LAYERS, 2, D), jnp.float32), 0.5, 1.5)
    norm_bias = bell_draw(keys[4], (LAYERS, 2, D), 0.5, 3.0, (), jnp.float32)
    attention_in = bell_draw(keys[5], (LAYERS, D, 3 * D), D ** -0.5, 0.21875)
    attention_out = bell_draw(keys[6], (LAYERS, D, D), (max(D // SEG, 1)) ** -0.5, 6.0)
    hidden_up = bell_draw(keys[7], (LAYERS, D, FF), D ** -0.5, 0.21875)
    hidden_down = bell_draw(keys[8], (LAYERS, FF, D), FF ** -0.5, 0.109375)
    cotangent = bell_draw(keys[9], (TILES, D), 1.0, 6.0, ((0, 32),))
    return dict(tile_embeddings=tile_embeddings, tile_valid=tile_valid, slide_bounds=slide_bounds, norm_gain=norm_gain, norm_bias=norm_bias, attention_in=attention_in, attention_out=attention_out, hidden_up=hidden_up, hidden_down=hidden_down, cotangent=cotangent)


ratios = (1, 2, 4, 8, 16)
neg_fill = -1e+30
eps_norm = 1e-05
highest = lax.Precision.HIGHEST

@jax.custom_vjp
def low(v):
    return lax.optimization_barrier(v.astype(jnp.bfloat16)).astype(jnp.float32)

@jax.custom_vjp
def low_back(v):
    return v

def low_keep(v):
    return (low(v), None)

def low_pass(kept, grad):
    return (grad,)

def back_keep(v):
    return (v, None)

def back_low(kept, grad):
    return (low(grad),)
low.defvjp(low_keep, low_pass)
low_back.defvjp(back_keep, back_low)

def layer_norm(stream, gain, shift):
    mean_row = lax.optimization_barrier(jnp.mean(stream, axis=-1, keepdims=True))
    centered = stream - mean_row
    spread = lax.optimization_barrier(jnp.mean(centered * centered, axis=-1, keepdims=True))
    return centered * lax.rsqrt(spread + eps_norm) * gain + shift

def slide_of(places, slide_bounds):
    return lax.optimization_barrier(jnp.sum((places[..., None] >= slide_bounds[1:-1]).astype(jnp.int32), axis=-1))

def sample_heads(source, dilation, segment_size):
    shaped = source.reshape((TILES // segment_size, segment_size // dilation, dilation, H) + source.shape[2:])
    return jnp.stack([shaped[:, :, head_index % dilation, head_index] for head_index in range(H)], axis=2)

def spread_heads(source, dilation, fill):
    widened = jnp.full(source.shape[:2] + (dilation,) + source.shape[2:], fill, dtype=source.dtype)
    for head_index in range(H):
        widened = widened.at[:, :, head_index % dilation, head_index].set(source[:, :, head_index])
    return widened.reshape((TILES,) + source.shape[2:])

def segment_attention(pieces, slide_bounds):
    query_part, key_part, value_part, place_part, live_part = pieces
    score_scale = HD ** (-0.5)
    raw_scores = low_back(jnp.einsum('qhd,khd->hqk', query_part, key_part, precision=highest) * score_scale)
    places = place_part.T
    slides = slide_of(places, slide_bounds)
    allowed = (slides[:, :, None] == slides[:, None, :]) & ((live_part.T[:, None, :] == 1) | (places[:, :, None] == places[:, None, :]))
    masked = jnp.where(allowed, raw_scores, neg_fill)
    row_lse = jax.nn.logsumexp(masked, axis=-1)
    softmax_probs = jnp.exp(masked - row_lse[:, :, None])
    branch_out = jnp.einsum('hqk,khd->qhd', low(softmax_probs), value_part, precision=highest)
    return (low_back(branch_out), row_lse.T)

def branch_attention(queries, key_rows, values, tile_valid, slide_bounds, dilation):
    segment_size = min(SEG * dilation, TILES)
    places = jnp.broadcast_to(jnp.arange(TILES, dtype=jnp.int32)[:, None], (TILES, H))
    live_keys = jnp.broadcast_to(tile_valid[:, None], (TILES, H))
    pieces = (sample_heads(queries, dilation, segment_size), sample_heads(key_rows, dilation, segment_size), sample_heads(values, dilation, segment_size), sample_heads(places, dilation, segment_size), sample_heads(live_keys, dilation, segment_size))
    branch_outs, branch_lses = lax.map(jax.checkpoint(partial(segment_attention, slide_bounds=slide_bounds)), pieces)
    return (spread_heads(branch_outs, dilation, 0.0), spread_heads(branch_lses, dilation, neg_fill))

def dilated_attention(queries, key_rows, values, tile_valid, slide_bounds):
    results = [branch_attention(queries, key_rows, values, tile_valid, slide_bounds, dilation) for dilation in ratios]
    lse_total = jax.nn.logsumexp(jnp.stack([result[1] for result in results]), axis=0)
    combined = jnp.zeros_like(queries)
    for branch_out, branch_lse in results:
        combined = combined + jnp.exp(branch_lse - lse_total)[:, :, None] * branch_out
    return combined

def layer_block(stream, gain, shift, attention_in, attention_out, hidden_up, hidden_down, tile_valid, slide_bounds):
    normed = low(layer_norm(stream, gain[0], shift[0]))
    projected = jnp.dot(normed, attention_in, precision=highest, preferred_element_type=jnp.float32).reshape(TILES, H, 3, HD)
    queries = low(low_back(projected[:, :, 0]))
    key_rows = low(low_back(projected[:, :, 1]))
    values = low(low_back(projected[:, :, 2]))
    attended = dilated_attention(queries, key_rows, values, tile_valid, slide_bounds)
    attended_low = low(low_back(attended.reshape(TILES, D)))
    midway = stream + low_back(jnp.dot(attended_low, attention_out, precision=highest, preferred_element_type=jnp.float32))
    second_normed = low(layer_norm(midway, gain[1], shift[1]))
    pre_act = low_back(jnp.dot(second_normed, hidden_up, precision=highest, preferred_element_type=jnp.float32))
    hidden = low(jax.nn.gelu(pre_act, approximate=False))
    return midway + low_back(jnp.dot(hidden, hidden_down, precision=highest, preferred_element_type=jnp.float32))

def reference(tile_embeddings, tile_valid, slide_bounds, norm_gain, norm_bias, attention_in, attention_out, hidden_up, hidden_down, cotangent):

    def forward(stream, gains, shifts, in_weights, out_weights, up_weights, down_weights):
        outputs = []
        for layer_index in range(LAYERS):
            stream = layer_block(stream, gains[layer_index], shifts[layer_index], in_weights[layer_index], out_weights[layer_index], up_weights[layer_index], down_weights[layer_index], tile_valid, slide_bounds)
            outputs.append(stream)
        return jnp.stack(outputs)
    stacked, pullback = jax.vjp(forward, tile_embeddings.astype(jnp.float32), norm_gain.astype(jnp.float32), norm_bias.astype(jnp.float32), attention_in.astype(jnp.float32), attention_out.astype(jnp.float32), hidden_up.astype(jnp.float32), hidden_down.astype(jnp.float32))
    cotangents = jnp.zeros_like(stacked).at[LAYERS - 1].set(cotangent.astype(jnp.float32))
    gradients = pullback(cotangents)
    return (stacked.astype(jnp.bfloat16), gradients[0], gradients[1], gradients[2], gradients[3], gradients[4], gradients[5], gradients[6])
```

```python
import functools
import numpy as np
import jax
import jax.numpy as jnp
from jax import lax
from jax.experimental import pallas as pl
from jax.experimental.pallas import tpu as pltpu
from jax.sharding import PartitionSpec as P

BLOCK = 1024
CHUNK = 32
ORDER = (0, 8, 4, 12, 2, 10, 6, 14, 1, 9, 5, 13, 3, 11, 7, 15)
ONE, BIAS, HIGH, LOW, VALUE = 48, 51, 52, 57, 64
NEG = -1e30
LOG2E = 1.4426950408889634
LN2 = 0.6931471805599453
F32, BF16 = jnp.float32, jnp.bfloat16


def low_np(x):
    return np.asarray(x, np.float32).astype(jnp.bfloat16).astype(np.float32)


def query_features(classes, level):
    table = np.zeros((len(classes), 128), np.float32)
    table[:, BIAS] = 1.0
    for at, mine in enumerate(classes):
        for theirs in range(5):
            met = min(mine, theirs) - level + 1
            value = np.log2(met) if met > 0 else NEG
            high = low_np(value)
            table[at, HIGH + theirs] = high
            table[at, LOW + theirs] = low_np(value - high) if met > 0 else 0.0
    return table.astype(jnp.bfloat16)


block_classes = [4] * 64 + [3] * 64 + [2] * 128 + [1] * 256 + [0] * 512
upper_classes = [4] * 128 + [3] * 128 + [2] * 256


def key_features():
    table = np.zeros((BLOCK, 128), np.float32)
    table[:, ONE : ONE + 3] = 1.0
    for at, mine in enumerate(block_classes):
        table[at, HIGH + mine] = 1.0
        table[at, LOW + mine] = 1.0
    return table.astype(jnp.bfloat16)


def nt(a, b):
    return lax.dot_general(a, b, (((1,), (1,)), ((), ())), preferred_element_type=F32)


def nn(a, b):
    return lax.dot_general(a, b, (((1,), (0,)), ((), ())), preferred_element_type=F32)


def lanes_of(shape):
    return lax.broadcasted_iota(jnp.int32, shape, len(shape) - 1)


def split3(column):
    high = column.astype(BF16)
    rest = column - high.astype(F32)
    mid = rest.astype(BF16)
    last = (rest - mid.astype(F32)).astype(BF16)
    return high, mid, last


def place3(base, column):
    high, mid, last = split3(column)
    lane = lanes_of(base.shape)
    out = jnp.where(lane == ONE, high.astype(F32), base)
    out = jnp.where(lane == ONE + 1, mid.astype(F32), out)
    return jnp.where(lane == ONE + 2, last.astype(F32), out)


def chunk_row(head, block, position, part, per_dev):
    residue = lax.rem(ORDER[position] + head, 16)
    return pl.multiple_of((2 * block + part) * per_dev + residue * CHUNK, CHUNK)


def prepare_kernel(heads, blocks, first_ref, x_ref, side_ref, place_ref, kf_ref, q_ref, kv_ref, work):
    kf = kf_ref[...]

    for head in range(heads):
        work[...] = nn(x_ref[...], place_ref[head]).astype(BF16)
        which = first_ref[0] + head

        for position in range(16):
            features = kf[position * 64 : position * 64 + CHUNK]
            for block in range(blocks):
                for part in range(2):
                    row = chunk_row(which, block, position, part, 512)
                    at = position * 64 + part * CHUNK
                    source = work[pl.ds(row, CHUNK), :]
                    q_ref[head, block, at : at + CHUNK, :] = source[:, :128]
                    kv_ref[head, block, at : at + CHUNK, :] = (
                        source[:, 128:] + features + side_ref[pl.ds(row, CHUNK), :]
                    )


def prepare(first, rows, side, place, kf):
    heads = place.shape[0]
    total = rows.shape[0]
    blocks = total // BLOCK
    shape = jax.ShapeDtypeStruct((heads, blocks, BLOCK, 128), BF16)
    return pl.pallas_call(
        functools.partial(prepare_kernel, heads, blocks),
        out_shape=(shape, shape),
        in_specs=[pl.BlockSpec(memory_space=pltpu.SMEM)]
        + [pl.BlockSpec(memory_space=pltpu.VMEM)] * 4,
        out_specs=(pl.BlockSpec(memory_space=pltpu.VMEM),) * 2,
        scratch_shapes=[pltpu.VMEM((total, 256), BF16)],
        compiler_params=pltpu.CompilerParams(vmem_limit_bytes=48 * 2**20),
        name="attention_prepare",
    )(first, rows, side, place, kf)


def lower_kernel(q_ref, kv_ref, f0_ref, f1_ref, o_ref):
    step = 256
    for block in range(2):
        own = kv_ref[0, block]
        near = kv_ref[0, 1 - block, :512]
        for at in range(0, BLOCK, step):
            rows = slice(at, at + step)
            base = q_ref[0, block, rows]
            s0 = nt(base + f0_ref[rows], own)
            top = jnp.max(s0, axis=1, keepdims=True)
            if at < 512:
                s1 = nt(base + f1_ref[rows], near)
                top = jnp.maximum(top, jnp.max(s1, axis=1, keepdims=True))
            own_rows = own[rows].astype(F32)
            meet = base.astype(F32) * own_rows
            alone = jnp.sum(meet, axis=1, keepdims=True)
            lane = lanes_of(own_rows.shape)
            bias = jnp.min(jnp.where(lane == BIAS, own_rows, 0.0), axis=1, keepdims=True)
            classes = sum((lax.broadcasted_iota(jnp.int32, (step, 1), 0) + at < edge).astype(F32) for edge in (512, 256, 128, 64))
            alone = jnp.where(bias < 0.0, alone + jnp.log2(classes + 1.0), NEG)
            top = jnp.maximum(top, alone)
            out = nn(jnp.exp2(s0 - top).astype(BF16), own)
            if at < 512:
                out = out + nn(jnp.exp2(s1 - top).astype(BF16), near)
            out = out + jnp.exp2(alone - top) * own_rows
            o_ref[0, block, rows] = jnp.where(lane == 0, top, out)


def lower_forward(q, kv, f0, f1):
    heads, blocks = q.shape[:2]
    spec = pl.BlockSpec((1, 2, BLOCK, 128), lambda h, p: (h, p, 0, 0))
    whole = lambda a: pl.BlockSpec(a.shape, lambda h, p: (0,) * a.ndim)
    return pl.pallas_call(
        lower_kernel,
        grid=(heads, blocks // 2),
        in_specs=[spec, spec, whole(f0), whole(f1)],
        out_specs=spec,
        out_shape=jax.ShapeDtypeStruct(q.shape, F32),
        compiler_params=pltpu.CompilerParams(vmem_limit_bytes=48 * 2**20),
        cost_estimate=pl.CostEstimate(flops=int(heads * blocks * 1.25 * 2**20 * 256 * 4), bytes_accessed=q.size * 8, transcendentals=int(heads * blocks * 1.25 * 2**20)),
        name="attention_lower",
    )(q, kv, f0, f1)


UPPER = ((0, 0, 64), (1, 0, 64), (0, 64, 128), (1, 64, 128), (0, 128, 256), (1, 128, 256))


def gather_upper(ref, lead):
    return jnp.concatenate([ref[(*lead, block, slice(low, high))] for block, low, high in UPPER], axis=0)


def upper_kernel(q_ref, o_ref, r2_ref, r3_ref, r4_ref, f2_ref, f3_ref, f4_ref, att_ref, qb_ref):
    merged = {}
    uq = gather_upper(q_ref, (0,))
    ol = gather_upper(o_ref, (0,))
    for low, high in ((0, 128), (128, 256), (256, 512)):
        base = uq[low:high]
        pairs = [(nt(base + f2_ref[low:high], r2_ref[0, 0]), r2_ref[0, 0])]
        if high <= 256:
            pairs.append((nt(base + f3_ref[low:high], r3_ref[0]), r3_ref[0]))
        if high <= 128:
            pairs.append((nt(base + f4_ref[low:high], r4_ref[0]), r4_ref[0]))
        old = ol[low:high]
        lane = lanes_of(old.shape)
        before = old[:, 0:1]
        top = before
        for scores, keys in pairs:
            top = jnp.maximum(top, jnp.max(scores, axis=1, keepdims=True))
        out = old * jnp.exp2(before - top)
        for scores, keys in pairs:
            out = out + nn(jnp.exp2(scores - top).astype(BF16), keys)
        merged[low] = jnp.where(lane == 0, top, out)
    whole = jnp.concatenate([merged[0], merged[128], merged[256]], axis=0)
    place = 0

    def finish(block, low, high, rows):
        lane = lanes_of(rows.shape)
        top = rows[:, 0:1]
        total = rows[:, ONE : ONE + 1]
        att_ref[0, block, low:high] = jnp.where((lane >= VALUE) & (lane < VALUE + 48), rows / total, 0.0)
        lse = top + jnp.log2(total)
        qb_ref[0, block, low:high] = place3(q_ref[0, block, low:high].astype(F32), -lse).astype(BF16)

    for block, low, high in UPPER:
        finish(block, low, high, whole[place : place + high - low])
        place += high - low
    for block in range(2):
        for low in (256, 512, 768):
            finish(block, low, low + 256, o_ref[0, block, low : low + 256])


def upper_forward(q, o, r2, r3, r4, f2, f3, f4):
    heads, blocks = q.shape[:2]
    spec = pl.BlockSpec((1, 2, BLOCK, 128), lambda h, p: (h, p, 0, 0))
    two = pl.BlockSpec((1, 1, 512, 128), lambda h, p: (h, p, 0, 0))
    far = pl.BlockSpec((1, 512, 128), lambda h, p: (h, 0, 0))
    whole = lambda a: pl.BlockSpec(a.shape, lambda h, p: (0,) * a.ndim)
    return pl.pallas_call(
        upper_kernel,
        grid=(heads, blocks // 2),
        in_specs=[spec, spec, two, far, far, whole(f2), whole(f3), whole(f4)],
        out_specs=(spec, spec),
        out_shape=(jax.ShapeDtypeStruct(q.shape, F32), jax.ShapeDtypeStruct(q.shape, BF16)),
        compiler_params=pltpu.CompilerParams(vmem_limit_bytes=48 * 2**20),
        name="attention_upper",
    )(q, o, r2, r3, r4, f2, f3, f4)


def chunk_place(head, residue, part):
    turn = lax.rem(residue - head + 32, 16)
    position = 8 * lax.rem(turn, 2) + 4 * lax.rem(turn // 2, 2) + 2 * lax.rem(turn // 4, 2) + turn // 8
    return pl.multiple_of(position * 64 + part * CHUNK, CHUNK)


def rows_kernel(heads, blocks, first_ref, a_ref, place_ref, out_ref, work):
    for head in range(heads):
        which = first_ref[0] + head
        for residue in range(16):
            for block in range(blocks):
                for part in range(2):
                    row = (2 * block + part) * 512 + residue * CHUNK
                    at = chunk_place(which, residue, part)
                    work[head, row : row + CHUNK, :] = a_ref[head, block, pl.ds(at, CHUNK), :].astype(BF16)
        value = nn(work[head], place_ref[head])
        if head == 0:
            out_ref[...] = value.astype(BF16)
        else:
            out_ref[...] = out_ref[...] + value.astype(BF16)


def to_rows(first, att, place):
    heads, blocks = att.shape[:2]
    width = place.shape[2]
    total = blocks * BLOCK
    return pl.pallas_call(
        functools.partial(rows_kernel, heads, blocks),
        out_shape=jax.ShapeDtypeStruct((total, width), BF16),
        in_specs=[pl.BlockSpec(memory_space=pltpu.SMEM)]
        + [pl.BlockSpec(memory_space=pltpu.VMEM)] * 2,
        out_specs=pl.BlockSpec(memory_space=pltpu.VMEM),
        scratch_shapes=[pltpu.VMEM((heads, total, 128), BF16)],
        compiler_params=pltpu.CompilerParams(vmem_limit_bytes=48 * 2**20),
        name="attention_rows",
    )(first, att, place)


def prepare_back_kernel(heads, blocks, first_ref, x_ref, place_ref, att_ref, g_ref, work):
    for head in range(heads):
        work[...] = nn(x_ref[...], place_ref[head]).astype(BF16)
        which = first_ref[0] + head
        for position in range(16):
            for block in range(blocks):
                for part in range(2):
                    row = chunk_row(which, block, position, part, 512)
                    at = position * 64 + part * CHUNK
                    g_ref[head, block, at : at + CHUNK, :] = work[pl.ds(row, CHUNK), :]
        for block in range(blocks):
            for at in range(0, BLOCK, 256):
                rows = slice(at, at + 256)
                grad = g_ref[head, block, rows].astype(F32)
                dots = jnp.sum(grad * att_ref[head, block, rows], axis=1, keepdims=True)
                g_ref[head, block, rows] = place3(grad, -dots).astype(BF16)


def prepare_back(first, rows, place, att):
    heads, blocks = att.shape[:2]
    total = blocks * BLOCK
    return pl.pallas_call(
        functools.partial(prepare_back_kernel, heads, blocks),
        out_shape=jax.ShapeDtypeStruct(att.shape, BF16),
        in_specs=[pl.BlockSpec(memory_space=pltpu.SMEM)]
        + [pl.BlockSpec(memory_space=pltpu.VMEM)] * 3,
        out_specs=pl.BlockSpec(memory_space=pltpu.VMEM),
        scratch_shapes=[pltpu.VMEM((total, 128), BF16)],
        compiler_params=pltpu.CompilerParams(vmem_limit_bytes=48 * 2**20),
        name="attention_prepare_back",
    )(first, rows, place, att)


def back_tile(kv, key_t, q_scores, g, q):
    probs = jnp.exp2(nt(kv, q_scores))
    grad_scores = (probs * nt(kv, g)).astype(BF16)
    grad_kv = nn(probs.astype(BF16), g) + nn(grad_scores, q)
    return grad_kv, nn(key_t, grad_scores)


def upper_back_kernel(qb_ref, g_ref, r2_ref, r3_ref, r4_ref, f2_ref, f3_ref, f4_ref, dq_ref, d2_ref, d3_ref, d4_ref):
    uq = gather_upper(qb_ref, (0,))
    ug = gather_upper(g_ref, (0,))
    dq = None
    lane = lanes_of((256, 128))
    for ref, out, f_ref, count in ((r2_ref.at[0], d2_ref.at[0], f2_ref, 512), (r3_ref, d3_ref.at[0], f3_ref, 256), (r4_ref, d4_ref.at[0], f4_ref, 128)):
        q = uq[:count]
        g = ug[:count]
        qs = q + f_ref[...]
        total = None
        for at in range(0, 512, 256):
            kv = ref[0, at : at + 256]
            key_t = kv.astype(F32).T[:48].astype(BF16)
            grad_kv, part = back_tile(kv, key_t, qs, g, q)
            out[0, at : at + 256] = jnp.where(lane < 48, grad_kv * LN2, grad_kv).astype(BF16)
            total = part if total is None else total + part
        rows = total.T
        if count < 512:
            rows = jnp.concatenate([rows, jnp.zeros((512 - count, 48), F32)], axis=0)
        dq = rows if dq is None else dq + rows
    dq_ref[0, 0] = jnp.concatenate([dq, jnp.zeros((512, 80), F32)], axis=1)


def upper_back(qb, g, r2, r3, r4, f2, f3, f4):
    heads, blocks = qb.shape[:2]
    pairs = blocks // 2
    spec = pl.BlockSpec((1, 2, BLOCK, 128), lambda h, p: (h, p, 0, 0))
    two = pl.BlockSpec((1, 1, 512, 128), lambda h, p: (h, p, 0, 0))
    far = pl.BlockSpec((1, 512, 128), lambda h, p: (h, 0, 0))
    whole = lambda a: pl.BlockSpec(a.shape, lambda h, p: (0,) * a.ndim)
    shape = (heads, pairs, 512, 128)
    return pl.pallas_call(
        upper_back_kernel,
        grid=(heads, pairs),
        in_specs=[spec, spec, two, far, far, whole(f2), whole(f3), whole(f4)],
        out_specs=(two,) * 4,
        out_shape=(jax.ShapeDtypeStruct(shape, F32),) + (jax.ShapeDtypeStruct(shape, BF16),) * 3,
        compiler_params=pltpu.CompilerParams(vmem_limit_bytes=48 * 2**20),
        name="attention_upper_back",
    )(qb, g, r2, r3, r4, f2, f3, f4)


def lower_back_kernel(qb_ref, g_ref, kv_ref, f0_ref, f1_ref, dq_ref, dkv_ref):
    step = 256
    lane = lanes_of((step, 128))
    totals = [None, None]
    for block in range(2):
        q = qb_ref[0, block]
        g = g_ref[0, block]
        q0 = q + f0_ref[...]
        far_q = qb_ref[0, 1 - block, :512]
        far_g = g_ref[0, 1 - block, :512]
        far_q1 = far_q + f1_ref[...]
        for at in range(0, BLOCK, step):
            rows = slice(at, at + step)
            kv = kv_ref[0, block, rows]
            key_t = kv.astype(F32).T[:48].astype(BF16)
            grad_kv, part = back_tile(kv, key_t, q0, g, q)
            totals[block] = part if totals[block] is None else totals[block] + part
            if at < 512:
                more_kv, part = back_tile(kv, key_t, far_q1, far_g, far_q)
                grad_kv = grad_kv + more_kv
                part = jnp.concatenate([part, jnp.zeros((48, 512), F32)], axis=1)
                totals[1 - block] = part if totals[1 - block] is None else totals[1 - block] + part
            kv_rows = kv.astype(F32)
            q_rows = q[rows].astype(F32)
            g_rows = g[rows].astype(F32)
            bias = jnp.min(jnp.where(lane == BIAS, kv_rows, 0.0), axis=1, keepdims=True)
            classes = sum((lax.broadcasted_iota(jnp.int32, (step, 1), 0) + at < edge).astype(F32) for edge in (512, 256, 128, 64))
            met = jnp.where(lane < ONE + 3, q_rows * kv_rows, 0.0)
            score = jnp.sum(met, axis=1, keepdims=True) + jnp.log2(classes + 1.0)
            prob = jnp.where(bias < 0.0, jnp.exp2(jnp.where(bias < 0.0, score, NEG)), 0.0)
            grad_score = prob * jnp.sum(jnp.where((lane >= ONE) & (lane != BIAS), g_rows * kv_rows, 0.0), axis=1, keepdims=True)
            grad_kv = grad_kv + prob * g_rows + grad_score * q_rows
            dkv_ref[0, block, rows] = jnp.where(lane < 48, grad_kv * LN2, grad_kv)
            dq_ref[0, block, rows] = grad_score * kv_rows
    for block in range(2):
        for at in range(0, BLOCK, step):
            rows = slice(at, at + step)
            value = totals[block][:, rows].T
            value = jnp.concatenate([value, jnp.zeros((step, 80), F32)], axis=1)
            dq_ref[0, block, rows] = dq_ref[0, block, rows] + value


def lower_back(qb, g, kv, f0, f1):
    heads, blocks = qb.shape[:2]
    spec = pl.BlockSpec((1, 2, BLOCK, 128), lambda h, p: (h, p, 0, 0))
    whole = lambda a: pl.BlockSpec(a.shape, lambda h, p: (0,) * a.ndim)
    return pl.pallas_call(
        lower_back_kernel,
        grid=(heads, blocks // 2),
        in_specs=[spec, spec, spec, whole(f0), whole(f1)],
        out_specs=(spec, spec),
        out_shape=(jax.ShapeDtypeStruct(qb.shape, F32),) * 2,
        compiler_params=pltpu.CompilerParams(vmem_limit_bytes=56 * 2**20),
        cost_estimate=pl.CostEstimate(flops=int(heads * blocks * 1.25 * 2**20 * 256 * 10), bytes_accessed=qb.size * 14, transcendentals=int(heads * blocks * 1.25 * 2**20)),
        name="attention_lower_back",
    )(qb, g, kv, f0, f1)


def rows_back_kernel(heads, blocks, scale, first_ref, dq_ref, du_ref, dkv_ref, x2_ref, place_ref, out_ref, work, sum_q, sum_kv):
    for head in range(heads):
        for block in range(blocks):
            start = 0
            for ub, low, high in UPPER:
                if ub == block % 2:
                    sum_q[head, block, low:high] = dq_ref[head, block, low:high] + du_ref[head, block // 2, start : start + high - low]
                start += high - low
            sum_q[head, block, 256:] = dq_ref[head, block, 256:]
            sum_kv[head, block, :256] = dkv_ref[head, block, :256] + x2_ref[head, block].astype(F32)
            sum_kv[head, block, 256:] = dkv_ref[head, block, 256:]
        which = first_ref[0] + head
        for residue in range(16):
            for block in range(blocks):
                for part in range(2):
                    row = (2 * block + part) * 512 + residue * CHUNK
                    at = chunk_place(which, residue, part)
                    grad_q = sum_q[head, block, pl.ds(at, CHUNK), :]
                    grad_kv = sum_kv[head, block, pl.ds(at, CHUNK), :]
                    lane = lanes_of(grad_q.shape)
                    work[head, row : row + CHUNK, :128] = jnp.where(lane < 48, grad_q * scale, 0.0).astype(BF16)
                    keep = (lane < 48) | ((lane >= VALUE) & (lane < VALUE + 48))
                    work[head, row : row + CHUNK, 128:] = jnp.where(keep, grad_kv, 0.0).astype(BF16)
        value = nn(work[head], place_ref[head])
        if head == 0:
            out_ref[...] = value.astype(BF16)
        else:
            out_ref[...] = out_ref[...] + value.astype(BF16)


def to_rows_back(first, dq, du, dkv, x2, place, scale):
    heads, blocks = dq.shape[:2]
    total = blocks * BLOCK
    return pl.pallas_call(
        functools.partial(rows_back_kernel, heads, blocks, scale),
        out_shape=jax.ShapeDtypeStruct((total, place.shape[2]), BF16),
        in_specs=[pl.BlockSpec(memory_space=pltpu.SMEM)]
        + [pl.BlockSpec(memory_space=pltpu.VMEM)] * 5,
        out_specs=pl.BlockSpec(memory_space=pltpu.VMEM),
        scratch_shapes=[pltpu.VMEM((heads, total, 256), BF16)] + [pltpu.VMEM(dq.shape, F32)] * 2,
        compiler_params=pltpu.CompilerParams(vmem_limit_bytes=56 * 2**20),
        name="attention_rows_back",
    )(first, dq, du, dkv, x2, place)


def placements(heads):
    full = np.zeros((heads, heads * 144, 256), np.float32)
    narrow = np.zeros((heads, heads * 48, 128), np.float32)
    for head in range(heads):
        for at in range(48):
            full[head, head * 144 + at, at] = 1.0
            full[head, head * 144 + 48 + at, 128 + at] = 1.0
            full[head, head * 144 + 96 + at, 128 + VALUE + at] = 1.0
            narrow[head, head * 48 + at, VALUE + at] = 1.0
    return full.astype(jnp.bfloat16), narrow.astype(jnp.bfloat16)


H = 16
SIZE = 48
eps_norm = 1e-05


def exchange(value, axis, bit):
    count = lax.axis_size(axis)
    return lax.ppermute(value, axis, [(at, at ^ (1 << bit)) for at in range(count)])


def to_major(x):
    rows, width = x.shape
    return x.reshape(rows // 16, 16, width).swapaxes(0, 1).reshape(rows, width)


def from_major(x):
    rows, width = x.shape
    return x.reshape(16, rows // 16, width).swapaxes(0, 1).reshape(rows, width)


def normalize(stream):
    centered = stream - jnp.mean(stream, axis=-1, keepdims=True)
    spread = jnp.mean(centered * centered, axis=-1, keepdims=True)
    scale = lax.rsqrt(spread + eps_norm)
    return centered * scale, scale


def normalize_back(stream, gain, e):
    xhat, scale = normalize(stream)
    dxh = e * gain
    back = scale * (dxh - jnp.mean(dxh, axis=-1, keepdims=True) - xhat * jnp.mean(dxh * xhat, axis=-1, keepdims=True))
    return back, jnp.sum(e * xhat, axis=0), jnp.sum(e, axis=0)


def gather_far(kv, geometry):
    blocks, base_bit, same = geometry["blocks"], geometry["bit"], geometry["same"]
    heads = kv.shape[0]
    near = kv[:, :, :256]
    if blocks == 2:
        r2 = exchange(near, "seq", 0)
        group = jnp.concatenate([near, r2], axis=1)
    else:
        r2 = jnp.concatenate([near[:, 2:], near[:, :2]], axis=1)
        group = near
    far3 = group[:, :, :128]
    r3 = exchange(far3, "seq", base_bit)
    far4 = jnp.concatenate([far3[:, :, :64], r3[:, :, :64]], axis=1)
    r4 = exchange(far4, "seq", base_bit + 1)
    bias_lane = lanes_of((1, 1, 1, 128)) == BIAS
    r3 = jnp.where(bias_lane & ~same[1], jnp.asarray(NEG, BF16), r3)
    alike = jnp.repeat(jnp.stack([same[2], same[3]]), 4)[None, :, None, None]
    r4 = jnp.where(bias_lane & ~alike, jnp.asarray(NEG, BF16), r4)
    return (
        r2.reshape(heads, blocks // 2, 512, 128),
        r3.reshape(heads, 512, 128),
        r4.reshape(heads, 512, 128),
    )


def return_far(d2, d3, d4, geometry):
    blocks, base_bit = geometry["blocks"], geometry["bit"]
    heads = d2.shape[0]

    def fold(d):
        return d[:, 0] if d.shape[1] == 1 else jnp.sum(d.astype(F32), axis=1).astype(BF16)

    def add(a, b):
        return (a.astype(F32) + b.astype(F32)).astype(BF16)

    d4 = fold(d4).reshape(heads, 8, 64, 128)
    d3 = fold(d3).reshape(heads, 4, 128, 128)
    d2 = d2.reshape(heads, blocks, 256, 128)
    x4 = exchange(d4, "seq", base_bit + 1)
    pad = jnp.zeros((heads, 4, 64, 128), BF16)
    d3 = add(d3, jnp.concatenate([x4[:, 4:], pad], axis=2))
    x3 = exchange(d3, "seq", base_bit)
    x3 = add(x3, jnp.concatenate([x4[:, :4], pad], axis=2))
    half = jnp.zeros((heads, 4, 128, 128), BF16)
    x3 = jnp.concatenate([x3, half], axis=2)
    if blocks == 2:
        x2 = exchange(add(d2, x3[:, 2:]), "seq", 0)
        return add(x2, x3[:, :2])
    x2 = jnp.concatenate([d2[:, 2:], d2[:, :2]], axis=1)
    return add(x2, x3)


def swap(value):
    return lax.all_to_all(value, "branch", split_axis=0, concat_axis=0, tiled=True)


def dot(spec, a, b):
    return jnp.einsum(spec, a, b, preferred_element_type=F32)


def layer_forward(stream, weights, gain, shift, side, tables, geometry):
    w_in, w_out, w_up, w_down = weights
    first = geometry["first"]
    xhat, _ = normalize(stream)
    normed = (xhat * gain[0] + shift[0]).astype(BF16)
    projected = (dot("td,bdc->btc", normed, w_in) * tables["scale"]).astype(BF16)
    rows = swap(projected)
    rows = rows.reshape(-1, rows.shape[2])
    q, kv = prepare(first, rows, side, tables["full"], tables["kf"])
    r2, r3, r4 = gather_far(kv, geometry)
    o = lower_forward(q, kv, tables["f0"], tables["f1"])
    att, qb = upper_forward(q, o, r2, r3, r4, tables["f2"], tables["f3"], tables["f4"])
    att_rows = to_rows(first, att, tables["wide"])
    att_rows = swap(att_rows.reshape(geometry["branch"], -1, att_rows.shape[1]))
    midway = stream + dot("btc,bcd->td", att_rows, w_out)
    xhat, _ = normalize(midway)
    second = (xhat * gain[1] + shift[1]).astype(BF16)
    pre_act = dot("td,df->tf", second, w_up)
    hidden = jax.nn.gelu(pre_act, approximate=False).astype(BF16)
    result = midway + dot("tf,fd->td", hidden, w_down)
    saved = (stream, normed, kv, r2, r3, r4, qb, att, att_rows, midway, second, pre_act, hidden)
    return result, saved


def layer_backward(gradient, saved, weights, gain, shift, tables, geometry):
    w_in, w_out, w_up, w_down = weights
    stream, normed, kv, r2, r3, r4, qb, att, att_rows, midway, second, pre_act, hidden = saved
    first = geometry["first"]
    down_in = gradient.astype(BF16)
    grad_down = dot("tf,td->fd", hidden, down_in)
    grad_hidden = dot("td,fd->tf", down_in, w_down)
    cdf = 0.5 * (1.0 + lax.erf(pre_act * np.float32(2**-0.5)))
    density = jnp.exp(-0.5 * pre_act * pre_act) * np.float32((2 * np.pi) ** -0.5)
    grad_pre = (grad_hidden * (cdf + pre_act * density)).astype(BF16)
    grad_up = dot("tm,tf->mf", second, grad_pre)
    grad_second = dot("tf,mf->tm", grad_pre, w_up)
    back, gain_two, shift_two = normalize_back(midway, gain[1], grad_second)
    grad_midway = gradient + back
    out_in = grad_midway.astype(BF16)
    grad_out = dot("btc,td->bcd", att_rows, out_in)
    grad_rows = dot("td,bcd->btc", out_in, w_out).astype(BF16)
    grad_rows = swap(grad_rows)
    grad_rows = grad_rows.reshape(-1, grad_rows.shape[2])
    g = prepare_back(first, grad_rows, tables["narrow"], att)
    du, d2, d3, d4 = upper_back(qb, g, r2, r3, r4, tables["f2"], tables["f3"], tables["f4"])
    x2 = return_far(d2, d3, d4, geometry)
    dq, dkv = lower_back(qb, g, kv, tables["f0"], tables["f1"])
    back_rows = to_rows_back(first, dq, du, dkv, x2, tables["back"], SIZE**-0.5)
    projected = swap(back_rows.reshape(geometry["branch"], -1, back_rows.shape[1]))
    grad_in = dot("td,btc->dbc", normed, projected)
    grad_first = dot("btc,bdc->td", projected, w_in)
    back, gain_one, shift_one = normalize_back(stream, gain[0], grad_first)
    width = stream.shape[1]
    grads = (
        jnp.stack([gain_one, gain_two]),
        jnp.stack([shift_one, shift_two]),
        grad_in.reshape(width, -1),
        grad_out.reshape(-1, width),
        grad_up,
        grad_down,
    )
    return grad_midway + back, grads


def local(tile_embeddings, tile_valid, slide_bounds, norm_gain, norm_bias, attention_in, attention_out, hidden_up, hidden_down, cotangent):
    branch = lax.axis_size("branch")
    seq = lax.axis_size("seq")
    heads = H // branch
    rows, width = tile_embeddings.shape
    shard = rows * branch
    blocks = shard // BLOCK
    seq_at = lax.axis_index("seq")
    start = seq_at * shard
    bit = 1 if blocks == 2 else 0

    def slide_at(place):
        return jnp.sum((place >= slide_bounds[1:-1]).astype(jnp.int32))

    def same(mask):
        return slide_at((seq_at ^ mask) * shard) == slide_at(start)

    low, high = 1 << bit, 2 << bit
    geometry = dict(
        branch=branch,
        blocks=blocks,
        bit=bit,
        first=(lax.axis_index("branch") * heads).astype(jnp.int32).reshape(1),
        same=(None, same(low), same(high), same(high | low)),
    )
    full, narrow = placements(heads)
    scale = np.where((np.arange(3 * SIZE * heads) // SIZE) % 3 == 0, LOG2E * SIZE**-0.5, 1.0)
    tables = dict(
        full=jnp.asarray(full),
        back=jnp.asarray(full.astype(np.float32).swapaxes(1, 2).astype(jnp.bfloat16)),
        narrow=jnp.asarray(narrow),
        kf=jnp.asarray(key_features()),
        scale=jnp.asarray(scale, F32),
        f0=jnp.asarray(query_features(block_classes, 0)),
        f1=jnp.asarray(query_features(block_classes[:512], 1)),
        f2=jnp.asarray(query_features(upper_classes, 2)),
        f3=jnp.asarray(query_features(upper_classes[:256], 3)),
        f4=jnp.asarray(query_features(upper_classes[:128], 4)),
    )
    tables["wide"] = jnp.asarray(narrow.astype(np.float32).swapaxes(1, 2).astype(jnp.bfloat16))
    valid = lax.dynamic_slice_in_dim(tile_valid, start, shard)
    valid = valid.reshape(branch, rows // 16, 16).swapaxes(1, 2).reshape(shard, 1)
    side = jnp.where((lanes_of((1, 128)) == BIAS) & (valid != 1), NEG, 0.0).astype(BF16)

    layers = attention_in.shape[0]
    weights = [
        (
            attention_in[layer].reshape(width, branch, -1).swapaxes(0, 1),
            attention_out[layer].reshape(branch, -1, width),
            hidden_up[layer],
            hidden_down[layer],
        )
        for layer in range(layers)
    ]
    stream = to_major(tile_embeddings).astype(F32)
    outputs, saved_all = [], []
    for layer in range(layers):
        stream, saved = layer_forward(stream, weights[layer], norm_gain[layer], norm_bias[layer], side, tables, geometry)
        outputs.append(from_major(stream.astype(BF16)))
        saved_all.append(saved)
    gradient = to_major(cotangent).astype(F32)
    per_layer = [None] * layers
    for layer in reversed(range(layers)):
        gradient, per_layer[layer] = layer_backward(gradient, saved_all[layer], weights[layer], norm_gain[layer], norm_bias[layer], tables, geometry)
    summed = sum_gradients(per_layer)
    return (jnp.stack(outputs), from_major(gradient)) + summed


BOTH = ("branch", "seq")


def sum_gradients(per_layer):
    stacked = [jnp.stack([grads[member] for grads in per_layer]) for member in range(6)]
    out = []
    for member, part in enumerate(stacked):
        dim = 2 if member < 2 else 1
        share = lax.psum_scatter(part, BOTH, scatter_dimension=dim, tiled=True).astype(BF16)
        out.append(lax.all_gather(share, BOTH, axis=dim, tiled=True).astype(F32))
    return tuple(out)


def solution(mesh):
    split = P(("seq", "branch"), None)
    in_specs = (split,) + (P(),) * 8 + (split,)
    out_specs = (P(None, ("seq", "branch"), None), split) + (P(),) * 6
    return jax.shard_map(local, mesh=mesh, in_specs=in_specs, out_specs=out_specs, check_vma=False)
```

```python
import functools
import numpy as np
import jax
import jax.numpy as jnp
from jax import lax
from jax.experimental import pallas as pl
from jax.experimental.pallas import tpu as pltpu
from jax.sharding import PartitionSpec as P

BLOCK = 1024
CHUNK = 32
ORDER = (0, 8, 4, 12, 2, 10, 6, 14, 1, 9, 5, 13, 3, 11, 7, 15)
ONE, BIAS, HIGH, LOW, VALUE = 48, 51, 52, 57, 64
NEG = -1e30
LOG2E = 1.4426950408889634
LN2 = 0.6931471805599453
F32, BF16 = jnp.float32, jnp.bfloat16


def low_np(x):
    return np.asarray(x, np.float32).astype(jnp.bfloat16).astype(np.float32)


def query_features(classes, level):
    table = np.zeros((len(classes), 128), np.float32)
    table[:, BIAS] = 1.0
    for at, mine in enumerate(classes):
        for theirs in range(5):
            met = min(mine, theirs) - level + 1
            value = np.log2(met) if met > 0 else NEG
            high = low_np(value)
            table[at, HIGH + theirs] = high
            table[at, LOW + theirs] = low_np(value - high) if met > 0 else 0.0
    return table.astype(jnp.bfloat16)


block_classes = [4] * 64 + [3] * 64 + [2] * 128 + [1] * 256 + [0] * 512
upper_classes = [4] * 128 + [3] * 128 + [2] * 256


def key_features():
    table = np.zeros((BLOCK, 128), np.float32)
    table[:, ONE : ONE + 3] = 1.0
    for at, mine in enumerate(block_classes):
        table[at, HIGH + mine] = 1.0
        table[at, LOW + mine] = 1.0
    return table.astype(jnp.bfloat16)


def nt(a, b):
    return lax.dot_general(a, b, (((1,), (1,)), ((), ())), preferred_element_type=F32)


def nn(a, b):
    return lax.dot_general(a, b, (((1,), (0,)), ((), ())), preferred_element_type=F32)


def lanes_of(shape):
    return lax.broadcasted_iota(jnp.int32, shape, len(shape) - 1)


def split3(column):
    high = column.astype(BF16)
    rest = column - high.astype(F32)
    mid = rest.astype(BF16)
    last = (rest - mid.astype(F32)).astype(BF16)
    return high, mid, last


def place3(base, column):
    high, mid, last = split3(column)
    lane = lanes_of(base.shape)
    out = jnp.where(lane == ONE, high.astype(F32), base)
    out = jnp.where(lane == ONE + 1, mid.astype(F32), out)
    return jnp.where(lane == ONE + 2, last.astype(F32), out)


def chunk_row(head, block, position, part, per_dev):
    residue = lax.rem(ORDER[position] + head, 16)
    return pl.multiple_of((2 * block + part) * per_dev + residue * CHUNK, CHUNK)


def prepare_kernel(heads, blocks, first_ref, x_ref, side_ref, place_ref, kf_ref, q_ref, kv_ref, work):
    kf = kf_ref[...]

    for head in range(heads):
        for part in range(x_ref.shape[0]):
            work[part * 512 : part * 512 + 512] = nn(x_ref[part], place_ref[head]).astype(BF16)
        which = first_ref[0] + head

        for position in range(16):
            features = kf[position * 64 : position * 64 + CHUNK]
            for block in range(blocks):
                for part in range(2):
                    row = chunk_row(which, block, position, part, 512)
                    at = position * 64 + part * CHUNK
                    source = work[pl.ds(row, CHUNK), :]
                    q_ref[head, block, at : at + CHUNK, :] = source[:, :128]
                    kv_ref[head, block, at : at + CHUNK, :] = (
                        source[:, 128:] + features + side_ref[pl.ds(row, CHUNK), :]
                    )


def prepare(first, rows, side, place, kf):
    heads = place.shape[0]
    total = rows.shape[0] * rows.shape[1]
    blocks = total // BLOCK
    shape = jax.ShapeDtypeStruct((heads, blocks, BLOCK, 128), BF16)
    return pl.pallas_call(
        functools.partial(prepare_kernel, heads, blocks),
        out_shape=(shape, shape),
        in_specs=[pl.BlockSpec(memory_space=pltpu.SMEM)]
        + [pl.BlockSpec(memory_space=pltpu.VMEM)] * 4,
        out_specs=(pl.BlockSpec(memory_space=pltpu.VMEM),) * 2,
        scratch_shapes=[pltpu.VMEM((total, 256), BF16)],
        compiler_params=pltpu.CompilerParams(vmem_limit_bytes=48 * 2**20),
        name="attention_prepare",
    )(first, rows, side, place, kf)


def lower_kernel(q_ref, kv_ref, f0_ref, f1_ref, *refs):
    o_ref = refs[-1]
    step = 256
    for block in range(2):
        own = kv_ref[0, block]
        near = kv_ref[0, 1 - block, :512]
        for at in range(0, BLOCK, step):
            rows = slice(at, at + step)
            base = q_ref[0, block, rows]
            s0 = nt(base + f0_ref[rows], own)
            top = jnp.max(s0, axis=1, keepdims=True)
            if at < 512:
                s1 = nt(base + f1_ref[rows], near)
                top = jnp.maximum(top, jnp.max(s1, axis=1, keepdims=True))
            own_rows = own[rows].astype(F32)
            meet = base.astype(F32) * own_rows
            alone = jnp.sum(meet, axis=1, keepdims=True)
            lane = lanes_of(own_rows.shape)
            bias = jnp.min(jnp.where(lane == BIAS, own_rows, 0.0), axis=1, keepdims=True)
            classes = sum((lax.broadcasted_iota(jnp.int32, (step, 1), 0) + at < edge).astype(F32) for edge in (512, 256, 128, 64))
            alone = jnp.where(bias < 0.0, alone + jnp.log2(classes + 1.0), NEG)
            top = jnp.maximum(top, alone)
            out = nn(jnp.exp2(s0 - top).astype(BF16), own)
            if at < 512:
                out = out + nn(jnp.exp2(s1 - top).astype(BF16), near)
            out = out + jnp.exp2(alone - top) * own_rows
            o_ref[0, block, rows] = jnp.where(lane == 0, top, out)


def part_call(kernel, name, operands, tables, outs, part, parts, base, cost):
    heads, blocks = operands[0].shape[:2]
    count = heads // parts
    spec = pl.BlockSpec((1, 2, BLOCK, 128), lambda h, p: (h + part * count, p, 0, 0))
    whole = lambda a: pl.BlockSpec(a.shape, lambda h, p: (0,) * a.ndim)
    ins = [spec] * len(operands) + [whole(table) for table in tables]
    arrays = list(operands) + list(tables)
    aliases = {}
    if base is not None:
        for at, array in enumerate(base):
            aliases[len(arrays)] = at
            arrays.append(array)
            ins.append(pl.BlockSpec(memory_space=pl.ANY))
    pairs = int(count * blocks * 1.25 * 2**20)
    return pl.pallas_call(
        kernel,
        grid=(count, blocks // 2),
        in_specs=ins,
        out_specs=(spec,) * outs,
        out_shape=(jax.ShapeDtypeStruct(operands[0].shape, F32),) * outs,
        input_output_aliases=aliases,
        compiler_params=pltpu.CompilerParams(vmem_limit_bytes=56 * 2**20),
        cost_estimate=pl.CostEstimate(flops=pairs * 256 * cost, bytes_accessed=operands[0].size * 8 // parts, transcendentals=pairs),
        name=name,
    )(*arrays)


def lower_forward(q, kv, f0, f1, part, parts, base):
    out = part_call(lower_kernel, "attention_lower", (q, kv), (f0, f1), 1, part, parts, None if base is None else (base,), 4)
    return out[0]


UPPER = ((0, 0, 64), (1, 0, 64), (0, 64, 128), (1, 64, 128), (0, 128, 256), (1, 128, 256))


def gather_upper(ref, lead):
    return jnp.concatenate([ref[(*lead, block, slice(low, high))] for block, low, high in UPPER], axis=0)


def upper_kernel(q_ref, o_ref, r2_ref, r3_ref, r4_ref, f2_ref, f3_ref, f4_ref, att_ref, qb_ref):
    merged = {}
    uq = gather_upper(q_ref, (0,))
    ol = gather_upper(o_ref, (0,))
    for low, high in ((0, 128), (128, 256), (256, 512)):
        base = uq[low:high]
        pairs = [(nt(base + f2_ref[low:high], r2_ref[0, 0]), r2_ref[0, 0])]
        if high <= 256:
            pairs.append((nt(base + f3_ref[low:high], r3_ref[0]), r3_ref[0]))
        if high <= 128:
            pairs.append((nt(base + f4_ref[low:high], r4_ref[0]), r4_ref[0]))
        old = ol[low:high]
        lane = lanes_of(old.shape)
        before = old[:, 0:1]
        top = before
        for scores, keys in pairs:
            top = jnp.maximum(top, jnp.max(scores, axis=1, keepdims=True))
        out = old * jnp.exp2(before - top)
        for scores, keys in pairs:
            out = out + nn(jnp.exp2(scores - top).astype(BF16), keys)
        merged[low] = jnp.where(lane == 0, top, out)
    whole = jnp.concatenate([merged[0], merged[128], merged[256]], axis=0)
    place = 0

    def finish(block, low, high, rows):
        lane = lanes_of(rows.shape)
        top = rows[:, 0:1]
        total = rows[:, ONE : ONE + 1]
        att_ref[0, block, low:high] = jnp.where((lane >= VALUE) & (lane < VALUE + 48), rows / total, 0.0)
        lse = top + jnp.log2(total)
        qb_ref[0, block, low:high] = place3(q_ref[0, block, low:high].astype(F32), -lse).astype(BF16)

    for block, low, high in UPPER:
        finish(block, low, high, whole[place : place + high - low])
        place += high - low
    for block in range(2):
        for low in (256, 512, 768):
            finish(block, low, low + 256, o_ref[0, block, low : low + 256])


def upper_forward(q, o, r2, r3, r4, f2, f3, f4):
    heads, blocks = q.shape[:2]
    spec = pl.BlockSpec((1, 2, BLOCK, 128), lambda h, p: (h, p, 0, 0))
    two = pl.BlockSpec((1, 1, 512, 128), lambda h, p: (h, p, 0, 0))
    far = pl.BlockSpec((1, 512, 128), lambda h, p: (h, 0, 0))
    whole = lambda a: pl.BlockSpec(a.shape, lambda h, p: (0,) * a.ndim)
    return pl.pallas_call(
        upper_kernel,
        grid=(heads, blocks // 2),
        in_specs=[spec, spec, two, far, far, whole(f2), whole(f3), whole(f4)],
        out_specs=(spec, spec),
        out_shape=(jax.ShapeDtypeStruct(q.shape, F32), jax.ShapeDtypeStruct(q.shape, BF16)),
        compiler_params=pltpu.CompilerParams(vmem_limit_bytes=48 * 2**20),
        name="attention_upper",
    )(q, o, r2, r3, r4, f2, f3, f4)


def chunk_place(head, residue, part):
    turn = lax.rem(residue - head + 32, 16)
    position = 8 * lax.rem(turn, 2) + 4 * lax.rem(turn // 2, 2) + 2 * lax.rem(turn // 4, 2) + turn // 8
    return pl.multiple_of(position * 64 + part * CHUNK, CHUNK)


def rows_kernel(heads, blocks, first_ref, a_ref, place_ref, out_ref, work):
    for head in range(heads):
        which = first_ref[0] + head
        for residue in range(16):
            for block in range(blocks):
                for part in range(2):
                    row = (2 * block + part) * 512 + residue * CHUNK
                    at = chunk_place(which, residue, part)
                    work[head, row : row + CHUNK, :] = a_ref[head, block, pl.ds(at, CHUNK), :].astype(BF16)
        for part in range(out_ref.shape[0]):
            value = nn(work[head, part * 512 : part * 512 + 512], place_ref[head]).astype(BF16)
            out_ref[part] = value if head == 0 else out_ref[part] + value


def to_rows(first, att, place):
    heads, blocks = att.shape[:2]
    width = place.shape[2]
    total = blocks * BLOCK
    return pl.pallas_call(
        functools.partial(rows_kernel, heads, blocks),
        out_shape=jax.ShapeDtypeStruct((total // 512, 512, width), BF16),
        in_specs=[pl.BlockSpec(memory_space=pltpu.SMEM)]
        + [pl.BlockSpec(memory_space=pltpu.VMEM)] * 2,
        out_specs=pl.BlockSpec(memory_space=pltpu.VMEM),
        scratch_shapes=[pltpu.VMEM((heads, total, 128), BF16)],
        compiler_params=pltpu.CompilerParams(vmem_limit_bytes=48 * 2**20),
        name="attention_rows",
    )(first, att, place)


def prepare_back_kernel(heads, blocks, first_ref, x_ref, place_ref, att_ref, g_ref, work):
    for head in range(heads):
        for part in range(x_ref.shape[0]):
            work[part * 512 : part * 512 + 512] = nn(x_ref[part], place_ref[head]).astype(BF16)
        which = first_ref[0] + head
        for position in range(16):
            for block in range(blocks):
                for part in range(2):
                    row = chunk_row(which, block, position, part, 512)
                    at = position * 64 + part * CHUNK
                    g_ref[head, block, at : at + CHUNK, :] = work[pl.ds(row, CHUNK), :]
        for block in range(blocks):
            for at in range(0, BLOCK, 256):
                rows = slice(at, at + 256)
                grad = g_ref[head, block, rows].astype(F32)
                dots = jnp.sum(grad * att_ref[head, block, rows], axis=1, keepdims=True)
                g_ref[head, block, rows] = place3(grad, -dots).astype(BF16)


def prepare_back(first, rows, place, att):
    heads, blocks = att.shape[:2]
    total = blocks * BLOCK
    return pl.pallas_call(
        functools.partial(prepare_back_kernel, heads, blocks),
        out_shape=jax.ShapeDtypeStruct(att.shape, BF16),
        in_specs=[pl.BlockSpec(memory_space=pltpu.SMEM)]
        + [pl.BlockSpec(memory_space=pltpu.VMEM)] * 3,
        out_specs=pl.BlockSpec(memory_space=pltpu.VMEM),
        scratch_shapes=[pltpu.VMEM((total, 128), BF16)],
        compiler_params=pltpu.CompilerParams(vmem_limit_bytes=48 * 2**20),
        name="attention_prepare_back",
    )(first, rows, place, att)


def back_tile(kv, key_t, q_scores, g, q):
    probs = jnp.exp2(nt(kv, q_scores))
    grad_scores = (probs * nt(kv, g)).astype(BF16)
    grad_kv = nn(probs.astype(BF16), g) + nn(grad_scores, q)
    return grad_kv, nn(key_t, grad_scores)


def upper_back_kernel(qb_ref, g_ref, r2_ref, r3_ref, r4_ref, f2_ref, f3_ref, f4_ref, dq_ref, d2_ref, d3_ref, d4_ref):
    uq = gather_upper(qb_ref, (0,))
    ug = gather_upper(g_ref, (0,))
    dq = None
    lane = lanes_of((256, 128))
    for ref, out, f_ref, count in ((r2_ref.at[0], d2_ref.at[0], f2_ref, 512), (r3_ref, d3_ref.at[0], f3_ref, 256), (r4_ref, d4_ref.at[0], f4_ref, 128)):
        q = uq[:count]
        g = ug[:count]
        qs = q + f_ref[...]
        total = None
        for at in range(0, 512, 256):
            kv = ref[0, at : at + 256]
            key_t = kv.astype(F32).T[:48].astype(BF16)
            grad_kv, part = back_tile(kv, key_t, qs, g, q)
            out[0, at : at + 256] = jnp.where(lane < 48, grad_kv * LN2, grad_kv).astype(BF16)
            total = part if total is None else total + part
        rows = total.T
        if count < 512:
            rows = jnp.concatenate([rows, jnp.zeros((512 - count, 48), F32)], axis=0)
        dq = rows if dq is None else dq + rows
    dq_ref[0, 0] = jnp.concatenate([dq, jnp.zeros((512, 80), F32)], axis=1)


def upper_back(qb, g, r2, r3, r4, f2, f3, f4):
    heads, blocks = qb.shape[:2]
    pairs = blocks // 2
    spec = pl.BlockSpec((1, 2, BLOCK, 128), lambda h, p: (h, p, 0, 0))
    two = pl.BlockSpec((1, 1, 512, 128), lambda h, p: (h, p, 0, 0))
    far = pl.BlockSpec((1, 512, 128), lambda h, p: (h, 0, 0))
    whole = lambda a: pl.BlockSpec(a.shape, lambda h, p: (0,) * a.ndim)
    shape = (heads, pairs, 512, 128)
    return pl.pallas_call(
        upper_back_kernel,
        grid=(heads, pairs),
        in_specs=[spec, spec, two, far, far, whole(f2), whole(f3), whole(f4)],
        out_specs=(two,) * 4,
        out_shape=(jax.ShapeDtypeStruct(shape, F32),) + (jax.ShapeDtypeStruct(shape, BF16),) * 3,
        compiler_params=pltpu.CompilerParams(vmem_limit_bytes=48 * 2**20),
        name="attention_upper_back",
    )(qb, g, r2, r3, r4, f2, f3, f4)


def lower_back_kernel(qb_ref, g_ref, kv_ref, f0_ref, f1_ref, *refs):
    dq_ref, dkv_ref = refs[-2:]
    step = 256
    lane = lanes_of((step, 128))
    totals = [None, None]
    for block in range(2):
        q = qb_ref[0, block]
        g = g_ref[0, block]
        q0 = q + f0_ref[...]
        far_q = qb_ref[0, 1 - block, :512]
        far_g = g_ref[0, 1 - block, :512]
        far_q1 = far_q + f1_ref[...]
        for at in range(0, BLOCK, step):
            rows = slice(at, at + step)
            kv = kv_ref[0, block, rows]
            key_t = kv.astype(F32).T[:48].astype(BF16)
            grad_kv, part = back_tile(kv, key_t, q0, g, q)
            totals[block] = part if totals[block] is None else totals[block] + part
            if at < 512:
                more_kv, part = back_tile(kv, key_t, far_q1, far_g, far_q)
                grad_kv = grad_kv + more_kv
                part = jnp.concatenate([part, jnp.zeros((48, 512), F32)], axis=1)
                totals[1 - block] = part if totals[1 - block] is None else totals[1 - block] + part
            kv_rows = kv.astype(F32)
            q_rows = q[rows].astype(F32)
            g_rows = g[rows].astype(F32)
            bias = jnp.min(jnp.where(lane == BIAS, kv_rows, 0.0), axis=1, keepdims=True)
            classes = sum((lax.broadcasted_iota(jnp.int32, (step, 1), 0) + at < edge).astype(F32) for edge in (512, 256, 128, 64))
            met = jnp.where(lane < ONE + 3, q_rows * kv_rows, 0.0)
            score = jnp.sum(met, axis=1, keepdims=True) + jnp.log2(classes + 1.0)
            prob = jnp.where(bias < 0.0, jnp.exp2(jnp.where(bias < 0.0, score, NEG)), 0.0)
            grad_score = prob * jnp.sum(jnp.where((lane >= ONE) & (lane != BIAS), g_rows * kv_rows, 0.0), axis=1, keepdims=True)
            grad_kv = grad_kv + prob * g_rows + grad_score * q_rows
            dkv_ref[0, block, rows] = jnp.where(lane < 48, grad_kv * LN2, grad_kv)
            dq_ref[0, block, rows] = grad_score * kv_rows
    for block in range(2):
        for at in range(0, BLOCK, step):
            rows = slice(at, at + step)
            value = totals[block][:, rows].T
            value = jnp.concatenate([value, jnp.zeros((step, 80), F32)], axis=1)
            dq_ref[0, block, rows] = dq_ref[0, block, rows] + value


def lower_back(qb, g, kv, f0, f1, part, parts, base):
    return part_call(lower_back_kernel, "attention_lower_back", (qb, g, kv), (f0, f1), 2, part, parts, base, 10)


def rows_back_kernel(heads, blocks, scale, first_ref, dq_ref, du_ref, dkv_ref, x2_ref, place_ref, out_ref, work, sum_q, sum_kv):
    for head in range(heads):
        for block in range(blocks):
            start = 0
            for ub, low, high in UPPER:
                if ub == block % 2:
                    sum_q[head, block, low:high] = dq_ref[head, block, low:high] + du_ref[head, block // 2, start : start + high - low]
                start += high - low
            sum_q[head, block, 256:] = dq_ref[head, block, 256:]
            sum_kv[head, block, :256] = dkv_ref[head, block, :256] + x2_ref[head, block].astype(F32)
            sum_kv[head, block, 256:] = dkv_ref[head, block, 256:]
        which = first_ref[0] + head
        for residue in range(16):
            for block in range(blocks):
                for part in range(2):
                    row = (2 * block + part) * 512 + residue * CHUNK
                    at = chunk_place(which, residue, part)
                    grad_q = sum_q[head, block, pl.ds(at, CHUNK), :]
                    grad_kv = sum_kv[head, block, pl.ds(at, CHUNK), :]
                    lane = lanes_of(grad_q.shape)
                    work[head, row : row + CHUNK, :128] = jnp.where(lane < 48, grad_q * scale, 0.0).astype(BF16)
                    keep = (lane < 48) | ((lane >= VALUE) & (lane < VALUE + 48))
                    work[head, row : row + CHUNK, 128:] = jnp.where(keep, grad_kv, 0.0).astype(BF16)
        for part in range(out_ref.shape[0]):
            value = nn(work[head, part * 512 : part * 512 + 512], place_ref[head]).astype(BF16)
            out_ref[part] = value if head == 0 else out_ref[part] + value


def to_rows_back(first, dq, du, dkv, x2, place, scale):
    heads, blocks = dq.shape[:2]
    total = blocks * BLOCK
    return pl.pallas_call(
        functools.partial(rows_back_kernel, heads, blocks, scale),
        out_shape=jax.ShapeDtypeStruct((total // 512, 512, place.shape[2]), BF16),
        in_specs=[pl.BlockSpec(memory_space=pltpu.SMEM)]
        + [pl.BlockSpec(memory_space=pltpu.VMEM)] * 5,
        out_specs=pl.BlockSpec(memory_space=pltpu.VMEM),
        scratch_shapes=[pltpu.VMEM((heads, total, 256), BF16)] + [pltpu.VMEM(dq.shape, F32)] * 2,
        compiler_params=pltpu.CompilerParams(vmem_limit_bytes=56 * 2**20),
        name="attention_rows_back",
    )(first, dq, du, dkv, x2, place)


def placements(heads):
    full = np.zeros((heads, heads * 144, 256), np.float32)
    narrow = np.zeros((heads, heads * 48, 128), np.float32)
    for head in range(heads):
        for at in range(48):
            full[head, head * 144 + at, at] = 1.0
            full[head, head * 144 + 48 + at, 128 + at] = 1.0
            full[head, head * 144 + 96 + at, 128 + VALUE + at] = 1.0
            narrow[head, head * 48 + at, VALUE + at] = 1.0
    return full.astype(jnp.bfloat16), narrow.astype(jnp.bfloat16)


H = 16
SIZE = 48
eps_norm = 1e-05


def exchange(value, axis, bit):
    count = lax.axis_size(axis)
    return lax.ppermute(value, axis, [(at, at ^ (1 << bit)) for at in range(count)])


def to_major(x):
    rows, width = x.shape
    return x.reshape(rows // 16, 16, width).swapaxes(0, 1).reshape(rows, width)


def from_major(x):
    rows, width = x.shape
    return x.reshape(16, rows // 16, width).swapaxes(0, 1).reshape(rows, width)


def normalize(stream):
    centered = stream - jnp.mean(stream, axis=-1, keepdims=True)
    spread = jnp.mean(centered * centered, axis=-1, keepdims=True)
    scale = lax.rsqrt(spread + eps_norm)
    return centered * scale, scale


def normalize_back(stream, gain, e):
    xhat, scale = normalize(stream)
    dxh = e * gain
    back = scale * (dxh - jnp.mean(dxh, axis=-1, keepdims=True) - xhat * jnp.mean(dxh * xhat, axis=-1, keepdims=True))
    return back, jnp.sum(e * xhat, axis=0), jnp.sum(e, axis=0)


class Task:
    def __init__(self, steps):
        self.steps = steps
        self.pending, self.result, self.done = None, None, False
        self.advance(None)

    def advance(self, value):
        try:
            self.pending = self.steps.send(value)
        except StopIteration as stop:
            self.result, self.pending, self.done = stop.value, None, True


def start(tasks, ins):
    tasks = [task for task in tasks if not task.done]
    operands = [task.pending[0] for task in tasks]
    operands, ins = lax.optimization_barrier((operands, ins))
    flights = [(task, jax.tree.map(lambda v: exchange(v, *task.pending[1:]), operand)) for task, operand in zip(tasks, operands)]
    return flights, ins


def land(flights, outs):
    if flights:
        values, _ = lax.optimization_barrier(([value for _, value in flights], outs))
        for (task, _), value in zip(flights, values):
            task.advance(value)


def gather_far(kv, geometry):
    blocks, same = geometry["blocks"], geometry["same"]
    heads = kv.shape[0]
    own2, own3, own4 = kv[:, :, :256], kv[:, :, :128], kv[:, :, :64]
    if blocks == 2:
        a3 = yield own3, "seq", 1
        a4 = yield jnp.concatenate([own4, a3[:, :, :64]], axis=1), "seq", 2
        r2, b3, b4 = yield (own2, a3, a4), "seq", 0
        r3 = jnp.concatenate([a3, b3], axis=1)
        r4 = jnp.concatenate([a4[:, :2], b4[:, :2], a4[:, 2:], b4[:, 2:]], axis=1)
    else:
        r2 = jnp.concatenate([own2[:, 2:], own2[:, :2]], axis=1)
        r3 = yield own3, "seq", 0
        r4 = yield jnp.concatenate([own4, r3[:, :, :64]], axis=1), "seq", 1
    bias_lane = lanes_of((1, 1, 1, 128)) == BIAS
    r3 = jnp.where(bias_lane & ~same[1], jnp.asarray(NEG, BF16), r3)
    alike = jnp.repeat(jnp.stack([same[2], same[3]]), 4)[None, :, None, None]
    r4 = jnp.where(bias_lane & ~alike, jnp.asarray(NEG, BF16), r4)
    return (
        r2.reshape(heads, blocks // 2, 512, 128),
        r3.reshape(heads, 512, 128),
        r4.reshape(heads, 512, 128),
    )


def return_far(d2, d3, d4, geometry):
    blocks = geometry["blocks"]
    heads = d2.shape[0]

    def fold(d):
        return d[:, 0] if d.shape[1] == 1 else jnp.sum(d.astype(F32), axis=1).astype(BF16)

    def add(a, b):
        return (a.astype(F32) + b.astype(F32)).astype(BF16)

    def grow(d):
        return jnp.concatenate([d, jnp.zeros_like(d)], axis=2)

    d4 = fold(d4).reshape(heads, 8, 64, 128)
    d3 = fold(d3).reshape(heads, 4, 128, 128)
    d2 = d2.reshape(heads, blocks, 256, 128)
    if blocks == 2:
        b4 = jnp.concatenate([d4[:, 2:4], d4[:, 6:8]], axis=1)
        a4 = jnp.concatenate([d4[:, 0:2], d4[:, 4:6]], axis=1)
        x2, y3, y4 = yield (d2, d3[:, 2:], b4), "seq", 0
        x4 = yield add(a4, y4), "seq", 2
        x3 = yield add(add(d3[:, :2], y3), grow(x4[:, 2:])), "seq", 1
        return add(x2, grow(add(x3, grow(x4[:, :2]))))
    x4 = yield d4, "seq", 1
    x3 = yield add(d3, grow(x4[:, 4:])), "seq", 0
    x3 = add(x3, grow(x4[:, :4]))
    x2 = jnp.concatenate([d2[:, 2:], d2[:, :2]], axis=1)
    return add(x2, grow(x3))


SHARES = 2


def split_groups(value, count):
    rows, width = value.shape
    value = value.reshape(rows, count, SHARES, width // (count * SHARES))
    return [value[:, :, share].swapaxes(0, 1) for share in range(SHARES)]


def join_groups(values):
    value = jnp.stack(values, axis=1)
    count, shares, rows, width = value.shape
    return value.transpose(2, 0, 1, 3).reshape(rows, count * shares * width)


def pin(first, then):
    return lax.optimization_barrier((first, then))[1]


def swap(value):
    return lax.all_to_all(value, "branch", split_axis=0, concat_axis=0, tiled=True)


def dot(spec, a, b):
    return jnp.einsum(spec, a, b, preferred_element_type=F32)


def axis_bit(axis, bit):
    return (lax.axis_index(axis) >> bit) & 1


def half(value, axis, which):
    size = value.shape[axis] // 2
    return lax.dynamic_slice_in_dim(value, which * size, size, axis)


def stage_order(flip):
    branch = [("branch", bit) for bit in range(lax.axis_size("branch").bit_length() - 1)]
    seq = [("seq", bit) for bit in range(1, lax.axis_size("seq").bit_length() - 1)]
    return (branch[::-1] if flip else branch) + seq


def reduce_product(a, b, order):
    core = axis_bit("seq", 0)
    side = axis_bit(*order[0])
    came = yield dot("tm,tn->mn", a, half(b, 1, 1 - core)).astype(BF16), "seq", 0
    mine = half(b, 1, core)
    other = dot("tm,tn->mn", half(a, 1, 1 - side), mine) + half(came, 0, 1 - side)
    first = yield other.astype(BF16), *order[0]
    part = dot("tm,tn->mn", half(a, 1, side), mine) + half(came, 0, side) + first
    for axis, bit in order[1:]:
        which = axis_bit(axis, bit)
        came = yield half(part, 0, 1 - which).astype(BF16), axis, bit
        part = half(part, 0, which) + came
    return part.astype(BF16)


def reduce_own(a, b, bits):
    core = axis_bit("seq", 0)
    came = yield dot("ktm,ktn->mn", half(a, 2, 1 - core), b).astype(BF16), "seq", 0
    part = dot("ktm,ktn->mn", half(a, 2, core), b) + came
    for bit in bits:
        which = axis_bit("seq", bit)
        came = yield half(part, 0, 1 - which).astype(BF16), "seq", bit
        part = half(part, 0, which) + came
    return part.astype(BF16)


def gather_kernel(orders, groups, sizes, *refs):
    count = len(orders)
    ins, outs = refs[:count], refs[count : 2 * count]
    own_sem, send_sem, recv_sem = refs[2 * count :]
    stages = len(orders[0])
    index = {axis: lax.axis_index(axis) for axis in sizes}

    def partner(axis, bit):
        mine = index[axis]
        step = 1 << bit
        return {axis: mine + step - 2 * step * lax.rem(mine // step, 2)}

    barrier = pltpu.get_barrier_semaphore()
    for axis, bit in orders[0]:
        pl.semaphore_signal(barrier, inc=1, device_id=partner(axis, bit), device_id_type=pl.DeviceIdType.MESH)
    slots = []
    for flow in range(count):
        slot = 0
        for stage, (axis, bit) in enumerate(orders[flow]):
            slot = slot + lax.rem(index[axis] // (1 << bit), 2) * (1 << stage)
        slots.append(slot)
    owns = [pltpu.make_async_copy(ins[flow], outs[flow].at[slots[flow]], own_sem.at[flow]) for flow in range(count)]
    for copy in owns:
        copy.start()
    pl.semaphore_wait(barrier, stages)
    for copy in owns:
        copy.wait()
    copies = {}

    def begin(flow, low, rows, at, stage):
        size = 1 << stage
        base = slots[flow] // size * size
        region = outs[flow].at[pl.ds(base, size), pl.ds(low, rows)]
        copies[at, stage] = pltpu.make_async_remote_copy(
            src_ref=region,
            dst_ref=region,
            send_sem=send_sem.at[at, stage],
            recv_sem=recv_sem.at[at, stage],
            device_id=partner(*orders[flow][stage]),
            device_id_type=pl.DeviceIdType.MESH,
        )
        copies[at, stage].start()

    numbered, at = [], 0
    for group in groups:
        numbered.append([(at + place,) + item for place, item in enumerate(group)])
        at += len(group)
    for turn in range(len(groups) + stages - 1):
        for number, group in enumerate(numbered):
            stage = turn - number
            if 0 <= stage < stages:
                for at, flow, low, rows in group:
                    if stage > 0:
                        copies[at, stage - 1].wait_recv()
                    begin(flow, low, rows, at, stage)
    for group in numbered:
        for at, flow, low, rows in group:
            copies[at, stages - 1].wait_recv()
    for copy in copies.values():
        copy.wait_send()


def gather_everywhere(pieces, orders, groups):
    stages = len(orders[0])
    count = len(pieces)
    items = sum(len(group) for group in groups)
    return pl.pallas_call(
        functools.partial(gather_kernel, orders, groups, ("branch", "seq")),
        out_shape=tuple(jax.ShapeDtypeStruct((1 << stages,) + piece.shape, piece.dtype) for piece in pieces),
        in_specs=[pl.BlockSpec(memory_space=pltpu.VMEM)] * count,
        out_specs=(pl.BlockSpec(memory_space=pl.ANY),) * count,
        scratch_shapes=[
            pltpu.SemaphoreType.DMA((count,)),
            pltpu.SemaphoreType.DMA((items, stages)),
            pltpu.SemaphoreType.DMA((items, stages)),
        ],
        compiler_params=pltpu.CompilerParams(collective_id=0, has_side_effects=True),
        name="gradient_gather",
    )(*pieces)


def columns_kernel(pieces_ref, *refs):
    out_ref = refs[-1]
    count, rows, columns = pieces_ref.shape[1:]
    for core in range(2):
        for at in range(count):
            out_ref[0, at * rows : (at + 1) * rows, core * columns : (core + 1) * columns] = pieces_ref[core, at].astype(F32)


def groups_kernel(groups, pieces_ref, *refs):
    out_ref = refs[-1]
    count, rows, columns = pieces_ref.shape
    depth = count // len(groups)
    for place, group in enumerate(groups):
        for at in range(depth):
            out_ref[0, at * rows : (at + 1) * rows, group * columns : (group + 1) * columns] = pieces_ref[at * len(groups) + place].astype(F32)


def write_layer(kernel, name, gathered, block, steps, shape, layer, layers, base):
    rows, width = shape
    index = (lambda at: (0, at, 0, 0)) if len(block) == 4 else (lambda at: (at, 0, 0))
    ins = [pl.BlockSpec(block, index)]
    operands = [gathered]
    aliases = {}
    if base is not None:
        ins.append(pl.BlockSpec(memory_space=pl.ANY))
        operands.append(base)
        aliases = {1: 0}
    return pl.pallas_call(
        kernel,
        grid=(steps,),
        in_specs=ins,
        out_specs=pl.BlockSpec((1, rows // steps, width), lambda at: (layer, at, 0)),
        out_shape=jax.ShapeDtypeStruct((layers, rows, width), F32),
        input_output_aliases=aliases,
        compiler_params=pltpu.CompilerParams(vmem_limit_bytes=48 * 2**20),
        name=name,
    )(*operands)


def write_columns(gathered, layer, layers, base):
    pieces, rows, columns = gathered.shape
    count = pieces // 2
    steps = min(count, 4)
    gathered = gathered.reshape(2, count, rows, columns)
    return write_layer(
        columns_kernel, "gradient_columns", gathered, (2, count // steps, rows, columns), steps, (count * rows, 2 * columns), layer, layers, base
    )


def write_groups(gathered, order, layer, layers, base):
    pieces, rows, columns = gathered.shape
    branch_bits = [bit for axis, bit in order if axis == "branch"]
    count = 1 << len(branch_bits)
    groups = [sum(((at >> place) & 1) << bit for place, bit in enumerate(branch_bits)) for at in range(count)]
    return write_layer(
        functools.partial(groups_kernel, groups), "gradient_groups", gathered, (pieces // 2, rows, columns), 2, (pieces // count * rows, count * columns), layer, layers, base
    )


def layer_forward(stream, weights, gain, shift, side, tables, geometry):
    w_in, w_out, w_up, w_down = weights
    first = geometry["first"]
    xhat, _ = normalize(stream)
    normed = (xhat * gain[0] + shift[0]).astype(BF16)
    projected = (dot("td,dc->tc", normed, w_in) * tables["scale"]).astype(BF16)
    sent = split_groups(projected, geometry["branch"])
    arrived = [swap(sent[0])]
    arrived[0], sent[1] = lax.optimization_barrier((arrived[0], sent[1]))
    arrived.append(swap(sent[1]))
    parts, far, lower = [], [], []
    for share in range(SHARES):
        q, kv = prepare(first[share], arrived[share], side, tables["full"], tables["kf"])
        far.append(Task(gather_far(kv, geometry)))
        flights, q = start(far, q)
        o = lower_forward(q, kv, tables["f0"], tables["f1"], 0, 1, None)
        land(flights, o)
        if share == 0:
            arrived[1] = pin(o, arrived[1])
        parts.append((q, kv))
        lower.append(o)
    normed_all = lax.all_gather(pin(lower[1], normed), "branch", axis=0, tiled=False)
    saved_parts, returned = [], []
    for share in range(SHARES):
        q, kv = parts[share]
        while not far[share].done:
            flights, q = start([far[share]], q)
            land(flights, q)
        flights, q = start(far[share + 1 :], q)
        r2, r3, r4 = far[share].result
        att, qb = upper_forward(q, lower[share], r2, r3, r4, tables["f2"], tables["f3"], tables["f4"])
        rows = to_rows(first[share], att, tables["wide"])
        land(flights, rows)
        returned.append(swap(rows))
        saved_parts.append((kv, r2, r3, r4, qb, att))
    att_rows = join_groups(returned)
    midway = stream + dot("tc,cd->td", att_rows, w_out)
    xhat, _ = normalize(midway)
    second = (xhat * gain[1] + shift[1]).astype(BF16)
    pre_act = dot("td,df->tf", second, w_up)
    hidden = (0.5 * pre_act * (1.0 + lax.erf(pre_act * np.float32(2**-0.5)))).astype(BF16)
    result = midway + dot("tf,fd->td", hidden, w_down)
    return result, (stream, normed_all, saved_parts, att_rows, midway, second, pre_act, hidden)


def layer_backward(gradient, saved, weights, gain, shift, tables, geometry, old, flights):
    w_in, w_out, w_up, w_down = weights
    stream, normed_all, parts, att_rows, midway, second, pre_act, hidden = saved
    first = geometry["first"]
    orders = geometry["orders"]
    down_in = gradient.astype(BF16)
    grad_hidden = dot("td,fd->tf", down_in, w_down)
    cdf = 0.5 * (1.0 + lax.erf(pre_act * np.float32(2**-0.5)))
    density = jnp.exp(-0.5 * pre_act * pre_act) * np.float32((2 * np.pi) ** -0.5)
    grad_pre = (grad_hidden * (cdf + pre_act * density)).astype(BF16)
    grad_second = dot("tf,mf->tm", grad_pre, w_up)
    back, gain_two, shift_two = normalize_back(midway, gain[1], grad_second)
    grad_midway = gradient + back
    out_in = grad_midway.astype(BF16)
    grad_rows = split_groups(dot("td,cd->tc", out_in, w_out).astype(BF16), geometry["branch"])
    if flights is not None:
        land(flights, grad_rows)
    grad_rows, hidden, second = lax.optimization_barrier((grad_rows, hidden, second))
    arrived = [swap(grad_rows[0])]
    down = Task(reduce_product(hidden, down_in, orders[1]))
    up = Task(reduce_product(second, grad_pre, orders[0]))
    out = Task(reduce_product(att_rows, out_in, orders[0]))
    new = [down, up, out]
    arrived[0], _, grad_rows[1] = lax.optimization_barrier((arrived[0], [task.pending[0] for task in new], grad_rows[1]))
    arrived.append(swap(grad_rows[1]))
    flights, arrived[0] = start(new + old, arrived[0])
    far, grads, upper = [], [], []
    for share in range(SHARES):
        kv, r2, r3, r4, qb, att = parts[share]
        short, arrived[share] = start(far, arrived[share])
        g = prepare_back(first[share], arrived[share], tables["narrow"], att)
        du, d2, d3, d4 = upper_back(qb, g, r2, r3, r4, tables["f2"], tables["f3"], tables["f4"])
        land(short, du)
        if share == 0:
            arrived[1] = pin(du, arrived[1])
        else:
            land(flights, du)
        far.append(Task(return_far(d2, d3, d4, geometry)))
        short, _ = start([far[share]], d2)
        land(short, d2)
        upper.append((g, du))
    back_rows, returned = [], []
    long, qb = start(new + old, parts[0][4])
    for share in range(SHARES):
        kv, r2, r3, r4, _, att = parts[share]
        g, du = upper[share]
        qb = parts[share][4] if share else qb
        short, qb = start(far, qb)
        dq, dkv = lower_back(qb, g, kv, tables["f0"], tables["f1"], 0, 1, None)
        land(short, dq)
        while not far[share].done:
            short, dq = start([far[share]], dq)
            land(short, dq)
        if share == SHARES - 1:
            returned[0] = pin(dq, returned[0])
            land(long, dq)
            flights, dq = start(new + old, dq)
        rows = to_rows_back(first[share], dq, du, dkv, far[share].result, tables["back"], SIZE**-0.5)
        back_rows.append(rows)
        if share == 0:
            parts[1] = parts[1][:4] + (pin(rows, parts[1][4]),) + parts[1][5:]
        returned.append(swap(rows))
    normed_all, back_rows = lax.optimization_barrier((normed_all, back_rows))
    enter = Task(reduce_own(normed_all, jnp.concatenate(back_rows, axis=2), geometry["seq_bits"]))
    returned[1] = pin(enter.pending[0], returned[1])
    extra, returned[1] = start([enter], returned[1])
    projected = join_groups(returned)
    grad_first = dot("tc,dc->td", projected, w_in)
    back, gain_one, shift_one = normalize_back(stream, gain[0], grad_first)
    vectors = jnp.stack([gain_one, gain_two, shift_one, shift_two])
    return grad_midway + back, vectors, new + [enter], flights + extra


def local(tile_embeddings, tile_valid, slide_bounds, norm_gain, norm_bias, attention_in, attention_out, hidden_up, hidden_down, cotangent):
    branch = lax.axis_size("branch")
    seq = lax.axis_size("seq")
    heads = H // branch
    rows, width = tile_embeddings.shape
    shard = rows * branch
    blocks = shard // BLOCK
    seq_at = lax.axis_index("seq")
    origin = seq_at * shard
    bit = 1 if blocks == 2 else 0

    def slide_at(place):
        return jnp.sum((place >= slide_bounds[1:-1]).astype(jnp.int32))

    def same(mask):
        return slide_at((seq_at ^ mask) * shard) == slide_at(origin)

    low, high = 1 << bit, 2 << bit
    geometry = dict(
        branch=branch,
        blocks=blocks,
        bit=bit,
        first=[(lax.axis_index("branch") * heads + share * (heads // SHARES)).astype(jnp.int32).reshape(1) for share in range(SHARES)],
        same=(None, same(low), same(high), same(high | low)),
    )
    full, narrow = placements(heads // SHARES)
    scale = np.where((np.arange(3 * SIZE * H) // SIZE) % 3 == 0, LOG2E * SIZE**-0.5, 1.0)
    tables = dict(
        full=jnp.asarray(full),
        back=jnp.asarray(full.astype(np.float32).swapaxes(1, 2).astype(jnp.bfloat16)),
        narrow=jnp.asarray(narrow),
        kf=jnp.asarray(key_features()),
        scale=jnp.asarray(scale, F32),
        f0=jnp.asarray(query_features(block_classes, 0)),
        f1=jnp.asarray(query_features(block_classes[:512], 1)),
        f2=jnp.asarray(query_features(upper_classes, 2)),
        f3=jnp.asarray(query_features(upper_classes[:256], 3)),
        f4=jnp.asarray(query_features(upper_classes[:128], 4)),
    )
    tables["wide"] = jnp.asarray(narrow.astype(np.float32).swapaxes(1, 2).astype(jnp.bfloat16))
    valid = lax.dynamic_slice_in_dim(tile_valid, origin, shard)
    valid = valid.reshape(branch, rows // 16, 16).swapaxes(1, 2).reshape(shard, 1)
    side = jnp.where((lanes_of((1, 128)) == BIAS) & (valid != 1), NEG, 0.0).astype(BF16)

    layers = attention_in.shape[0]
    orders = (stage_order(False), stage_order(True))
    geometry["orders"] = orders
    geometry["seq_bits"] = [bit for axis, bit in orders[0] if axis == "seq"]
    weights = [(attention_in[at], attention_out[at], hidden_up[at], hidden_down[at]) for at in range(layers)]
    stream = to_major(tile_embeddings).astype(F32)
    outputs, saved_all = [], []
    for layer in range(layers):
        stream, saved = layer_forward(stream, weights[layer], norm_gain[layer], norm_bias[layer], side, tables, geometry)
        outputs.append(from_major(stream.astype(BF16)))
        saved_all.append(saved)
    gradient = to_major(cotangent).astype(F32)
    vectors = [None] * layers
    tasks, flights = [], None
    for layer in reversed(range(layers)):
        gradient, vectors[layer], new, flights = layer_backward(
            gradient, saved_all[layer], weights[layer], norm_gain[layer], norm_bias[layer], tables, geometry, [task for _, _, task in tasks], flights
        )
        tasks += [(layer, member, task) for member, task in enumerate(new)]
    land(flights, gradient)
    for task in [task for _, _, task in tasks]:
        while not task.done:
            task.advance(jax.tree.map(lambda v: exchange(v, *task.pending[1:]), task.pending[0]))
    rounds = [order[::-1] + [("seq", 0)] for order in orders]
    seq_stages = [stage for stage in rounds[0] if stage[0] == "seq"]
    flip = [stage for stage in rounds[1] if stage[0] == "branch"]
    member_round = (rounds[1], rounds[0], rounds[0], flip + seq_stages)
    pieces = [task.result for _, _, task in tasks] + [jnp.stack(vectors).reshape(-1, width)]
    groups = [[(flow, 0, piece.shape[0]) for flow, piece in enumerate(pieces)]]
    gathered = gather_everywhere(pieces, [member_round[member] for _, member, _ in tasks] + [rounds[0]], groups)
    vectors = jnp.sum(gathered[-1], axis=0).reshape(layers, 2, 2, width)
    sums = [None] * 4
    for (layer, member, _), whole in zip(tasks, gathered[:-1]):
        if member == 3:
            sums[member] = write_groups(whole, member_round[member], layer, layers, sums[member])
        else:
            sums[member] = write_columns(whole, layer, layers, sums[member])
    down, up, out, enter = sums
    return (jnp.stack(outputs), from_major(gradient), vectors[:, 0], vectors[:, 1], enter, out, up, down)


def solution(mesh):
    split = P(("seq", "branch"), None)
    in_specs = (split,) + (P(),) * 8 + (split,)
    out_specs = (P(None, ("seq", "branch"), None), split) + (P(),) * 6
    return jax.shard_map(local, mesh=mesh, in_specs=in_specs, out_specs=out_specs, check_vma=False)
```

```python
import functools
import numpy as np
import jax
import jax.numpy as jnp
from jax import lax
from jax.experimental import pallas as pl
from jax.experimental.pallas import tpu as pltpu
from jax.sharding import PartitionSpec as P

BLOCK = 1024
CHUNK = 32
ORDER = (0, 8, 4, 12, 2, 10, 6, 14, 1, 9, 5, 13, 3, 11, 7, 15)
ONE, BIAS, HIGH, LOW, VALUE = 48, 51, 52, 57, 64
NEG = -1e30
LOG2E = 1.4426950408889634
LN2 = 0.6931471805599453
F32, BF16 = jnp.float32, jnp.bfloat16


def low_np(x):
    return np.asarray(x, np.float32).astype(jnp.bfloat16).astype(np.float32)


def query_features(classes, level):
    table = np.zeros((len(classes), 128), np.float32)
    table[:, BIAS] = 1.0
    for at, mine in enumerate(classes):
        for theirs in range(5):
            met = min(mine, theirs) - level + 1
            value = np.log2(met) if met > 0 else NEG
            high = low_np(value)
            table[at, HIGH + theirs] = high
            table[at, LOW + theirs] = low_np(value - high) if met > 0 else 0.0
    return table.astype(jnp.bfloat16)


block_classes = [4] * 64 + [3] * 64 + [2] * 128 + [1] * 256 + [0] * 512
upper_classes = [4] * 128 + [3] * 128 + [2] * 256


def key_features():
    table = np.zeros((BLOCK, 128), np.float32)
    table[:, ONE : ONE + 3] = 1.0
    for at, mine in enumerate(block_classes):
        table[at, HIGH + mine] = 1.0
        table[at, LOW + mine] = 1.0
    return table.astype(jnp.bfloat16)


def nt(a, b):
    return lax.dot_general(a, b, (((1,), (1,)), ((), ())), preferred_element_type=F32)


def tn(a, b):
    return lax.dot_general(a, b, (((0,), (0,)), ((), ())), preferred_element_type=F32)


def nn(a, b):
    return lax.dot_general(a, b, (((1,), (0,)), ((), ())), preferred_element_type=F32)


def lanes_of(shape):
    return lax.broadcasted_iota(jnp.int32, shape, len(shape) - 1)


def split3(column):
    high = column.astype(BF16)
    rest = column - high.astype(F32)
    mid = rest.astype(BF16)
    last = (rest - mid.astype(F32)).astype(BF16)
    return high, mid, last


def place3(base, column):
    high, mid, last = split3(column)
    lane = lanes_of(base.shape)
    out = jnp.where(lane == ONE, high.astype(F32), base)
    out = jnp.where(lane == ONE + 1, mid.astype(F32), out)
    return jnp.where(lane == ONE + 2, last.astype(F32), out)


def chunk_row(head, block, position, part, per_dev):
    residue = lax.rem(ORDER[position] + head, 16)
    return pl.multiple_of((2 * block + part) * per_dev + residue * CHUNK, CHUNK)


def prepare_kernel(heads, blocks, first_ref, x_ref, side_ref, place_ref, kf_ref, q_ref, kv_ref, work):
    kf = kf_ref[...]

    for head in range(heads):
        for part in range(x_ref.shape[0]):
            work[part * 512 : part * 512 + 512] = tn(x_ref[part], place_ref[head]).astype(BF16)
        which = first_ref[0] + head

        for position in range(16):
            features = kf[position * 64 : position * 64 + CHUNK]
            for block in range(blocks):
                for part in range(2):
                    row = chunk_row(which, block, position, part, 512)
                    at = position * 64 + part * CHUNK
                    source = work[pl.ds(row, CHUNK), :]
                    q_ref[head, block, at : at + CHUNK, :] = source[:, :128]
                    kv_ref[head, block, at : at + CHUNK, :] = (
                        source[:, 128:] + features + side_ref[pl.ds(row, CHUNK), :]
                    )


def prepare(first, rows, side, place, kf):
    heads = place.shape[0]
    total = rows.shape[0] * rows.shape[2]
    blocks = total // BLOCK
    shape = jax.ShapeDtypeStruct((heads, blocks, BLOCK, 128), BF16)
    return pl.pallas_call(
        functools.partial(prepare_kernel, heads, blocks),
        out_shape=(shape, shape),
        in_specs=[pl.BlockSpec(memory_space=pltpu.SMEM)]
        + [pl.BlockSpec(memory_space=pltpu.VMEM)] * 4,
        out_specs=(pl.BlockSpec(memory_space=pltpu.VMEM),) * 2,
        scratch_shapes=[pltpu.VMEM((total, 256), BF16)],
        compiler_params=pltpu.CompilerParams(vmem_limit_bytes=48 * 2**20),
        name="attention_prepare",
    )(first, rows, side, place, kf)


def lower_kernel(q_ref, kv_ref, f0_ref, f1_ref, *refs):
    o_ref = refs[-1]
    step = 256
    for block in range(2):
        own = kv_ref[0, block]
        near = kv_ref[0, 1 - block, :512]
        for at in range(0, BLOCK, step):
            rows = slice(at, at + step)
            base = q_ref[0, block, rows]
            s0 = nt(base + f0_ref[rows], own)
            top = jnp.max(s0, axis=1, keepdims=True)
            if at < 512:
                s1 = nt(base + f1_ref[rows], near)
                top = jnp.maximum(top, jnp.max(s1, axis=1, keepdims=True))
            own_rows = own[rows].astype(F32)
            meet = base.astype(F32) * own_rows
            alone = jnp.sum(meet, axis=1, keepdims=True)
            lane = lanes_of(own_rows.shape)
            bias = jnp.min(jnp.where(lane == BIAS, own_rows, 0.0), axis=1, keepdims=True)
            classes = sum((lax.broadcasted_iota(jnp.int32, (step, 1), 0) + at < edge).astype(F32) for edge in (512, 256, 128, 64))
            alone = jnp.where(bias < 0.0, alone + jnp.log2(classes + 1.0), NEG)
            top = jnp.maximum(top, alone)
            out = nn(jnp.exp2(s0 - top).astype(BF16), own)
            if at < 512:
                out = out + nn(jnp.exp2(s1 - top).astype(BF16), near)
            out = out + jnp.exp2(alone - top) * own_rows
            o_ref[0, block, rows] = jnp.where(lane == 0, top, out)


def part_call(kernel, name, operands, tables, outs, part, parts, base, cost):
    heads, blocks = operands[0].shape[:2]
    count = heads // parts
    spec = pl.BlockSpec((1, 2, BLOCK, 128), lambda h, p: (h + part * count, p, 0, 0))
    whole = lambda a: pl.BlockSpec(a.shape, lambda h, p: (0,) * a.ndim)
    ins = [spec] * len(operands) + [whole(table) for table in tables]
    arrays = list(operands) + list(tables)
    aliases = {}
    if base is not None:
        for at, array in enumerate(base):
            aliases[len(arrays)] = at
            arrays.append(array)
            ins.append(pl.BlockSpec(memory_space=pl.ANY))
    pairs = int(count * blocks * 1.25 * 2**20)
    return pl.pallas_call(
        kernel,
        grid=(count, blocks // 2),
        in_specs=ins,
        out_specs=(spec,) * outs,
        out_shape=(jax.ShapeDtypeStruct(operands[0].shape, F32),) * outs,
        input_output_aliases=aliases,
        compiler_params=pltpu.CompilerParams(vmem_limit_bytes=56 * 2**20),
        cost_estimate=pl.CostEstimate(flops=pairs * 256 * cost, bytes_accessed=operands[0].size * 8 // parts, transcendentals=pairs),
        name=name,
    )(*arrays)


def lower_forward(q, kv, f0, f1, part, parts, base):
    out = part_call(lower_kernel, "attention_lower", (q, kv), (f0, f1), 1, part, parts, None if base is None else (base,), 4)
    return out[0]


UPPER = ((0, 0, 64), (1, 0, 64), (0, 64, 128), (1, 64, 128), (0, 128, 256), (1, 128, 256))


def gather_upper(ref, lead):
    return jnp.concatenate([ref[(*lead, block, slice(low, high))] for block, low, high in UPPER], axis=0)


def upper_kernel(q_ref, o_ref, r2_ref, r3_ref, r4_ref, f2_ref, f3_ref, f4_ref, att_ref, qb_ref):
    merged = {}
    uq = gather_upper(q_ref, (0,))
    ol = gather_upper(o_ref, (0,))
    for low, high in ((0, 128), (128, 256), (256, 512)):
        base = uq[low:high]
        pairs = [(nt(base + f2_ref[low:high], r2_ref[0, 0]), r2_ref[0, 0])]
        if high <= 256:
            pairs.append((nt(base + f3_ref[low:high], r3_ref[0]), r3_ref[0]))
        if high <= 128:
            pairs.append((nt(base + f4_ref[low:high], r4_ref[0]), r4_ref[0]))
        old = ol[low:high]
        lane = lanes_of(old.shape)
        before = old[:, 0:1]
        top = before
        for scores, keys in pairs:
            top = jnp.maximum(top, jnp.max(scores, axis=1, keepdims=True))
        out = old * jnp.exp2(before - top)
        for scores, keys in pairs:
            out = out + nn(jnp.exp2(scores - top).astype(BF16), keys)
        merged[low] = jnp.where(lane == 0, top, out)
    whole = jnp.concatenate([merged[0], merged[128], merged[256]], axis=0)
    place = 0

    def finish(block, low, high, rows):
        lane = lanes_of(rows.shape)
        top = rows[:, 0:1]
        total = rows[:, ONE : ONE + 1]
        att_ref[0, block, low:high] = jnp.where((lane >= VALUE) & (lane < VALUE + 48), rows / total, 0.0)
        lse = top + jnp.log2(total)
        qb_ref[0, block, low:high] = place3(q_ref[0, block, low:high].astype(F32), -lse).astype(BF16)

    for block, low, high in UPPER:
        finish(block, low, high, whole[place : place + high - low])
        place += high - low
    for block in range(2):
        for low in (256, 512, 768):
            finish(block, low, low + 256, o_ref[0, block, low : low + 256])


def upper_forward(q, o, r2, r3, r4, f2, f3, f4):
    heads, blocks = q.shape[:2]
    spec = pl.BlockSpec((1, 2, BLOCK, 128), lambda h, p: (h, p, 0, 0))
    two = pl.BlockSpec((1, 1, 512, 128), lambda h, p: (h, p, 0, 0))
    far = pl.BlockSpec((1, 512, 128), lambda h, p: (h, 0, 0))
    whole = lambda a: pl.BlockSpec(a.shape, lambda h, p: (0,) * a.ndim)
    return pl.pallas_call(
        upper_kernel,
        grid=(heads, blocks // 2),
        in_specs=[spec, spec, two, far, far, whole(f2), whole(f3), whole(f4)],
        out_specs=(spec, spec),
        out_shape=(jax.ShapeDtypeStruct(q.shape, F32), jax.ShapeDtypeStruct(q.shape, BF16)),
        compiler_params=pltpu.CompilerParams(vmem_limit_bytes=48 * 2**20),
        name="attention_upper",
    )(q, o, r2, r3, r4, f2, f3, f4)


def chunk_place(head, residue, part):
    turn = lax.rem(residue - head + 32, 16)
    position = 8 * lax.rem(turn, 2) + 4 * lax.rem(turn // 2, 2) + 2 * lax.rem(turn // 4, 2) + turn // 8
    return pl.multiple_of(position * 64 + part * CHUNK, CHUNK)


def rows_kernel(heads, blocks, first_ref, a_ref, place_ref, out_ref, work):
    for head in range(heads):
        which = first_ref[0] + head
        for residue in range(16):
            for block in range(blocks):
                for part in range(2):
                    row = (2 * block + part) * 512 + residue * CHUNK
                    at = chunk_place(which, residue, part)
                    work[head, row : row + CHUNK, :] = a_ref[head, block, pl.ds(at, CHUNK), :].astype(BF16)
        for part in range(out_ref.shape[0]):
            value = nt(place_ref[head], work[head, part * 512 : part * 512 + 512]).astype(BF16)
            out_ref[part] = value if head == 0 else out_ref[part] + value


def to_rows(first, att, place):
    heads, blocks = att.shape[:2]
    width = place.shape[1]
    total = blocks * BLOCK
    return pl.pallas_call(
        functools.partial(rows_kernel, heads, blocks),
        out_shape=jax.ShapeDtypeStruct((total // 512, width, 512), BF16),
        in_specs=[pl.BlockSpec(memory_space=pltpu.SMEM)]
        + [pl.BlockSpec(memory_space=pltpu.VMEM)] * 2,
        out_specs=pl.BlockSpec(memory_space=pltpu.VMEM),
        scratch_shapes=[pltpu.VMEM((heads, total, 128), BF16)],
        compiler_params=pltpu.CompilerParams(vmem_limit_bytes=48 * 2**20),
        name="attention_rows",
    )(first, att, place)


def prepare_back_kernel(heads, blocks, first_ref, x_ref, place_ref, att_ref, g_ref, work):
    for head in range(heads):
        for part in range(x_ref.shape[0]):
            work[part * 512 : part * 512 + 512] = tn(x_ref[part], place_ref[head]).astype(BF16)
        which = first_ref[0] + head
        for position in range(16):
            for block in range(blocks):
                for part in range(2):
                    row = chunk_row(which, block, position, part, 512)
                    at = position * 64 + part * CHUNK
                    g_ref[head, block, at : at + CHUNK, :] = work[pl.ds(row, CHUNK), :]
        for block in range(blocks):
            for at in range(0, BLOCK, 256):
                rows = slice(at, at + 256)
                grad = g_ref[head, block, rows].astype(F32)
                dots = jnp.sum(grad * att_ref[head, block, rows], axis=1, keepdims=True)
                g_ref[head, block, rows] = place3(grad, -dots).astype(BF16)


def prepare_back(first, rows, place, att):
    heads, blocks = att.shape[:2]
    total = blocks * BLOCK
    return pl.pallas_call(
        functools.partial(prepare_back_kernel, heads, blocks),
        out_shape=jax.ShapeDtypeStruct(att.shape, BF16),
        in_specs=[pl.BlockSpec(memory_space=pltpu.SMEM)]
        + [pl.BlockSpec(memory_space=pltpu.VMEM)] * 3,
        out_specs=pl.BlockSpec(memory_space=pltpu.VMEM),
        scratch_shapes=[pltpu.VMEM((total, 128), BF16)],
        compiler_params=pltpu.CompilerParams(vmem_limit_bytes=48 * 2**20),
        name="attention_prepare_back",
    )(first, rows, place, att)


def back_tile(kv, key_t, q_scores, g, q):
    probs = jnp.exp2(nt(kv, q_scores))
    grad_scores = (probs * nt(kv, g)).astype(BF16)
    grad_kv = nn(probs.astype(BF16), g) + nn(grad_scores, q)
    return grad_kv, nn(key_t, grad_scores)


def upper_back_kernel(qb_ref, g_ref, r2_ref, r3_ref, r4_ref, f2_ref, f3_ref, f4_ref, dq_ref, d2_ref, d3_ref, d4_ref):
    uq = gather_upper(qb_ref, (0,))
    ug = gather_upper(g_ref, (0,))
    dq = None
    lane = lanes_of((256, 128))
    for ref, out, f_ref, count in ((r2_ref.at[0], d2_ref.at[0], f2_ref, 512), (r3_ref, d3_ref.at[0], f3_ref, 256), (r4_ref, d4_ref.at[0], f4_ref, 128)):
        q = uq[:count]
        g = ug[:count]
        qs = q + f_ref[...]
        total = None
        for at in range(0, 512, 256):
            kv = ref[0, at : at + 256]
            key_t = kv.astype(F32).T[:48].astype(BF16)
            grad_kv, part = back_tile(kv, key_t, qs, g, q)
            out[0, at : at + 256] = jnp.where(lane < 48, grad_kv * LN2, grad_kv).astype(BF16)
            total = part if total is None else total + part
        rows = total.T
        if count < 512:
            rows = jnp.concatenate([rows, jnp.zeros((512 - count, 48), F32)], axis=0)
        dq = rows if dq is None else dq + rows
    dq_ref[0, 0] = jnp.concatenate([dq, jnp.zeros((512, 80), F32)], axis=1)


def upper_back(qb, g, r2, r3, r4, f2, f3, f4):
    heads, blocks = qb.shape[:2]
    pairs = blocks // 2
    spec = pl.BlockSpec((1, 2, BLOCK, 128), lambda h, p: (h, p, 0, 0))
    two = pl.BlockSpec((1, 1, 512, 128), lambda h, p: (h, p, 0, 0))
    far = pl.BlockSpec((1, 512, 128), lambda h, p: (h, 0, 0))
    whole = lambda a: pl.BlockSpec(a.shape, lambda h, p: (0,) * a.ndim)
    shape = (heads, pairs, 512, 128)
    return pl.pallas_call(
        upper_back_kernel,
        grid=(heads, pairs),
        in_specs=[spec, spec, two, far, far, whole(f2), whole(f3), whole(f4)],
        out_specs=(two,) * 4,
        out_shape=(jax.ShapeDtypeStruct(shape, F32),) + (jax.ShapeDtypeStruct(shape, BF16),) * 3,
        compiler_params=pltpu.CompilerParams(vmem_limit_bytes=48 * 2**20),
        name="attention_upper_back",
    )(qb, g, r2, r3, r4, f2, f3, f4)


def lower_back_kernel(qb_ref, g_ref, kv_ref, f0_ref, f1_ref, *refs):
    dq_ref, dkv_ref = refs[-2:]
    step = 256
    lane = lanes_of((step, 128))
    totals = [None, None]
    for block in range(2):
        q = qb_ref[0, block]
        g = g_ref[0, block]
        q0 = q + f0_ref[...]
        far_q = qb_ref[0, 1 - block, :512]
        far_g = g_ref[0, 1 - block, :512]
        far_q1 = far_q + f1_ref[...]
        for at in range(0, BLOCK, step):
            rows = slice(at, at + step)
            kv = kv_ref[0, block, rows]
            key_t = kv.astype(F32).T[:48].astype(BF16)
            grad_kv, part = back_tile(kv, key_t, q0, g, q)
            totals[block] = part if totals[block] is None else totals[block] + part
            if at < 512:
                more_kv, part = back_tile(kv, key_t, far_q1, far_g, far_q)
                grad_kv = grad_kv + more_kv
                part = jnp.concatenate([part, jnp.zeros((48, 512), F32)], axis=1)
                totals[1 - block] = part if totals[1 - block] is None else totals[1 - block] + part
            kv_rows = kv.astype(F32)
            q_rows = q[rows].astype(F32)
            g_rows = g[rows].astype(F32)
            bias = jnp.min(jnp.where(lane == BIAS, kv_rows, 0.0), axis=1, keepdims=True)
            classes = sum((lax.broadcasted_iota(jnp.int32, (step, 1), 0) + at < edge).astype(F32) for edge in (512, 256, 128, 64))
            met = jnp.where(lane < ONE + 3, q_rows * kv_rows, 0.0)
            score = jnp.sum(met, axis=1, keepdims=True) + jnp.log2(classes + 1.0)
            prob = jnp.where(bias < 0.0, jnp.exp2(jnp.where(bias < 0.0, score, NEG)), 0.0)
            grad_score = prob * jnp.sum(jnp.where((lane >= ONE) & (lane != BIAS), g_rows * kv_rows, 0.0), axis=1, keepdims=True)
            grad_kv = grad_kv + prob * g_rows + grad_score * q_rows
            dkv_ref[0, block, rows] = jnp.where(lane < 48, grad_kv * LN2, grad_kv)
            dq_ref[0, block, rows] = grad_score * kv_rows
    for block in range(2):
        for at in range(0, BLOCK, step):
            rows = slice(at, at + step)
            value = totals[block][:, rows].T
            value = jnp.concatenate([value, jnp.zeros((step, 80), F32)], axis=1)
            dq_ref[0, block, rows] = dq_ref[0, block, rows] + value


def lower_back(qb, g, kv, f0, f1, part, parts, base):
    return part_call(lower_back_kernel, "attention_lower_back", (qb, g, kv), (f0, f1), 2, part, parts, base, 10)


def rows_back_kernel(heads, blocks, scale, first_ref, dq_ref, du_ref, dkv_ref, x2_ref, place_ref, out_ref, work, sum_q, sum_kv):
    for head in range(heads):
        for block in range(blocks):
            start = 0
            for ub, low, high in UPPER:
                if ub == block % 2:
                    sum_q[head, block, low:high] = dq_ref[head, block, low:high] + du_ref[head, block // 2, start : start + high - low]
                start += high - low
            sum_q[head, block, 256:] = dq_ref[head, block, 256:]
            sum_kv[head, block, :256] = dkv_ref[head, block, :256] + x2_ref[head, block].astype(F32)
            sum_kv[head, block, 256:] = dkv_ref[head, block, 256:]
        which = first_ref[0] + head
        for residue in range(16):
            for block in range(blocks):
                for part in range(2):
                    row = (2 * block + part) * 512 + residue * CHUNK
                    at = chunk_place(which, residue, part)
                    grad_q = sum_q[head, block, pl.ds(at, CHUNK), :]
                    grad_kv = sum_kv[head, block, pl.ds(at, CHUNK), :]
                    lane = lanes_of(grad_q.shape)
                    work[head, row : row + CHUNK, :128] = jnp.where(lane < 48, grad_q * scale, 0.0).astype(BF16)
                    keep = (lane < 48) | ((lane >= VALUE) & (lane < VALUE + 48))
                    work[head, row : row + CHUNK, 128:] = jnp.where(keep, grad_kv, 0.0).astype(BF16)
        for part in range(out_ref.shape[0]):
            value = nt(place_ref[head], work[head, part * 512 : part * 512 + 512]).astype(BF16)
            out_ref[part] = value if head == 0 else out_ref[part] + value


def to_rows_back(first, dq, du, dkv, x2, place, scale):
    heads, blocks = dq.shape[:2]
    total = blocks * BLOCK
    return pl.pallas_call(
        functools.partial(rows_back_kernel, heads, blocks, scale),
        out_shape=jax.ShapeDtypeStruct((total // 512, place.shape[1], 512), BF16),
        in_specs=[pl.BlockSpec(memory_space=pltpu.SMEM)]
        + [pl.BlockSpec(memory_space=pltpu.VMEM)] * 5,
        out_specs=pl.BlockSpec(memory_space=pltpu.VMEM),
        scratch_shapes=[pltpu.VMEM((heads, total, 256), BF16)] + [pltpu.VMEM(dq.shape, F32)] * 2,
        compiler_params=pltpu.CompilerParams(vmem_limit_bytes=56 * 2**20),
        name="attention_rows_back",
    )(first, dq, du, dkv, x2, place)


def placements(heads):
    full = np.zeros((heads, heads * 144, 256), np.float32)
    narrow = np.zeros((heads, heads * 48, 128), np.float32)
    for head in range(heads):
        for at in range(48):
            full[head, head * 144 + at, at] = 1.0
            full[head, head * 144 + 48 + at, 128 + at] = 1.0
            full[head, head * 144 + 96 + at, 128 + VALUE + at] = 1.0
            narrow[head, head * 48 + at, VALUE + at] = 1.0
    return full.astype(jnp.bfloat16), narrow.astype(jnp.bfloat16)


H = 16
SIZE = 48
eps_norm = 1e-05


def exchange(value, axis, bit):
    count = lax.axis_size(axis)
    return lax.ppermute(value, axis, [(at, at ^ (1 << bit)) for at in range(count)])


def to_major(x):
    rows, width = x.shape
    return x.reshape(rows // 16, 16, width).swapaxes(0, 1).reshape(rows, width)


def from_major(x):
    rows, width = x.shape
    return x.reshape(16, rows // 16, width).swapaxes(0, 1).reshape(rows, width)


def normalize(stream):
    centered = stream - jnp.mean(stream, axis=-1, keepdims=True)
    spread = jnp.mean(centered * centered, axis=-1, keepdims=True)
    scale = lax.rsqrt(spread + eps_norm)
    return centered * scale, scale


def normalize_back(stream, gain, e):
    xhat, scale = normalize(stream)
    dxh = e * gain
    back = scale * (dxh - jnp.mean(dxh, axis=-1, keepdims=True) - xhat * jnp.mean(dxh * xhat, axis=-1, keepdims=True))
    return back, jnp.sum(e * xhat, axis=0), jnp.sum(e, axis=0)


class Task:
    def __init__(self, steps):
        self.steps = steps
        self.pending, self.result, self.done = None, None, False
        self.advance(None)

    def advance(self, value):
        try:
            self.pending = self.steps.send(value)
        except StopIteration as stop:
            self.result, self.pending, self.done = stop.value, None, True


def start(tasks, ins):
    tasks = [task for task in tasks if not task.done]
    operands = [task.pending[0] for task in tasks]
    operands, ins = lax.optimization_barrier((operands, ins))
    flights = [(task, jax.tree.map(lambda v: exchange(v, *task.pending[1:]), operand)) for task, operand in zip(tasks, operands)]
    return flights, ins


def land(flights, outs):
    if flights:
        values, _ = lax.optimization_barrier(([value for _, value in flights], outs))
        for (task, _), value in zip(flights, values):
            task.advance(value)


def gather_far(kv, geometry):
    blocks, same = geometry["blocks"], geometry["same"]
    heads = kv.shape[0]
    own2, own3, own4 = kv[:, :, :256], kv[:, :, :128], kv[:, :, :64]
    if blocks == 2:
        a3 = yield own3, "seq", 1
        a4 = yield jnp.concatenate([own4, a3[:, :, :64]], axis=1), "seq", 2
        r2, b3, b4 = yield (own2, a3, a4), "seq", 0
        r3 = jnp.concatenate([a3, b3], axis=1)
        r4 = jnp.concatenate([a4[:, :2], b4[:, :2], a4[:, 2:], b4[:, 2:]], axis=1)
    else:
        r2 = jnp.concatenate([own2[:, 2:], own2[:, :2]], axis=1)
        r3 = yield own3, "seq", 0
        r4 = yield jnp.concatenate([own4, r3[:, :, :64]], axis=1), "seq", 1
    bias_lane = lanes_of((1, 1, 1, 128)) == BIAS
    r3 = jnp.where(bias_lane & ~same[1], jnp.asarray(NEG, BF16), r3)
    alike = jnp.repeat(jnp.stack([same[2], same[3]]), 4)[None, :, None, None]
    r4 = jnp.where(bias_lane & ~alike, jnp.asarray(NEG, BF16), r4)
    return (
        r2.reshape(heads, blocks // 2, 512, 128),
        r3.reshape(heads, 512, 128),
        r4.reshape(heads, 512, 128),
    )


def return_far(d2, d3, d4, geometry):
    blocks = geometry["blocks"]
    heads = d2.shape[0]

    def fold(d):
        return d[:, 0] if d.shape[1] == 1 else jnp.sum(d.astype(F32), axis=1).astype(BF16)

    def add(a, b):
        return (a.astype(F32) + b.astype(F32)).astype(BF16)

    def grow(d):
        return jnp.concatenate([d, jnp.zeros_like(d)], axis=2)

    d4 = fold(d4).reshape(heads, 8, 64, 128)
    d3 = fold(d3).reshape(heads, 4, 128, 128)
    d2 = d2.reshape(heads, blocks, 256, 128)
    if blocks == 2:
        b4 = jnp.concatenate([d4[:, 2:4], d4[:, 6:8]], axis=1)
        a4 = jnp.concatenate([d4[:, 0:2], d4[:, 4:6]], axis=1)
        x2, y3, y4 = yield (d2, d3[:, 2:], b4), "seq", 0
        x4 = yield add(a4, y4), "seq", 2
        x3 = yield add(add(d3[:, :2], y3), grow(x4[:, 2:])), "seq", 1
        return add(x2, grow(add(x3, grow(x4[:, :2]))))
    x4 = yield d4, "seq", 1
    x3 = yield add(d3, grow(x4[:, 4:])), "seq", 0
    x3 = add(x3, grow(x4[:, :4]))
    x2 = jnp.concatenate([d2[:, 2:], d2[:, :2]], axis=1)
    return add(x2, grow(x3))


def split_groups(value, count):
    return value.reshape(count, -1, value.shape[1])


def join_groups(value):
    return value.reshape(-1, value.shape[2])


def pin(first, then):
    return lax.optimization_barrier((first, then))[1]


def swap(value):
    return lax.all_to_all(value, "branch", split_axis=0, concat_axis=0, tiled=True)


def dot(spec, a, b):
    return jnp.einsum(spec, a, b, preferred_element_type=F32)


def axis_bit(axis, bit):
    return (lax.axis_index(axis) >> bit) & 1


def half(value, axis, which):
    size = value.shape[axis] // 2
    return lax.dynamic_slice_in_dim(value, which * size, size, axis)


def bits_of(axis, low=0):
    return [(axis, bit) for bit in range(low, lax.axis_size(axis).bit_length() - 1)]


def halving_order():
    return bits_of("branch") + bits_of("seq", 1)


def flipped_order():
    return bits_of("branch")[::-1] + bits_of("seq", 1)


def doubling_order(flip, branch_first=False):
    branch = bits_of("branch") if flip else bits_of("branch")[::-1]
    seq = bits_of("seq", 1)[::-1]
    return (branch + seq if branch_first else seq + branch) + [("seq", 0)]


def reduce_product(a, b, order, parts=1):
    core = axis_bit("seq", 0)
    side = axis_bit(*order[0])
    came = yield dot("tm,tn->mn", a, half(b, 1, 1 - core)).astype(BF16), "seq", 0
    mine = half(b, 1, core)
    other = dot("tm,tn->mn", half(a, 1, 1 - side), mine) + half(came, 0, 1 - side)
    size = other.shape[0] // parts
    firsts = []
    for at in range(parts):
        came_part = yield other[at * size : (at + 1) * size].astype(BF16), *order[0]
        firsts.append(came_part)
    first = jnp.concatenate(firsts, axis=0)
    part = dot("tm,tn->mn", half(a, 1, side), mine) + half(came, 0, side) + first
    for axis, bit in order[1:]:
        which = axis_bit(axis, bit)
        came = yield half(part, 0, 1 - which).astype(BF16), axis, bit
        part = half(part, 0, which) + came
    return part.astype(BF16)


def product_halves(a, b, halving):
    core = axis_bit("seq", 0)
    blocks = 1 << len(halving)

    def part(which):
        value = dot("tm,tn->mn", a, half(b, 1, which)).astype(BF16)
        return value.reshape(blocks, -1, value.shape[1])

    return part(1 - core), part(core)


def own_halves(a, b, halving):
    core = axis_bit("seq", 0)
    blocks = 1 << len(halving)

    def part(which):
        value = dot("ktm,knt->mn", half(a, 2, which), b).astype(BF16)
        return value.reshape(blocks, -1, value.shape[1])

    return part(1 - core), part(core)


def reduce_own(a, b, bits):
    core = axis_bit("seq", 0)
    came = yield dot("ktm,knt->mn", half(a, 2, 1 - core), b).astype(BF16), "seq", 0
    part = dot("ktm,knt->mn", half(a, 2, core), b) + came
    for bit in bits:
        which = axis_bit("seq", bit)
        came = yield half(part, 0, 1 - which).astype(BF16), "seq", bit
        part = half(part, 0, which) + came
    return part.astype(BF16)


def finish_kernel(halvings, rounds, done, turns, sizes, *refs):
    fresh, count = len(halvings), len(rounds)
    stages = len(rounds[0])
    steps = [len(halving) for halving in halvings]
    at = 2 * fresh + count - fresh
    sents, mines, pieces = refs[:fresh], refs[fresh : 2 * fresh], refs[2 * fresh : at]
    outs, scratch = refs[at : at + count], list(refs[at + count :])
    own_sem, half_send, half_recv, send_sem, recv_sem = scratch[:5]
    scratch = scratch[5:]
    buffers = []
    for flow in range(fresh):
        first, total, piece = scratch[:3]
        pairs = [(scratch[3 + 2 * step], scratch[4 + 2 * step]) for step in range(steps[flow] - 1)]
        scratch = scratch[1 + 2 * steps[flow] :]
        buffers.append((first, total, piece, pairs))
    index = {axis: lax.axis_index(axis) for axis in sizes}

    def bit_of(axis, bit):
        return lax.rem(index[axis] // (1 << bit), 2)

    def partner(axis, bit):
        return {axis: index[axis] + (1 << bit) * (1 - 2 * bit_of(axis, bit))}

    barrier = pltpu.get_barrier_semaphore()
    for axis, bit in rounds[0]:
        pl.semaphore_signal(barrier, inc=1, device_id=partner(axis, bit), device_id_type=pl.DeviceIdType.MESH)
    slots = []
    for flow in range(count):
        slot = 0
        for stage, (axis, bit) in enumerate(rounds[flow]):
            slot = slot + bit_of(axis, bit) * (1 << stage)
        slots.append(slot)

    def region(flow, stage):
        size = 1 << stage
        return outs[flow].at[pl.ds(slots[flow] // size * size, size)]

    def own(flow, source):
        return pltpu.make_async_copy(source, region(flow, done[flow]), own_sem.at[flow])

    def send(source, target, send, recv, stage):
        copy = pltpu.make_async_remote_copy(
            src_ref=source, dst_ref=target, send_sem=send, recv_sem=recv, device_id=partner(*stage), device_id_type=pl.DeviceIdType.MESH
        )
        copy.start()
        return copy

    owns = {flow: own(flow, pieces[flow - fresh]) for flow in range(fresh, count)}
    for copy in owns.values():
        copy.start()
    pl.semaphore_wait(barrier, stages)
    halves, copies = {}, {}
    place = [0] * fresh

    def reduce_step(flow, step):
        first, total, piece, pairs = buffers[flow]
        if step == 0:
            halves[flow, 0] = send(sents[flow], first, half_send.at[flow, 0], half_recv.at[flow, 0], halvings[flow][0])
            return
        halves[flow, step - 1].wait_recv()
        if step == 1:
            total[...] = mines[flow][...].astype(F32) + first[...].astype(F32)
        else:
            size = pairs[step - 2][1].shape[0]
            kept = pl.ds(place[flow], size)
            total[kept] = total[kept] + pairs[step - 2][1][...].astype(F32)
        if step < steps[flow]:
            sent, came = pairs[step - 1]
            size = sent.shape[0]
            side = bit_of(*halvings[flow][step])
            sent[...] = total[pl.ds(place[flow] + (1 - side) * size, size)].astype(BF16)
            place[flow] = place[flow] + side * size
            halves[flow, step] = send(sent, came, half_send.at[flow, step], half_recv.at[flow, step], halvings[flow][step])
        else:
            piece[...] = total[pl.ds(place[flow], 1)].astype(BF16)
            owns[flow] = own(flow, piece)
            owns[flow].start()

    def gather_step(flow, step):
        stage = done[flow] + step
        if step == 0:
            owns[flow].wait()
        else:
            copies[flow, stage - 1].wait_recv()
        if stage < stages:
            here = region(flow, stage)
            copies[flow, stage] = send(here, here, send_sem.at[flow, stage], recv_sem.at[flow, stage], rounds[flow][stage])

    for turn in range(max(steps) + stages + 1):
        for flow in range(count):
            if flow < fresh:
                if turn <= steps[flow]:
                    reduce_step(flow, turn)
                if 0 <= turn - steps[flow] <= stages:
                    gather_step(flow, turn - steps[flow])
            elif turn in turns:
                gather_step(flow, turns.index(turn))
    for copy in list(halves.values()) + list(copies.values()):
        copy.wait_send()


def finish_everywhere(sents, mines, halvings, pieces, rounds):
    stages = len(rounds[0])
    fresh, count = len(sents), len(rounds)
    shapes = [sent.shape[1:] for sent in sents] + [piece.shape[1:] for piece in pieces]
    kinds = [BF16] * fresh + [piece.dtype for piece in pieces]
    done = [0] * fresh + [piece.shape[0].bit_length() - 1 for piece in pieces]
    branch = len([stage for stage in rounds[0] if stage[0] == "branch"])
    seq = stages - 1 - branch
    turns = list(range(seq + 1)) + [seq + 1 + 2 * at for at in range(1, branch)]
    turns = turns + [max(turns) + 3, max(turns) + 4]
    buffers = []
    for sent, halving in zip(sents, halvings):
        blocks, rows, columns = sent.shape
        buffers += [pltpu.VMEM(sent.shape, BF16), pltpu.VMEM(sent.shape, F32), pltpu.VMEM((1, rows, columns), BF16)]
        for step in range(1, len(halving)):
            buffers += [pltpu.VMEM((blocks >> step, rows, columns), BF16)] * 2
    most = max(len(halving) for halving in halvings)
    return pl.pallas_call(
        functools.partial(finish_kernel, halvings, rounds, done, turns, ("branch", "seq")),
        out_shape=tuple(jax.ShapeDtypeStruct((1 << stages,) + shape, kind) for shape, kind in zip(shapes, kinds)),
        in_specs=[pl.BlockSpec(memory_space=pltpu.VMEM)] * (2 * fresh + len(pieces)),
        out_specs=(pl.BlockSpec(memory_space=pl.ANY),) * count,
        scratch_shapes=[
            pltpu.SemaphoreType.DMA((count,)),
            pltpu.SemaphoreType.DMA((fresh, most)),
            pltpu.SemaphoreType.DMA((fresh, most)),
            pltpu.SemaphoreType.DMA((count, stages)),
            pltpu.SemaphoreType.DMA((count, stages)),
        ]
        + buffers,
        compiler_params=pltpu.CompilerParams(collective_id=0, has_side_effects=True, vmem_limit_bytes=60 * 2**20),
        name="gradient_finish",
    )(*sents, *mines, *pieces)


def columns_kernel(pieces_ref, *refs):
    out_ref = refs[-1]
    count, rows, columns = pieces_ref.shape[2:]
    for core in range(2):
        for at in range(count):
            out_ref[0, at * rows : (at + 1) * rows, core * columns : (core + 1) * columns] = pieces_ref[core, 0, at].astype(F32)


def groups_kernel(groups, branch_first, pieces_ref, *refs):
    out_ref = refs[-1]
    rows, columns = pieces_ref.shape[3:]
    depth = pieces_ref.shape[1 if branch_first else 2]
    for place, group in enumerate(groups):
        for at in range(depth):
            piece = pieces_ref[0, at, place] if branch_first else pieces_ref[0, place, at]
            out_ref[0, at * rows : (at + 1) * rows, group * columns : (group + 1) * columns] = piece.astype(F32)


def write_layer(kernel, name, gathered, block, index, steps, shape, layer, layers, base):
    rows, width = shape
    ins = [pl.BlockSpec(block, index)]
    operands = [gathered]
    aliases = {}
    if base is not None:
        ins.append(pl.BlockSpec(memory_space=pl.ANY))
        operands.append(base)
        aliases = {1: 0}
    return pl.pallas_call(
        kernel,
        grid=(steps,),
        in_specs=ins,
        out_specs=pl.BlockSpec((1, rows // steps, width), lambda at: (layer, at, 0)),
        out_shape=jax.ShapeDtypeStruct((layers, rows, width), F32),
        input_output_aliases=aliases,
        compiler_params=pltpu.CompilerParams(vmem_limit_bytes=48 * 2**20),
        name=name,
    )(*operands)


def branch_places(order):
    stages = [stage for stage in order if stage[0] == "branch"]
    return [stages.index(("branch", bit)) for bit in range(len(stages))]


def write_columns(gathered, order, halving, layer, layers, base):
    pieces, rows, columns = gathered.shape
    places = branch_places(order)
    branch = 1 << len(places)
    seq = pieces // (2 * branch)

    def index(at):
        slot = 0
        for rank, (_, bit) in enumerate(halving[: len(places)]):
            slot = slot + (at // (1 << (len(places) - 1 - rank))) % 2 * (1 << places[bit])
        return 0, slot, 0, 0, 0

    gathered = gathered.reshape(2, branch, seq, rows, columns)
    shape = (branch * seq * rows, 2 * columns)
    return write_layer(columns_kernel, "gradient_columns", gathered, (2, 1, seq, rows, columns), index, branch, shape, layer, layers, base)


def write_groups(gathered, order, layer, layers, base):
    pieces, rows, columns = gathered.shape
    places = branch_places(order)
    branch = 1 << len(places)
    seq = pieces // (2 * branch)
    groups = [sum(((at >> place) & 1) << bit for bit, place in enumerate(places)) for at in range(branch)]
    branch_first = order[0][0] == "branch"
    split = (seq, branch) if branch_first else (branch, seq)
    gathered = gathered.reshape((2,) + split + (rows, columns))
    kernel = functools.partial(groups_kernel, groups, branch_first)
    shape = (2 * seq * rows, branch * columns)
    return write_layer(kernel, "gradient_groups", gathered, (1,) + split + (rows, columns), lambda at: (at, 0, 0, 0, 0), 2, shape, layer, layers, base)


def layer_forward(stream, weights, gain, shift, side, tables, geometry):
    w_in, w_out, w_up, w_down = weights
    first = geometry["first"]
    xhat, _ = normalize(stream)
    normed = (xhat * gain[0] + shift[0]).astype(BF16)
    projected = (dot("dc,td->ct", w_in, normed) * tables["scale"][:, None]).astype(BF16)
    rows = swap(split_groups(projected, geometry["branch"]))
    q, kv = prepare(first, rows, side, tables["full"], tables["kf"])
    far = Task(gather_far(kv, geometry))
    lower = None
    for part in range(2):
        flights, q = start([far], q)
        lower = lower_forward(q, kv, tables["f0"], tables["f1"], part, 2, lower)
        land(flights, lower)
    normed_all = lax.all_gather(pin(lower, normed), "branch", axis=0, tiled=False)
    while not far.done:
        flights, lower = start([far], lower)
        land(flights, lower)
    r2, r3, r4 = far.result
    att, qb = upper_forward(q, lower, r2, r3, r4, tables["f2"], tables["f3"], tables["f4"])
    saved_parts = (kv, r2, r3, r4, qb, att)
    att_rows = join_groups(swap(to_rows(first, att, tables["narrow"])))
    midway = stream + dot("ct,cd->td", att_rows, w_out)
    xhat, _ = normalize(midway)
    second = (xhat * gain[1] + shift[1]).astype(BF16)
    pre_act = dot("td,df->tf", second, w_up)
    hidden = (0.5 * pre_act * (1.0 + lax.erf(pre_act * np.float32(2**-0.5)))).astype(BF16)
    result = midway + dot("tf,fd->td", hidden, w_down)
    return result, (stream, normed_all, saved_parts, att_rows, midway, second, pre_act, hidden)


def layer_backward(gradient, saved, weights, gain, shift, tables, geometry, old, flights, last):
    w_in, w_out, w_up, w_down = weights
    stream, normed_all, parts, att_rows, midway, second, pre_act, hidden = saved
    kv, r2, r3, r4, qb, att = parts
    first = geometry["first"]
    halving = halving_order()
    seq_bits = [bit for _, bit in bits_of("seq", 1)]

    down_in = gradient.astype(BF16)
    new, ahead = [], []
    if not last:
        down = Task(reduce_product(hidden, down_in, halving))
        ahead, down_in = start([down], down_in)
    grad_hidden = dot("td,fd->tf", down_in, w_down)
    cdf = 0.5 * (1.0 + lax.erf(pre_act * np.float32(2**-0.5)))
    density = jnp.exp(-0.5 * pre_act * pre_act) * np.float32((2 * np.pi) ** -0.5)
    grad_pre = (grad_hidden * (cdf + pre_act * density)).astype(BF16)
    grad_second = dot("tf,mf->tm", grad_pre, w_up)
    back, gain_two, shift_two = normalize_back(midway, gain[1], grad_second)
    grad_midway = gradient + back
    out_in = grad_midway.astype(BF16)
    grad_rows = split_groups(dot("cd,td->ct", w_out, out_in).astype(BF16), geometry["branch"])
    land(flights + ahead, grad_rows)
    grad_rows, second, att_rows = lax.optimization_barrier((grad_rows, second, att_rows))
    if not last:
        ahead, grad_rows = start([down], grad_rows)
    waiting, grad_rows = start(old, grad_rows)
    rows = swap(grad_rows)
    if last:
        new = [
            product_halves(hidden, down_in, flipped_order()),
            product_halves(second, grad_pre, halving),
            product_halves(att_rows.T, out_in, halving),
        ]
        rows = pin(new, rows)
        ours = []
    else:
        up = Task(reduce_product(second, grad_pre, halving, 2))
        out = Task(reduce_product(att_rows.T, out_in, halving))
        rows = pin([up.pending[0], out.pending[0]], rows)
        new = [down, up, out]
        ours = new
    flights, rows = start(ours[1:], rows)
    g = prepare_back(first, rows, tables["narrow"], att)
    du, d2, d3, d4 = upper_back(qb, g, r2, r3, r4, tables["f2"], tables["f3"], tables["f4"])
    far = Task(return_far(d2, d3, d4, geometry))
    short, _ = start([far], d2)
    land(flights + ahead + waiting, du)
    land(short, d2)
    grads = None
    for part in range(2):
        flights, qb = start([far] + ours + old, qb)
        grads = lower_back(qb, g, kv, tables["f0"], tables["f1"], part, 2, grads)
        land(flights, grads)
    dq, dkv = grads
    flights, dq = start(ours + old, dq)
    back_rows = to_rows_back(first, dq, du, dkv, far.result, tables["full"], SIZE**-0.5)
    returned = swap(back_rows)
    normed_all, back_rows = lax.optimization_barrier((normed_all, back_rows))
    if last:
        enter = own_halves(normed_all, back_rows, bits_of("seq", 1))
        returned = pin(enter, returned)
    else:
        enter = Task(reduce_own(normed_all, back_rows, seq_bits))
        returned = pin(enter.pending[0], returned)
        extra, returned = start([enter], returned)
        flights = flights + extra
    projected = join_groups(returned)
    grad_first = dot("ct,dc->td", projected, w_in)
    back, gain_one, shift_one = normalize_back(stream, gain[0], grad_first)
    vectors = jnp.stack([gain_one, gain_two, shift_one, shift_two])
    return grad_midway + back, vectors, new + [enter], flights


def local(tile_embeddings, tile_valid, slide_bounds, norm_gain, norm_bias, attention_in, attention_out, hidden_up, hidden_down, cotangent):
    branch = lax.axis_size("branch")
    seq = lax.axis_size("seq")
    heads = H // branch
    rows, width = tile_embeddings.shape
    shard = rows * branch
    blocks = shard // BLOCK
    seq_at = lax.axis_index("seq")
    origin = seq_at * shard
    bit = 1 if blocks == 2 else 0

    def slide_at(place):
        return jnp.sum((place >= slide_bounds[1:-1]).astype(jnp.int32))

    def same(mask):
        return slide_at((seq_at ^ mask) * shard) == slide_at(origin)

    low, high = 1 << bit, 2 << bit
    geometry = dict(
        branch=branch,
        blocks=blocks,
        bit=bit,
        first=(lax.axis_index("branch") * heads).astype(jnp.int32).reshape(1),
        same=(None, same(low), same(high), same(high | low)),
    )
    full, narrow = placements(heads)
    scale = np.where((np.arange(3 * SIZE * H) // SIZE) % 3 == 0, LOG2E * SIZE**-0.5, 1.0)
    tables = dict(
        full=jnp.asarray(full),
        narrow=jnp.asarray(narrow),
        kf=jnp.asarray(key_features()),
        scale=jnp.asarray(scale, F32),
        f0=jnp.asarray(query_features(block_classes, 0)),
        f1=jnp.asarray(query_features(block_classes[:512], 1)),
        f2=jnp.asarray(query_features(upper_classes, 2)),
        f3=jnp.asarray(query_features(upper_classes[:256], 3)),
        f4=jnp.asarray(query_features(upper_classes[:128], 4)),
    )
    valid = lax.dynamic_slice_in_dim(tile_valid, origin, shard)
    valid = valid.reshape(branch, rows // 16, 16).swapaxes(1, 2).reshape(shard, 1)
    side = jnp.where((lanes_of((1, 128)) == BIAS) & (valid != 1), NEG, 0.0).astype(BF16)

    layers = attention_in.shape[0]
    weights = [(attention_in[at], attention_out[at], hidden_up[at], hidden_down[at]) for at in range(layers)]
    stream = to_major(tile_embeddings).astype(F32)
    outputs, saved_all = [], []
    for layer in range(layers):
        stream, saved = layer_forward(stream, weights[layer], norm_gain[layer], norm_bias[layer], side, tables, geometry)
        outputs.append(from_major(stream.astype(BF16)))
        saved_all.append(saved)
    gradient = to_major(cotangent).astype(F32)
    vectors = [None] * layers
    tasks, flights = [], []
    first_round, flipped = doubling_order(False), doubling_order(True)
    rounds = [[flipped, first_round, first_round, first_round] for _ in range(layers)]
    rounds[0][3] = doubling_order(True, branch_first=True)
    for layer in reversed(range(layers)):
        gradient, vectors[layer], new, flights = layer_backward(
            gradient, saved_all[layer], weights[layer], norm_gain[layer], norm_bias[layer], tables, geometry, tasks, flights, layer == 0
        )
        if layer:
            tasks = tasks + new
    land(flights, gradient)
    for task in tasks:
        while not task.done:
            task.advance(jax.tree.map(lambda v: exchange(v, *task.pending[1:]), task.pending[0]))
    core = [("seq", 0)]
    halving = halving_order()
    halvings = [core + flipped_order(), core + halving, core + halving, core + bits_of("seq", 1)]
    pieces = [task.result[None] for task in tasks] + [jnp.stack(vectors).reshape(1, -1, width)]
    order = rounds[0] + [order for layer in reversed(range(1, layers)) for order in rounds[layer]] + [first_round]
    gathered = finish_everywhere([sent for sent, _ in new], [mine for _, mine in new], halvings, pieces, order)
    places = [(0, member) for member in range(4)] + [(layer, member) for layer in reversed(range(1, layers)) for member in range(4)]
    vectors = jnp.sum(gathered[-1], axis=0).reshape(layers, 2, 2, width)
    sums = [None] * 4
    for (layer, member), whole in zip(places, gathered[:-1]):
        if member == 3:
            sums[member] = write_groups(whole, rounds[layer][member], layer, layers, sums[member])
        else:
            follows = halvings[member][1:] if layer == 0 else halving
            sums[member] = write_columns(whole, rounds[layer][member], follows, layer, layers, sums[member])
    down, up, out, enter = sums
    return (jnp.stack(outputs), from_major(gradient), vectors[:, 0], vectors[:, 1], enter, out, up, down)


def solution(mesh):
    split = P(("seq", "branch"), None)
    in_specs = (split,) + (P(),) * 8 + (split,)
    out_specs = (P(None, ("seq", "branch"), None), split) + (P(),) * 6
    return jax.shard_map(local, mesh=mesh, in_specs=in_specs, out_specs=out_specs, check_vma=False)
```

```python
import functools
import numpy as np
import jax
import jax.numpy as jnp
from jax import lax
from jax.experimental import pallas as pl
from jax.experimental.pallas import tpu as pltpu
from jax.sharding import PartitionSpec as P

BLOCK = 1024
CHUNK = 32
ORDER = (0, 8, 4, 12, 2, 10, 6, 14, 1, 9, 5, 13, 3, 11, 7, 15)
ONE, BIAS, HIGH, LOW, VALUE = 48, 51, 52, 57, 64
NEG = -1e30
LOG2E = 1.4426950408889634
LN2 = 0.6931471805599453
F32, BF16 = jnp.float32, jnp.bfloat16


def low_np(x):
    return np.asarray(x, np.float32).astype(jnp.bfloat16).astype(np.float32)


def query_features(classes, level):
    table = np.zeros((len(classes), 128), np.float32)
    table[:, BIAS] = 1.0
    for at, mine in enumerate(classes):
        for theirs in range(5):
            met = min(mine, theirs) - level + 1
            value = np.log2(met) if met > 0 else NEG
            high = low_np(value)
            table[at, HIGH + theirs] = high
            table[at, LOW + theirs] = low_np(value - high) if met > 0 else 0.0
    return table.astype(jnp.bfloat16)


block_classes = [4] * 64 + [3] * 64 + [2] * 128 + [1] * 256 + [0] * 512
upper_classes = [4] * 128 + [3] * 128 + [2] * 256


def key_features():
    table = np.zeros((BLOCK, 128), np.float32)
    table[:, ONE : ONE + 3] = 1.0
    for at, mine in enumerate(block_classes):
        table[at, HIGH + mine] = 1.0
        table[at, LOW + mine] = 1.0
    return table.astype(jnp.bfloat16)


def nt(a, b):
    return lax.dot_general(a, b, (((1,), (1,)), ((), ())), preferred_element_type=F32)


def tn(a, b):
    return lax.dot_general(a, b, (((0,), (0,)), ((), ())), preferred_element_type=F32)


def nn(a, b):
    return lax.dot_general(a, b, (((1,), (0,)), ((), ())), preferred_element_type=F32)


def lanes_of(shape):
    return lax.broadcasted_iota(jnp.int32, shape, len(shape) - 1)


def split3(column):
    high = column.astype(BF16)
    rest = column - high.astype(F32)
    mid = rest.astype(BF16)
    last = (rest - mid.astype(F32)).astype(BF16)
    return high, mid, last


def place3(base, column):
    high, mid, last = split3(column)
    lane = lanes_of(base.shape)
    out = jnp.where(lane == ONE, high.astype(F32), base)
    out = jnp.where(lane == ONE + 1, mid.astype(F32), out)
    return jnp.where(lane == ONE + 2, last.astype(F32), out)


def chunk_row(head, block, position, part, per_dev):
    residue = lax.rem(ORDER[position] + head, 16)
    return pl.multiple_of((2 * block + part) * per_dev + residue * CHUNK, CHUNK)


def prepare_kernel(heads, blocks, scale, bits, layer, x_ref, side_ref, weights_ref, kf_ref, q_ref, kv_ref, *refs):
    near_refs, (all_ref, rows_all, work, placed, weight_ref, send_sem, recv_sem, in_sem, out_sem) = refs[:3], refs[3:]
    weight = pltpu.make_async_copy(weights_ref.at[layer], weight_ref, in_sem)
    weight.start()
    me = lax.axis_index("branch")
    count, rows = rows_all.shape[:2]

    def away(mask):
        place = me
        for bit in range(bits):
            if mask >> bit & 1:
                place = place + (1 << bit) * (1 - 2 * lax.rem(me // (1 << bit), 2))
        return place

    def place_weight(head):
        shape = (weight_ref.shape[1], 256)
        lane = lax.broadcasted_iota(jnp.int32, shape, 1)
        column = lax.broadcasted_iota(jnp.int32, shape, 0) - (me * heads + head) * 144
        query = (lane < 48) & (column == lane)
        key = (lane >= 128) & (lane < 176) & (column == lane - 80)
        value = (lane >= 128 + VALUE) & (lane < 128 + VALUE + 48) & (column == lane - (32 + VALUE))
        chosen = (query | key | value).astype(F32).astype(BF16)
        placed[head] = nn(weight_ref[...], chosen).astype(BF16)

    barrier = pltpu.get_barrier_semaphore()
    for bit in range(bits):
        pl.semaphore_signal(barrier, inc=1, device_id={"branch": away(1 << bit)}, device_id_type=pl.DeviceIdType.MESH)
    rows_all[pl.ds(me, 1)] = x_ref[...][None]
    pl.semaphore_wait(barrier, bits)
    orders = (list(range(bits)), list(range(bits))[::-1])
    size = rows // 2
    copies = {}

    def begin(flow, stage):
        order = orders[flow]
        masks = [0]
        for bit in order[:stage]:
            masks = masks + [mask | 1 << bit for mask in masks]
        for number, mask in enumerate(masks):
            place = (1 << stage) - 1 + number
            here = rows_all.at[away(mask), pl.ds(flow * size, size)]
            copy = pltpu.make_async_remote_copy(
                src_ref=here,
                dst_ref=here,
                send_sem=send_sem.at[flow, place],
                recv_sem=recv_sem.at[flow, place],
                device_id={"branch": away(1 << order[stage])},
                device_id_type=pl.DeviceIdType.MESH,
            )
            copy.start()
            copies.setdefault((flow, stage), []).append(copy)

    def project(mask):
        place = away(mask)
        at = pl.multiple_of(place * rows, rows)
        source = rows_all[place]
        for head in range(heads):
            value = nn(source, placed[head])
            work[head, pl.ds(at, rows), :128] = (value[:, :128] * scale).astype(BF16)
            work[head, pl.ds(at, rows), 128:] = value[:, 128:].astype(BF16)

    for stage in range(bits):
        for flow in range(2):
            if stage > 0:
                for copy in copies[flow, stage - 1]:
                    copy.wait_recv()
            begin(flow, stage)
        if stage == 0:
            weight.wait()
            for head in range(heads):
                place_weight(head)
            project(0)
    for flow in range(2):
        for copy in copies[flow, bits - 1]:
            copy.wait_recv()
    kept = pltpu.make_async_copy(rows_all, all_ref, out_sem)
    kept.start()
    for mask in range(1, count):
        project(mask)
    kf = kf_ref[...]
    for head in range(heads):
        which = me * heads + head
        for position in range(16):
            features = kf[position * 64 : position * 64 + CHUNK]
            for block in range(blocks):
                for part in range(2):
                    row = chunk_row(which, block, position, part, rows)
                    at = position * 64 + part * CHUNK
                    source = work[head, pl.ds(row, CHUNK), :]
                    q_ref[head, block, at : at + CHUNK, :] = source[:, :128]
                    key_value = source[:, 128:] + features + side_ref[pl.ds(row, CHUNK), :]
                    kv_ref[head, block, at : at + CHUNK, :] = key_value
                    for near_ref in near_refs:
                        if at < near_ref.shape[2]:
                            near_ref[head, block, at : at + CHUNK, :] = key_value
    kept.wait()
    for group in copies.values():
        for copy in group:
            copy.wait_send()


def prepare(rows, side, weights, layer, kf, scale, count):
    heads = weights.shape[2] // (144 * count)
    total = rows.shape[0] * count
    blocks = total // BLOCK
    bits = count.bit_length() - 1
    shape = jax.ShapeDtypeStruct((heads, blocks, BLOCK, 128), BF16)
    whole = (count,) + rows.shape
    near = tuple(jax.ShapeDtypeStruct((heads, blocks, size, 128), BF16) for size in (256, 128, 64))
    return pl.pallas_call(
        functools.partial(prepare_kernel, heads, blocks, scale, bits, layer),
        out_shape=(shape, shape) + near + (jax.ShapeDtypeStruct(whole, BF16),),
        in_specs=[pl.BlockSpec(memory_space=pltpu.VMEM if at != 2 else pl.ANY) for at in range(4)],
        out_specs=(pl.BlockSpec(memory_space=pltpu.VMEM),) * 5 + (pl.BlockSpec(memory_space=pl.ANY),),
        scratch_shapes=[
            pltpu.VMEM(whole, BF16),
            pltpu.VMEM((heads, total, 256), BF16),
            pltpu.VMEM((heads, weights.shape[1], 256), BF16),
            pltpu.VMEM(weights.shape[1:], BF16),
            pltpu.SemaphoreType.DMA((2, count - 1)),
            pltpu.SemaphoreType.DMA((2, count - 1)),
            pltpu.SemaphoreType.DMA,
            pltpu.SemaphoreType.DMA,
        ],
        compiler_params=pltpu.CompilerParams(collective_id=1 + layer, has_side_effects=True, vmem_limit_bytes=48 * 2**20),
        name="attention_prepare",
    )(rows, side, weights, kf)


def lower_kernel(q_ref, kv_ref, f0_ref, f1_ref, *refs):
    o_ref = refs[-1]
    step = 256
    for block in range(2):
        own = kv_ref[0, block]
        near = kv_ref[0, 1 - block, :512]
        for at in range(0, BLOCK, step):
            rows = slice(at, at + step)
            base = q_ref[0, block, rows]
            s0 = nt(base + f0_ref[rows], own)
            top = jnp.max(s0, axis=1, keepdims=True)
            if at < 512:
                s1 = nt(base + f1_ref[rows], near)
                top = jnp.maximum(top, jnp.max(s1, axis=1, keepdims=True))
            own_rows = own[rows].astype(F32)
            meet = base.astype(F32) * own_rows
            alone = jnp.sum(meet, axis=1, keepdims=True)
            lane = lanes_of(own_rows.shape)
            bias = jnp.min(jnp.where(lane == BIAS, own_rows, 0.0), axis=1, keepdims=True)
            classes = sum((lax.broadcasted_iota(jnp.int32, (step, 1), 0) + at < edge).astype(F32) for edge in (512, 256, 128, 64))
            alone = jnp.where(bias < 0.0, alone + jnp.log2(classes + 1.0), NEG)
            top = jnp.maximum(top, alone)
            out = nn(jnp.exp2(s0 - top).astype(BF16), own)
            if at < 512:
                out = out + nn(jnp.exp2(s1 - top).astype(BF16), near)
            out = out + jnp.exp2(alone - top) * own_rows
            o_ref[0, block, rows] = jnp.where(lane == 0, top, out)


def part_call(kernel, name, operands, tables, outs, part, parts, base, cost):
    heads, blocks = operands[0].shape[:2]
    count = heads // parts
    spec = pl.BlockSpec((1, 2, BLOCK, 128), lambda h, p: (h + part * count, p, 0, 0))
    whole = lambda a: pl.BlockSpec(a.shape, lambda h, p: (0,) * a.ndim)
    ins = [spec] * len(operands) + [whole(table) for table in tables]
    arrays = list(operands) + list(tables)
    aliases = {}
    if base is not None:
        for at, array in enumerate(base):
            aliases[len(arrays)] = at
            arrays.append(array)
            ins.append(pl.BlockSpec(memory_space=pl.ANY))
    pairs = int(count * blocks * 1.25 * 2**20)
    return pl.pallas_call(
        kernel,
        grid=(count, blocks // 2),
        in_specs=ins,
        out_specs=(spec,) * outs,
        out_shape=(jax.ShapeDtypeStruct(operands[0].shape, F32),) * outs,
        input_output_aliases=aliases,
        compiler_params=pltpu.CompilerParams(vmem_limit_bytes=56 * 2**20),
        cost_estimate=pl.CostEstimate(flops=pairs * 256 * cost, bytes_accessed=operands[0].size * 8 // parts, transcendentals=pairs),
        name=name,
    )(*arrays)


def lower_forward(q, kv, f0, f1, part, parts, base):
    out = part_call(lower_kernel, "attention_lower", (q, kv), (f0, f1), 1, part, parts, None if base is None else (base,), 4)
    return out[0]


UPPER = ((0, 0, 64), (1, 0, 64), (0, 64, 128), (1, 64, 128), (0, 128, 256), (1, 128, 256))


def gather_upper(ref, lead):
    return jnp.concatenate([ref[(*lead, block, slice(low, high))] for block, low, high in UPPER], axis=0)


def upper_kernel(q_ref, o_ref, r2_ref, r3_ref, r4_ref, f2_ref, f3_ref, f4_ref, att_ref, qb_ref):
    merged = {}
    uq = gather_upper(q_ref, (0,))
    ol = gather_upper(o_ref, (0,))
    for low, high in ((0, 128), (128, 256), (256, 512)):
        base = uq[low:high]
        pairs = [(nt(base + f2_ref[low:high], r2_ref[0, 0]), r2_ref[0, 0])]
        if high <= 256:
            pairs.append((nt(base + f3_ref[low:high], r3_ref[0]), r3_ref[0]))
        if high <= 128:
            pairs.append((nt(base + f4_ref[low:high], r4_ref[0]), r4_ref[0]))
        old = ol[low:high]
        lane = lanes_of(old.shape)
        before = old[:, 0:1]
        top = before
        for scores, keys in pairs:
            top = jnp.maximum(top, jnp.max(scores, axis=1, keepdims=True))
        out = old * jnp.exp2(before - top)
        for scores, keys in pairs:
            out = out + nn(jnp.exp2(scores - top).astype(BF16), keys)
        merged[low] = jnp.where(lane == 0, top, out)
    whole = jnp.concatenate([merged[0], merged[128], merged[256]], axis=0)
    place = 0

    def finish(block, low, high, rows):
        lane = lanes_of(rows.shape)
        top = rows[:, 0:1]
        total = rows[:, ONE : ONE + 1]
        att_ref[0, block, low:high] = jnp.where((lane >= VALUE) & (lane < VALUE + 48), rows / total, 0.0)
        lse = top + jnp.log2(total)
        qb_ref[0, block, low:high] = place3(q_ref[0, block, low:high].astype(F32), -lse).astype(BF16)

    for block, low, high in UPPER:
        finish(block, low, high, whole[place : place + high - low])
        place += high - low
    for block in range(2):
        for low in (256, 512, 768):
            finish(block, low, low + 256, o_ref[0, block, low : low + 256])


def upper_forward(q, o, r2, r3, r4, f2, f3, f4):
    heads, blocks = q.shape[:2]
    spec = pl.BlockSpec((1, 2, BLOCK, 128), lambda h, p: (h, p, 0, 0))
    two = pl.BlockSpec((1, 1, 512, 128), lambda h, p: (h, p, 0, 0))
    far = pl.BlockSpec((1, 512, 128), lambda h, p: (h, 0, 0))
    whole = lambda a: pl.BlockSpec(a.shape, lambda h, p: (0,) * a.ndim)
    return pl.pallas_call(
        upper_kernel,
        grid=(heads, blocks // 2),
        in_specs=[spec, spec, two, far, far, whole(f2), whole(f3), whole(f4)],
        out_specs=(spec, spec),
        out_shape=(jax.ShapeDtypeStruct(q.shape, F32), jax.ShapeDtypeStruct(q.shape, BF16)),
        compiler_params=pltpu.CompilerParams(vmem_limit_bytes=48 * 2**20),
        name="attention_upper",
    )(q, o, r2, r3, r4, f2, f3, f4)


def chunk_place(head, residue, part):
    turn = lax.rem(residue - head + 32, 16)
    position = 8 * lax.rem(turn, 2) + 4 * lax.rem(turn // 2, 2) + 2 * lax.rem(turn // 4, 2) + turn // 8
    return pl.multiple_of(position * 64 + part * CHUNK, CHUNK)


def rows_kernel(heads, blocks, first_ref, a_ref, place_ref, out_ref, work):
    for head in range(heads):
        which = first_ref[0] + head
        for residue in range(16):
            for block in range(blocks):
                for part in range(2):
                    row = (2 * block + part) * 512 + residue * CHUNK
                    at = chunk_place(which, residue, part)
                    work[head, row : row + CHUNK, :] = a_ref[head, block, pl.ds(at, CHUNK), :].astype(BF16)
        for part in range(out_ref.shape[0]):
            value = nt(place_ref[head], work[head, part * 512 : part * 512 + 512]).astype(BF16)
            out_ref[part] = value if head == 0 else out_ref[part] + value


def to_rows(first, att, place):
    heads, blocks = att.shape[:2]
    width = place.shape[1]
    total = blocks * BLOCK
    return pl.pallas_call(
        functools.partial(rows_kernel, heads, blocks),
        out_shape=jax.ShapeDtypeStruct((total // 512, width, 512), BF16),
        in_specs=[pl.BlockSpec(memory_space=pltpu.SMEM)]
        + [pl.BlockSpec(memory_space=pltpu.VMEM)] * 2,
        out_specs=pl.BlockSpec(memory_space=pltpu.VMEM),
        scratch_shapes=[pltpu.VMEM((heads, total, 128), BF16)],
        compiler_params=pltpu.CompilerParams(vmem_limit_bytes=48 * 2**20),
        name="attention_rows",
    )(first, att, place)


def prepare_back_kernel(heads, blocks, first_ref, x_ref, place_ref, att_ref, g_ref, work):
    for head in range(heads):
        for part in range(x_ref.shape[0]):
            work[part * 512 : part * 512 + 512] = tn(x_ref[part], place_ref[head]).astype(BF16)
        which = first_ref[0] + head
        for position in range(16):
            for block in range(blocks):
                for part in range(2):
                    row = chunk_row(which, block, position, part, 512)
                    at = position * 64 + part * CHUNK
                    g_ref[head, block, at : at + CHUNK, :] = work[pl.ds(row, CHUNK), :]
        for block in range(blocks):
            for at in range(0, BLOCK, 256):
                rows = slice(at, at + 256)
                grad = g_ref[head, block, rows].astype(F32)
                dots = jnp.sum(grad * att_ref[head, block, rows], axis=1, keepdims=True)
                g_ref[head, block, rows] = place3(grad, -dots).astype(BF16)


def prepare_back(first, rows, place, att):
    heads, blocks = att.shape[:2]
    total = blocks * BLOCK
    return pl.pallas_call(
        functools.partial(prepare_back_kernel, heads, blocks),
        out_shape=jax.ShapeDtypeStruct(att.shape, BF16),
        in_specs=[pl.BlockSpec(memory_space=pltpu.SMEM)]
        + [pl.BlockSpec(memory_space=pltpu.VMEM)] * 3,
        out_specs=pl.BlockSpec(memory_space=pltpu.VMEM),
        scratch_shapes=[pltpu.VMEM((total, 128), BF16)],
        compiler_params=pltpu.CompilerParams(vmem_limit_bytes=48 * 2**20),
        name="attention_prepare_back",
    )(first, rows, place, att)


def back_tile(kv, key_t, q_scores, g, q):
    probs = jnp.exp2(nt(kv, q_scores))
    grad_scores = (probs * nt(kv, g)).astype(BF16)
    grad_kv = nn(probs.astype(BF16), g) + nn(grad_scores, q)
    return grad_kv, nn(key_t, grad_scores)


def upper_back_kernel(qb_ref, g_ref, r2_ref, r3_ref, r4_ref, f2_ref, f3_ref, f4_ref, dq_ref, d2_ref, d3_ref, d4_ref):
    uq = gather_upper(qb_ref, (0,))
    ug = gather_upper(g_ref, (0,))
    dq = None
    lane = lanes_of((256, 128))
    for ref, out, f_ref, count in ((r2_ref.at[0], d2_ref.at[0], f2_ref, 512), (r3_ref, d3_ref.at[0], f3_ref, 256), (r4_ref, d4_ref.at[0], f4_ref, 128)):
        q = uq[:count]
        g = ug[:count]
        qs = q + f_ref[...]
        total = None
        for at in range(0, 512, 256):
            kv = ref[0, at : at + 256]
            key_t = kv.astype(F32).T[:48].astype(BF16)
            grad_kv, part = back_tile(kv, key_t, qs, g, q)
            out[0, at : at + 256] = jnp.where(lane < 48, grad_kv * LN2, grad_kv).astype(BF16)
            total = part if total is None else total + part
        rows = total.T
        if count < 512:
            rows = jnp.concatenate([rows, jnp.zeros((512 - count, 48), F32)], axis=0)
        dq = rows if dq is None else dq + rows
    dq_ref[0, 0] = jnp.concatenate([dq, jnp.zeros((512, 80), F32)], axis=1)


def upper_back(qb, g, r2, r3, r4, f2, f3, f4):
    heads, blocks = qb.shape[:2]
    pairs = blocks // 2
    spec = pl.BlockSpec((1, 2, BLOCK, 128), lambda h, p: (h, p, 0, 0))
    two = pl.BlockSpec((1, 1, 512, 128), lambda h, p: (h, p, 0, 0))
    far = pl.BlockSpec((1, 512, 128), lambda h, p: (h, 0, 0))
    whole = lambda a: pl.BlockSpec(a.shape, lambda h, p: (0,) * a.ndim)
    shape = (heads, pairs, 512, 128)
    return pl.pallas_call(
        upper_back_kernel,
        grid=(heads, pairs),
        in_specs=[spec, spec, two, far, far, whole(f2), whole(f3), whole(f4)],
        out_specs=(two,) * 4,
        out_shape=(jax.ShapeDtypeStruct(shape, F32),) + (jax.ShapeDtypeStruct(shape, BF16),) * 3,
        compiler_params=pltpu.CompilerParams(vmem_limit_bytes=48 * 2**20),
        name="attention_upper_back",
    )(qb, g, r2, r3, r4, f2, f3, f4)


def lower_back_kernel(qb_ref, g_ref, kv_ref, f0_ref, f1_ref, *refs):
    dq_ref, dkv_ref = refs[-2:]
    step = 256
    lane = lanes_of((step, 128))
    totals = [None, None]
    for block in range(2):
        q = qb_ref[0, block]
        g = g_ref[0, block]
        q0 = q + f0_ref[...]
        far_q = qb_ref[0, 1 - block, :512]
        far_g = g_ref[0, 1 - block, :512]
        far_q1 = far_q + f1_ref[...]
        for at in range(0, BLOCK, step):
            rows = slice(at, at + step)
            kv = kv_ref[0, block, rows]
            key_t = kv.astype(F32).T[:48].astype(BF16)
            grad_kv, part = back_tile(kv, key_t, q0, g, q)
            totals[block] = part if totals[block] is None else totals[block] + part
            if at < 512:
                more_kv, part = back_tile(kv, key_t, far_q1, far_g, far_q)
                grad_kv = grad_kv + more_kv
                part = jnp.concatenate([part, jnp.zeros((48, 512), F32)], axis=1)
                totals[1 - block] = part if totals[1 - block] is None else totals[1 - block] + part
            kv_rows = kv.astype(F32)
            q_rows = q[rows].astype(F32)
            g_rows = g[rows].astype(F32)
            bias = jnp.min(jnp.where(lane == BIAS, kv_rows, 0.0), axis=1, keepdims=True)
            classes = sum((lax.broadcasted_iota(jnp.int32, (step, 1), 0) + at < edge).astype(F32) for edge in (512, 256, 128, 64))
            met = jnp.where(lane < ONE + 3, q_rows * kv_rows, 0.0)
            score = jnp.sum(met, axis=1, keepdims=True) + jnp.log2(classes + 1.0)
            prob = jnp.where(bias < 0.0, jnp.exp2(jnp.where(bias < 0.0, score, NEG)), 0.0)
            grad_score = prob * jnp.sum(jnp.where((lane >= ONE) & (lane != BIAS), g_rows * kv_rows, 0.0), axis=1, keepdims=True)
            grad_kv = grad_kv + prob * g_rows + grad_score * q_rows
            dkv_ref[0, block, rows] = jnp.where(lane < 48, grad_kv * LN2, grad_kv)
            dq_ref[0, block, rows] = grad_score * kv_rows
    for block in range(2):
        for at in range(0, BLOCK, step):
            rows = slice(at, at + step)
            value = totals[block][:, rows].T
            value = jnp.concatenate([value, jnp.zeros((step, 80), F32)], axis=1)
            dq_ref[0, block, rows] = dq_ref[0, block, rows] + value


def lower_back(qb, g, kv, f0, f1, part, parts, base):
    return part_call(lower_back_kernel, "attention_lower_back", (qb, g, kv), (f0, f1), 2, part, parts, base, 10)


def rows_back_kernel(heads, blocks, scale, first_ref, dq_ref, du_ref, dkv_ref, x2_ref, place_ref, out_ref, work, sum_q, sum_kv):
    for head in range(heads):
        for block in range(blocks):
            start = 0
            for ub, low, high in UPPER:
                if ub == block % 2:
                    sum_q[head, block, low:high] = dq_ref[head, block, low:high] + du_ref[head, block // 2, start : start + high - low]
                start += high - low
            sum_q[head, block, 256:] = dq_ref[head, block, 256:]
            sum_kv[head, block, :256] = dkv_ref[head, block, :256] + x2_ref[head, block].astype(F32)
            sum_kv[head, block, 256:] = dkv_ref[head, block, 256:]
        which = first_ref[0] + head
        for residue in range(16):
            for block in range(blocks):
                for part in range(2):
                    row = (2 * block + part) * 512 + residue * CHUNK
                    at = chunk_place(which, residue, part)
                    grad_q = sum_q[head, block, pl.ds(at, CHUNK), :]
                    grad_kv = sum_kv[head, block, pl.ds(at, CHUNK), :]
                    lane = lanes_of(grad_q.shape)
                    work[head, row : row + CHUNK, :128] = jnp.where(lane < 48, grad_q * scale, 0.0).astype(BF16)
                    keep = (lane < 48) | ((lane >= VALUE) & (lane < VALUE + 48))
                    work[head, row : row + CHUNK, 128:] = jnp.where(keep, grad_kv, 0.0).astype(BF16)
        for part in range(out_ref.shape[0]):
            value = nt(place_ref[head], work[head, part * 512 : part * 512 + 512]).astype(BF16)
            out_ref[part] = value if head == 0 else out_ref[part] + value


def to_rows_back(first, dq, du, dkv, x2, place, scale):
    heads, blocks = dq.shape[:2]
    total = blocks * BLOCK
    return pl.pallas_call(
        functools.partial(rows_back_kernel, heads, blocks, scale),
        out_shape=jax.ShapeDtypeStruct((total // 512, place.shape[1], 512), BF16),
        in_specs=[pl.BlockSpec(memory_space=pltpu.SMEM)]
        + [pl.BlockSpec(memory_space=pltpu.VMEM)] * 5,
        out_specs=pl.BlockSpec(memory_space=pltpu.VMEM),
        scratch_shapes=[pltpu.VMEM((heads, total, 256), BF16)] + [pltpu.VMEM(dq.shape, F32)] * 2,
        compiler_params=pltpu.CompilerParams(vmem_limit_bytes=56 * 2**20),
        name="attention_rows_back",
    )(first, dq, du, dkv, x2, place)


def placements(heads):
    full = np.zeros((heads, heads * 144, 256), np.float32)
    narrow = np.zeros((heads, heads * 48, 128), np.float32)
    for head in range(heads):
        for at in range(48):
            full[head, head * 144 + at, at] = 1.0
            full[head, head * 144 + 48 + at, 128 + at] = 1.0
            full[head, head * 144 + 96 + at, 128 + VALUE + at] = 1.0
            narrow[head, head * 48 + at, VALUE + at] = 1.0
    return full.astype(jnp.bfloat16), narrow.astype(jnp.bfloat16)


H = 16
SIZE = 48
eps_norm = 1e-05


def exchange(value, axis, bit):
    count = lax.axis_size(axis)
    return lax.ppermute(value, axis, [(at, at ^ (1 << bit)) for at in range(count)])


def to_major(x):
    rows, width = x.shape
    return x.reshape(rows // 16, 16, width).swapaxes(0, 1).reshape(rows, width)


def from_major(x):
    rows, width = x.shape
    return x.reshape(16, rows // 16, width).swapaxes(0, 1).reshape(rows, width)


def normalize(stream):
    centered = stream - jnp.mean(stream, axis=-1, keepdims=True)
    spread = jnp.mean(centered * centered, axis=-1, keepdims=True)
    scale = lax.rsqrt(spread + eps_norm)
    return centered * scale, scale


def normalize_back(stream, gain, e):
    xhat, scale = normalize(stream)
    dxh = e * gain
    back = scale * (dxh - jnp.mean(dxh, axis=-1, keepdims=True) - xhat * jnp.mean(dxh * xhat, axis=-1, keepdims=True))
    return back, jnp.sum(e * xhat, axis=0), jnp.sum(e, axis=0)


class Task:
    def __init__(self, steps):
        self.steps = steps
        self.pending, self.result, self.done = None, None, False
        self.advance(None)

    def advance(self, value):
        try:
            self.pending = self.steps.send(value)
        except StopIteration as stop:
            self.result, self.pending, self.done = stop.value, None, True


def start(tasks, ins):
    tasks = [task for task in tasks if not task.done]
    operands = [task.pending[0] for task in tasks]
    operands, ins = lax.optimization_barrier((operands, ins))
    flights = [(task, jax.tree.map(lambda v: exchange(v, *task.pending[1:]), operand)) for task, operand in zip(tasks, operands)]
    return flights, ins


def land(flights, outs):
    if flights:
        values, _ = lax.optimization_barrier(([value for _, value in flights], outs))
        for (task, _), value in zip(flights, values):
            task.advance(value)


def gather_far(own2, own3, own4, geometry):
    blocks, same = geometry["blocks"], geometry["same"]
    heads = own2.shape[0]
    if blocks == 2:
        a3 = yield own3, "seq", 1
        a4 = yield jnp.concatenate([own4, a3[:, :, :64]], axis=1), "seq", 2
        r2, b3, b4 = yield (own2, a3, a4), "seq", 0
        r3 = jnp.concatenate([a3, b3], axis=1)
        r4 = jnp.concatenate([a4[:, :2], b4[:, :2], a4[:, 2:], b4[:, 2:]], axis=1)
    else:
        r2 = jnp.concatenate([own2[:, 2:], own2[:, :2]], axis=1)
        r3 = yield own3, "seq", 0
        r4 = yield jnp.concatenate([own4, r3[:, :, :64]], axis=1), "seq", 1
    bias_lane = lanes_of((1, 1, 1, 128)) == BIAS
    r3 = jnp.where(bias_lane & ~same[1], jnp.asarray(NEG, BF16), r3)
    alike = jnp.repeat(jnp.stack([same[2], same[3]]), 4)[None, :, None, None]
    r4 = jnp.where(bias_lane & ~alike, jnp.asarray(NEG, BF16), r4)
    return (
        r2.reshape(heads, blocks // 2, 512, 128),
        r3.reshape(heads, 512, 128),
        r4.reshape(heads, 512, 128),
    )


def return_far(d2, d3, d4, geometry):
    blocks = geometry["blocks"]
    heads = d2.shape[0]

    def fold(d):
        return d[:, 0] if d.shape[1] == 1 else jnp.sum(d.astype(F32), axis=1).astype(BF16)

    def add(a, b):
        return (a.astype(F32) + b.astype(F32)).astype(BF16)

    def grow(d):
        return jnp.concatenate([d, jnp.zeros_like(d)], axis=2)

    d4 = fold(d4).reshape(heads, 8, 64, 128)
    d3 = fold(d3).reshape(heads, 4, 128, 128)
    d2 = d2.reshape(heads, blocks, 256, 128)
    if blocks == 2:
        b4 = jnp.concatenate([d4[:, 2:4], d4[:, 6:8]], axis=1)
        a4 = jnp.concatenate([d4[:, 0:2], d4[:, 4:6]], axis=1)
        x2, y3, y4 = yield (d2, d3[:, 2:], b4), "seq", 0
        x4 = yield add(a4, y4), "seq", 2
        x3 = yield add(add(d3[:, :2], y3), grow(x4[:, 2:])), "seq", 1
        return add(x2, grow(add(x3, grow(x4[:, :2]))))
    x4 = yield d4, "seq", 1
    x3 = yield add(d3, grow(x4[:, 4:])), "seq", 0
    x3 = add(x3, grow(x4[:, :4]))
    x2 = jnp.concatenate([d2[:, 2:], d2[:, :2]], axis=1)
    return add(x2, grow(x3))


def split_groups(value, count):
    return value.reshape(count, -1, value.shape[1])


def join_groups(value):
    return value.reshape(-1, value.shape[2])


def pin(first, then):
    return lax.optimization_barrier((first, then))[1]


def swap(value):
    return lax.all_to_all(value, "branch", split_axis=0, concat_axis=0, tiled=True)


def dot(spec, a, b):
    return jnp.einsum(spec, a, b, preferred_element_type=F32)


def axis_bit(axis, bit):
    return (lax.axis_index(axis) >> bit) & 1


def half(value, axis, which):
    size = value.shape[axis] // 2
    return lax.dynamic_slice_in_dim(value, which * size, size, axis)


def bits_of(axis, low=0):
    return [(axis, bit) for bit in range(low, lax.axis_size(axis).bit_length() - 1)]


def halving_order():
    return bits_of("branch") + bits_of("seq", 1)


def flipped_order():
    return bits_of("branch")[::-1] + bits_of("seq", 1)


def doubling_order(flip, branch_first=False):
    branch = bits_of("branch") if flip else bits_of("branch")[::-1]
    seq = bits_of("seq", 1)[::-1]
    return (branch + seq if branch_first else seq + branch) + [("seq", 0)]


def reduce_product(a, b, order, parts=1):
    core = axis_bit("seq", 0)
    side = axis_bit(*order[0])
    came = yield dot("tm,tn->mn", a, half(b, 1, 1 - core)).astype(BF16), "seq", 0
    mine = half(b, 1, core)
    other = dot("tm,tn->mn", half(a, 1, 1 - side), mine) + half(came, 0, 1 - side)
    size = other.shape[0] // parts
    firsts = []
    for at in range(parts):
        came_part = yield other[at * size : (at + 1) * size].astype(BF16), *order[0]
        firsts.append(came_part)
    first = jnp.concatenate(firsts, axis=0)
    part = dot("tm,tn->mn", half(a, 1, side), mine) + half(came, 0, side) + first
    for axis, bit in order[1:]:
        which = axis_bit(axis, bit)
        came = yield half(part, 0, 1 - which).astype(BF16), axis, bit
        part = half(part, 0, which) + came
    return part.astype(BF16)


def product_halves(a, b, halving):
    core = axis_bit("seq", 0)
    blocks = 1 << len(halving)

    def part(which):
        value = dot("tm,tn->mn", a, half(b, 1, which)).astype(BF16)
        return value.reshape(blocks, -1, value.shape[1])

    return part(1 - core), part(core)


def own_halves(a, b, halving):
    core = axis_bit("seq", 0)
    blocks = 1 << len(halving)

    def part(which):
        value = dot("ktm,knt->mn", half(a, 2, which), b).astype(BF16)
        return value.reshape(blocks, -1, value.shape[1])

    return part(1 - core), part(core)


def reduce_own(a, b, bits):
    core = axis_bit("seq", 0)
    came = yield dot("ktm,knt->mn", half(a, 2, 1 - core), b).astype(BF16), "seq", 0
    part = dot("ktm,knt->mn", half(a, 2, core), b) + came
    for bit in bits:
        which = axis_bit("seq", bit)
        came = yield half(part, 0, 1 - which).astype(BF16), "seq", bit
        part = half(part, 0, which) + came
    return part.astype(BF16)


def finish_kernel(halvings, rounds, done, turns, sizes, *refs):
    fresh, count = len(halvings), len(rounds)
    stages = len(rounds[0])
    steps = [len(halving) for halving in halvings]
    at = 2 * fresh + count - fresh
    sents, mines, pieces = refs[:fresh], refs[fresh : 2 * fresh], refs[2 * fresh : at]
    outs, scratch = refs[at : at + count], list(refs[at + count :])
    own_sem, half_send, half_recv, send_sem, recv_sem = scratch[:5]
    scratch = scratch[5:]
    buffers = []
    for flow in range(fresh):
        first, total, piece = scratch[:3]
        pairs = [(scratch[3 + 2 * step], scratch[4 + 2 * step]) for step in range(steps[flow] - 1)]
        scratch = scratch[1 + 2 * steps[flow] :]
        buffers.append((first, total, piece, pairs))
    index = {axis: lax.axis_index(axis) for axis in sizes}

    def bit_of(axis, bit):
        return lax.rem(index[axis] // (1 << bit), 2)

    def partner(axis, bit):
        return {axis: index[axis] + (1 << bit) * (1 - 2 * bit_of(axis, bit))}

    barrier = pltpu.get_barrier_semaphore()
    for axis, bit in rounds[0]:
        pl.semaphore_signal(barrier, inc=1, device_id=partner(axis, bit), device_id_type=pl.DeviceIdType.MESH)
    slots = []
    for flow in range(count):
        slot = 0
        for stage, (axis, bit) in enumerate(rounds[flow]):
            slot = slot + bit_of(axis, bit) * (1 << stage)
        slots.append(slot)

    def region(flow, stage):
        size = 1 << stage
        return outs[flow].at[pl.ds(slots[flow] // size * size, size)]

    def own(flow, source):
        return pltpu.make_async_copy(source, region(flow, done[flow]), own_sem.at[flow])

    def send(source, target, send, recv, stage):
        copy = pltpu.make_async_remote_copy(
            src_ref=source, dst_ref=target, send_sem=send, recv_sem=recv, device_id=partner(*stage), device_id_type=pl.DeviceIdType.MESH
        )
        copy.start()
        return copy

    owns = {flow: own(flow, pieces[flow - fresh]) for flow in range(fresh, count)}
    for copy in owns.values():
        copy.start()
    pl.semaphore_wait(barrier, stages)
    halves, copies = {}, {}
    place = [0] * fresh

    def reduce_step(flow, step):
        first, total, piece, pairs = buffers[flow]
        if step == 0:
            halves[flow, 0] = send(sents[flow], first, half_send.at[flow, 0], half_recv.at[flow, 0], halvings[flow][0])
            return
        halves[flow, step - 1].wait_recv()
        if step == 1:
            total[...] = mines[flow][...].astype(F32) + first[...].astype(F32)
        else:
            size = pairs[step - 2][1].shape[0]
            kept = pl.ds(place[flow], size)
            total[kept] = total[kept] + pairs[step - 2][1][...].astype(F32)
        if step < steps[flow]:
            sent, came = pairs[step - 1]
            size = sent.shape[0]
            side = bit_of(*halvings[flow][step])
            sent[...] = total[pl.ds(place[flow] + (1 - side) * size, size)].astype(BF16)
            place[flow] = place[flow] + side * size
            halves[flow, step] = send(sent, came, half_send.at[flow, step], half_recv.at[flow, step], halvings[flow][step])
        else:
            piece[...] = total[pl.ds(place[flow], 1)].astype(BF16)
            owns[flow] = own(flow, piece)
            owns[flow].start()

    def gather_step(flow, step):
        stage = done[flow] + step
        if step == 0:
            owns[flow].wait()
        else:
            copies[flow, stage - 1].wait_recv()
        if stage < stages:
            here = region(flow, stage)
            copies[flow, stage] = send(here, here, send_sem.at[flow, stage], recv_sem.at[flow, stage], rounds[flow][stage])

    for turn in range(max(steps) + stages + 1):
        for flow in range(count):
            if flow < fresh:
                if turn <= steps[flow]:
                    reduce_step(flow, turn)
                if 0 <= turn - steps[flow] <= stages:
                    gather_step(flow, turn - steps[flow])
            elif turn in turns:
                gather_step(flow, turns.index(turn))
    for copy in list(halves.values()) + list(copies.values()):
        copy.wait_send()


def finish_everywhere(sents, mines, halvings, pieces, rounds):
    stages = len(rounds[0])
    fresh, count = len(sents), len(rounds)
    shapes = [sent.shape[1:] for sent in sents] + [piece.shape[1:] for piece in pieces]
    kinds = [BF16] * fresh + [piece.dtype for piece in pieces]
    done = [0] * fresh + [piece.shape[0].bit_length() - 1 for piece in pieces]
    branch = len([stage for stage in rounds[0] if stage[0] == "branch"])
    seq = stages - 1 - branch
    turns = list(range(seq + 1)) + [seq + 1 + 2 * at for at in range(1, branch)]
    turns = turns + [max(turns) + 3, max(turns) + 4]
    buffers = []
    for sent, halving in zip(sents, halvings):
        blocks, rows, columns = sent.shape
        buffers += [pltpu.VMEM(sent.shape, BF16), pltpu.VMEM(sent.shape, F32), pltpu.VMEM((1, rows, columns), BF16)]
        for step in range(1, len(halving)):
            buffers += [pltpu.VMEM((blocks >> step, rows, columns), BF16)] * 2
    most = max(len(halving) for halving in halvings)
    return pl.pallas_call(
        functools.partial(finish_kernel, halvings, rounds, done, turns, ("branch", "seq")),
        out_shape=tuple(jax.ShapeDtypeStruct((1 << stages,) + shape, kind) for shape, kind in zip(shapes, kinds)),
        in_specs=[pl.BlockSpec(memory_space=pltpu.VMEM)] * (2 * fresh + len(pieces)),
        out_specs=(pl.BlockSpec(memory_space=pl.ANY),) * count,
        scratch_shapes=[
            pltpu.SemaphoreType.DMA((count,)),
            pltpu.SemaphoreType.DMA((fresh, most)),
            pltpu.SemaphoreType.DMA((fresh, most)),
            pltpu.SemaphoreType.DMA((count, stages)),
            pltpu.SemaphoreType.DMA((count, stages)),
        ]
        + buffers,
        compiler_params=pltpu.CompilerParams(collective_id=0, has_side_effects=True, vmem_limit_bytes=60 * 2**20),
        name="gradient_finish",
    )(*sents, *mines, *pieces)


def columns_kernel(pieces_ref, *refs):
    out_ref = refs[-1]
    count, rows, columns = pieces_ref.shape[2:]
    for core in range(2):
        for at in range(count):
            out_ref[0, at * rows : (at + 1) * rows, core * columns : (core + 1) * columns] = pieces_ref[core, 0, at].astype(F32)


def groups_kernel(groups, branch_first, pieces_ref, *refs):
    out_ref = refs[-1]
    rows, columns = pieces_ref.shape[3:]
    depth = pieces_ref.shape[1 if branch_first else 2]
    for place, group in enumerate(groups):
        for at in range(depth):
            piece = pieces_ref[0, at, place] if branch_first else pieces_ref[0, place, at]
            out_ref[0, at * rows : (at + 1) * rows, group * columns : (group + 1) * columns] = piece.astype(F32)


def write_layer(kernel, name, gathered, block, index, steps, shape, layer, layers, base):
    rows, width = shape
    ins = [pl.BlockSpec(block, index)]
    operands = [gathered]
    aliases = {}
    if base is not None:
        ins.append(pl.BlockSpec(memory_space=pl.ANY))
        operands.append(base)
        aliases = {1: 0}
    return pl.pallas_call(
        kernel,
        grid=(steps,),
        in_specs=ins,
        out_specs=pl.BlockSpec((1, rows // steps, width), lambda at: (layer, at, 0)),
        out_shape=jax.ShapeDtypeStruct((layers, rows, width), F32),
        input_output_aliases=aliases,
        compiler_params=pltpu.CompilerParams(vmem_limit_bytes=48 * 2**20),
        name=name,
    )(*operands)


def branch_places(order):
    stages = [stage for stage in order if stage[0] == "branch"]
    return [stages.index(("branch", bit)) for bit in range(len(stages))]


def write_columns(gathered, order, halving, layer, layers, base):
    pieces, rows, columns = gathered.shape
    places = branch_places(order)
    branch = 1 << len(places)
    seq = pieces // (2 * branch)

    def index(at):
        slot = 0
        for rank, (_, bit) in enumerate(halving[: len(places)]):
            slot = slot + (at // (1 << (len(places) - 1 - rank))) % 2 * (1 << places[bit])
        return 0, slot, 0, 0, 0

    gathered = gathered.reshape(2, branch, seq, rows, columns)
    shape = (branch * seq * rows, 2 * columns)
    return write_layer(columns_kernel, "gradient_columns", gathered, (2, 1, seq, rows, columns), index, branch, shape, layer, layers, base)


def write_groups(gathered, order, layer, layers, base):
    pieces, rows, columns = gathered.shape
    places = branch_places(order)
    branch = 1 << len(places)
    seq = pieces // (2 * branch)
    groups = [sum(((at >> place) & 1) << bit for bit, place in enumerate(places)) for at in range(branch)]
    branch_first = order[0][0] == "branch"
    split = (seq, branch) if branch_first else (branch, seq)
    gathered = gathered.reshape((2,) + split + (rows, columns))
    kernel = functools.partial(groups_kernel, groups, branch_first)
    shape = (2 * seq * rows, branch * columns)
    return write_layer(kernel, "gradient_groups", gathered, (1,) + split + (rows, columns), lambda at: (at, 0, 0, 0, 0), 2, shape, layer, layers, base)


def layer_forward(stream, layer, weights, gain, shift, side, tables, geometry):
    w_in, w_out, w_up, w_down = weights
    first = geometry["first"]
    xhat, _ = normalize(stream)
    normed = (xhat * gain[0] + shift[0]).astype(BF16)
    q, kv, own2, own3, own4, normed_all = prepare(normed, side, geometry["attention_in"], layer, tables["kf"], LOG2E * SIZE**-0.5, geometry["branch"])
    far = Task(gather_far(own2, own3, own4, geometry))
    lower = None
    for part in range(2):
        flights, q = start([far], q)
        lower = lower_forward(q, kv, tables["f0"], tables["f1"], part, 2, lower)
        land(flights, lower)
    while not far.done:
        flights, lower = start([far], lower)
        land(flights, lower)
    r2, r3, r4 = far.result
    att, qb = upper_forward(q, lower, r2, r3, r4, tables["f2"], tables["f3"], tables["f4"])
    saved_parts = (kv, r2, r3, r4, qb, att)
    att_rows = join_groups(swap(to_rows(first, att, tables["narrow"])))
    midway = stream + dot("ct,cd->td", att_rows, w_out)
    xhat, _ = normalize(midway)
    second = (xhat * gain[1] + shift[1]).astype(BF16)
    pre_act = dot("td,df->tf", second, w_up)
    hidden = (0.5 * pre_act * (1.0 + lax.erf(pre_act * np.float32(2**-0.5)))).astype(BF16)
    result = midway + dot("tf,fd->td", hidden, w_down)
    return result, (stream, normed_all, saved_parts, att_rows, midway, second, pre_act, hidden)


def layer_backward(gradient, saved, weights, gain, shift, tables, geometry, old, flights, last):
    w_in, w_out, w_up, w_down = weights
    stream, normed_all, parts, att_rows, midway, second, pre_act, hidden = saved
    kv, r2, r3, r4, qb, att = parts
    first = geometry["first"]
    halving = halving_order()
    seq_bits = [bit for _, bit in bits_of("seq", 1)]

    down_in = gradient.astype(BF16)
    new, ahead = [], []
    if not last:
        down = Task(reduce_product(hidden, down_in, halving))
        ahead, down_in = start([down], down_in)
    grad_hidden = dot("td,fd->tf", down_in, w_down)
    cdf = 0.5 * (1.0 + lax.erf(pre_act * np.float32(2**-0.5)))
    density = jnp.exp(-0.5 * pre_act * pre_act) * np.float32((2 * np.pi) ** -0.5)
    grad_pre = (grad_hidden * (cdf + pre_act * density)).astype(BF16)
    grad_second = dot("tf,mf->tm", grad_pre, w_up)
    back, gain_two, shift_two = normalize_back(midway, gain[1], grad_second)
    grad_midway = gradient + back
    out_in = grad_midway.astype(BF16)
    grad_rows = split_groups(dot("cd,td->ct", w_out, out_in).astype(BF16), geometry["branch"])
    land(flights + ahead, grad_rows)
    grad_rows, second, att_rows = lax.optimization_barrier((grad_rows, second, att_rows))
    if not last:
        ahead, grad_rows = start([down], grad_rows)
    waiting, grad_rows = start(old, grad_rows)
    rows = swap(grad_rows)
    if last:
        new = [
            product_halves(hidden, down_in, flipped_order()),
            product_halves(second, grad_pre, halving),
            product_halves(att_rows.T, out_in, halving),
        ]
        rows = pin(new, rows)
        ours = []
    else:
        up = Task(reduce_product(second, grad_pre, halving, 2))
        out = Task(reduce_product(att_rows.T, out_in, halving))
        rows = pin([up.pending[0], out.pending[0]], rows)
        new = [down, up, out]
        ours = new
    flights, rows = start(ours[1:], rows)
    g = prepare_back(first, rows, tables["narrow"], att)
    du, d2, d3, d4 = upper_back(qb, g, r2, r3, r4, tables["f2"], tables["f3"], tables["f4"])
    far = Task(return_far(d2, d3, d4, geometry))
    short, _ = start([far], d2)
    land(flights + ahead + waiting, du)
    land(short, d2)
    grads = None
    for part in range(2):
        moving = [task for task in ours + old if part or task is not ours[-1]] if ours else old
        flights, qb = start([far] + moving, qb)
        grads = lower_back(qb, g, kv, tables["f0"], tables["f1"], part, 2, grads)
        land(flights, grads)
    dq, dkv = grads
    flights, dq = start(ours + old, dq)
    back_rows = to_rows_back(first, dq, du, dkv, far.result, tables["full"], SIZE**-0.5)
    returned = swap(back_rows)
    normed_all, back_rows = lax.optimization_barrier((normed_all, back_rows))
    if last:
        enter = own_halves(normed_all, back_rows, bits_of("seq", 1))
        returned = pin(enter, returned)
    else:
        enter = Task(reduce_own(normed_all, back_rows, seq_bits))
        returned = pin(enter.pending[0], returned)
        extra, returned = start([enter], returned)
        flights = flights + extra
    projected = join_groups(returned)
    grad_first = dot("ct,dc->td", projected, w_in)
    back, gain_one, shift_one = normalize_back(stream, gain[0], grad_first)
    vectors = jnp.stack([gain_one, gain_two, shift_one, shift_two])
    return grad_midway + back, vectors, new + [enter], flights


def local(tile_embeddings, tile_valid, slide_bounds, norm_gain, norm_bias, attention_in, attention_out, hidden_up, hidden_down, cotangent):
    branch = lax.axis_size("branch")
    seq = lax.axis_size("seq")
    heads = H // branch
    rows, width = tile_embeddings.shape
    shard = rows * branch
    blocks = shard // BLOCK
    seq_at = lax.axis_index("seq")
    origin = seq_at * shard
    bit = 1 if blocks == 2 else 0

    def slide_at(place):
        return jnp.sum((place >= slide_bounds[1:-1]).astype(jnp.int32))

    def same(mask):
        return slide_at((seq_at ^ mask) * shard) == slide_at(origin)

    low, high = 1 << bit, 2 << bit
    geometry = dict(
        attention_in=attention_in,
        branch=branch,
        blocks=blocks,
        bit=bit,
        first=(lax.axis_index("branch") * heads).astype(jnp.int32).reshape(1),
        same=(None, same(low), same(high), same(high | low)),
    )
    full, narrow = placements(heads)
    tables = dict(
        full=jnp.asarray(full),
        narrow=jnp.asarray(narrow),
        kf=jnp.asarray(key_features()),
        f0=jnp.asarray(query_features(block_classes, 0)),
        f1=jnp.asarray(query_features(block_classes[:512], 1)),
        f2=jnp.asarray(query_features(upper_classes, 2)),
        f3=jnp.asarray(query_features(upper_classes[:256], 3)),
        f4=jnp.asarray(query_features(upper_classes[:128], 4)),
    )
    valid = lax.dynamic_slice_in_dim(tile_valid, origin, shard)
    valid = valid.reshape(branch, rows // 16, 16).swapaxes(1, 2).reshape(shard, 1)
    side = jnp.where((lanes_of((1, 128)) == BIAS) & (valid != 1), NEG, 0.0).astype(BF16)

    layers = attention_in.shape[0]
    weights = [(attention_in[at], attention_out[at], hidden_up[at], hidden_down[at]) for at in range(layers)]
    stream = to_major(tile_embeddings).astype(F32)
    outputs, saved_all = [], []
    for layer in range(layers):
        stream, saved = layer_forward(stream, layer, weights[layer], norm_gain[layer], norm_bias[layer], side, tables, geometry)
        outputs.append(from_major(stream.astype(BF16)))
        saved_all.append(saved)
    gradient = to_major(cotangent).astype(F32)
    vectors = [None] * layers
    tasks, flights = [], []
    first_round, flipped = doubling_order(False), doubling_order(True)
    rounds = [[flipped, first_round, first_round, first_round] for _ in range(layers)]
    rounds[0][3] = doubling_order(True, branch_first=True)
    for layer in reversed(range(layers)):
        gradient, vectors[layer], new, flights = layer_backward(
            gradient, saved_all[layer], weights[layer], norm_gain[layer], norm_bias[layer], tables, geometry, tasks, flights, layer == 0
        )
        if layer:
            tasks = tasks + new
    land(flights, gradient)
    for task in tasks:
        while not task.done:
            task.advance(jax.tree.map(lambda v: exchange(v, *task.pending[1:]), task.pending[0]))
    core = [("seq", 0)]
    halving = halving_order()
    halvings = [core + flipped_order(), core + halving, core + halving, core + bits_of("seq", 1)]
    pieces = [task.result[None] for task in tasks] + [jnp.stack(vectors).reshape(1, -1, width)]
    order = rounds[0] + [order for layer in reversed(range(1, layers)) for order in rounds[layer]] + [first_round]
    gathered = finish_everywhere([sent for sent, _ in new], [mine for _, mine in new], halvings, pieces, order)
    places = [(0, member) for member in range(4)] + [(layer, member) for layer in reversed(range(1, layers)) for member in range(4)]
    vectors = jnp.sum(gathered[-1], axis=0).reshape(layers, 2, 2, width)
    sums = [None] * 4
    for (layer, member), whole in zip(places, gathered[:-1]):
        if member == 3:
            sums[member] = write_groups(whole, rounds[layer][member], layer, layers, sums[member])
        else:
            follows = halvings[member][1:] if layer == 0 else halving
            sums[member] = write_columns(whole, rounds[layer][member], follows, layer, layers, sums[member])
    down, up, out, enter = sums
    return (jnp.stack(outputs), from_major(gradient), vectors[:, 0], vectors[:, 1], enter, out, up, down)


def solution(mesh):
    split = P(("seq", "branch"), None)
    in_specs = (split,) + (P(),) * 8 + (split,)
    out_specs = (P(None, ("seq", "branch"), None), split) + (P(),) * 6
    return jax.shard_map(local, mesh=mesh, in_specs=in_specs, out_specs=out_specs, check_vma=False)
```

```python
import functools
import numpy as np
import jax
import jax.numpy as jnp
from jax import lax
from jax.experimental import pallas as pl
from jax.experimental.pallas import tpu as pltpu
from jax.sharding import PartitionSpec as P

BLOCK = 1024
CHUNK = 32
ORDER = (0, 8, 4, 12, 2, 10, 6, 14, 1, 9, 5, 13, 3, 11, 7, 15)
ONE, BIAS, HIGH, LOW, VALUE = 48, 51, 52, 57, 64
NEG = -1e30
LOG2E = 1.4426950408889634
LN2 = 0.6931471805599453
F32, BF16 = jnp.float32, jnp.bfloat16


def low_np(x):
    return np.asarray(x, np.float32).astype(jnp.bfloat16).astype(np.float32)


def query_features(classes, level):
    table = np.zeros((len(classes), 128), np.float32)
    table[:, BIAS] = 1.0
    for at, mine in enumerate(classes):
        for theirs in range(5):
            met = min(mine, theirs) - level + 1
            value = np.log2(met) if met > 0 else NEG
            high = low_np(value)
            table[at, HIGH + theirs] = high
            table[at, LOW + theirs] = low_np(value - high) if met > 0 else 0.0
    return table.astype(jnp.bfloat16)


block_classes = [4] * 64 + [3] * 64 + [2] * 128 + [1] * 256 + [0] * 512
upper_classes = [4] * 128 + [3] * 128 + [2] * 256


def key_features():
    table = np.zeros((BLOCK, 128), np.float32)
    table[:, ONE : ONE + 3] = 1.0
    for at, mine in enumerate(block_classes):
        table[at, HIGH + mine] = 1.0
        table[at, LOW + mine] = 1.0
    return table.astype(jnp.bfloat16)


def nt(a, b):
    return lax.dot_general(a, b, (((1,), (1,)), ((), ())), preferred_element_type=F32)


def tn(a, b):
    return lax.dot_general(a, b, (((0,), (0,)), ((), ())), preferred_element_type=F32)


def nn(a, b):
    return lax.dot_general(a, b, (((1,), (0,)), ((), ())), preferred_element_type=F32)


def lanes_of(shape):
    return lax.broadcasted_iota(jnp.int32, shape, len(shape) - 1)


def split3(column):
    high = column.astype(BF16)
    rest = column - high.astype(F32)
    mid = rest.astype(BF16)
    last = (rest - mid.astype(F32)).astype(BF16)
    return high, mid, last


def place3(base, column):
    high, mid, last = split3(column)
    lane = lanes_of(base.shape)
    out = jnp.where(lane == ONE, high.astype(F32), base)
    out = jnp.where(lane == ONE + 1, mid.astype(F32), out)
    return jnp.where(lane == ONE + 2, last.astype(F32), out)


def chunk_row(head, block, position, part, per_dev):
    residue = lax.rem(ORDER[position] + head, 16)
    return pl.multiple_of((2 * block + part) * per_dev + residue * CHUNK, CHUNK)


def prepare_kernel(heads, blocks, scale, bits, layer, x_ref, side_ref, weights_ref, kf_ref, q_ref, kv_ref, *refs):
    near_refs, (all_ref, rows_all, work, placed, weight_ref, send_sem, recv_sem, in_sem, out_sem) = refs[:3], refs[3:]
    weight = pltpu.make_async_copy(weights_ref.at[layer], weight_ref, in_sem)
    weight.start()
    me = lax.axis_index("branch")
    count, rows = rows_all.shape[:2]

    def away(mask):
        place = me
        for bit in range(bits):
            if mask >> bit & 1:
                place = place + (1 << bit) * (1 - 2 * lax.rem(me // (1 << bit), 2))
        return place

    def place_weight(head):
        shape = (weight_ref.shape[1], 256)
        lane = lax.broadcasted_iota(jnp.int32, shape, 1)
        column = lax.broadcasted_iota(jnp.int32, shape, 0) - (me * heads + head) * 144
        query = (lane < 48) & (column == lane)
        key = (lane >= 128) & (lane < 176) & (column == lane - 80)
        value = (lane >= 128 + VALUE) & (lane < 128 + VALUE + 48) & (column == lane - (32 + VALUE))
        chosen = (query | key | value).astype(F32).astype(BF16)
        placed[head] = nn(weight_ref[...], chosen).astype(BF16)

    barrier = pltpu.get_barrier_semaphore()
    for bit in range(bits):
        pl.semaphore_signal(barrier, inc=1, device_id={"branch": away(1 << bit)}, device_id_type=pl.DeviceIdType.MESH)
    rows_all[pl.ds(me, 1)] = x_ref[...][None]
    pl.semaphore_wait(barrier, bits)
    orders = (list(range(bits)), list(range(bits))[::-1])
    size = rows // 2
    copies = {}

    def begin(flow, stage):
        order = orders[flow]
        masks = [0]
        for bit in order[:stage]:
            masks = masks + [mask | 1 << bit for mask in masks]
        for number, mask in enumerate(masks):
            place = (1 << stage) - 1 + number
            here = rows_all.at[away(mask), pl.ds(flow * size, size)]
            copy = pltpu.make_async_remote_copy(
                src_ref=here,
                dst_ref=here,
                send_sem=send_sem.at[flow, place],
                recv_sem=recv_sem.at[flow, place],
                device_id={"branch": away(1 << order[stage])},
                device_id_type=pl.DeviceIdType.MESH,
            )
            copy.start()
            copies.setdefault((flow, stage), []).append(copy)

    def project(mask):
        place = away(mask)
        at = pl.multiple_of(place * rows, rows)
        source = rows_all[place]
        for head in range(heads):
            value = nn(source, placed[head])
            work[head, pl.ds(at, rows), :128] = (value[:, :128] * scale).astype(BF16)
            work[head, pl.ds(at, rows), 128:] = value[:, 128:].astype(BF16)

    for stage in range(bits):
        for flow in range(2):
            if stage > 0:
                for copy in copies[flow, stage - 1]:
                    copy.wait_recv()
            begin(flow, stage)
        if stage == 0:
            weight.wait()
            for head in range(heads):
                place_weight(head)
            project(0)
    for flow in range(2):
        for copy in copies[flow, bits - 1]:
            copy.wait_recv()
    kept = pltpu.make_async_copy(rows_all, all_ref, out_sem)
    kept.start()
    for mask in range(1, count):
        project(mask)
    kf = kf_ref[...]
    for head in range(heads):
        which = me * heads + head
        for position in range(16):
            features = kf[position * 64 : position * 64 + CHUNK]
            for block in range(blocks):
                for part in range(2):
                    row = chunk_row(which, block, position, part, rows)
                    at = position * 64 + part * CHUNK
                    source = work[head, pl.ds(row, CHUNK), :]
                    q_ref[head, block, at : at + CHUNK, :] = source[:, :128]
                    key_value = source[:, 128:] + features + side_ref[pl.ds(row, CHUNK), :]
                    kv_ref[head, block, at : at + CHUNK, :] = key_value
                    for near_ref in near_refs:
                        if at < near_ref.shape[2]:
                            near_ref[head, block, at : at + CHUNK, :] = key_value
    kept.wait()
    for group in copies.values():
        for copy in group:
            copy.wait_send()


def prepare(rows, side, weights, layer, kf, scale, count):
    heads = weights.shape[2] // (144 * count)
    total = rows.shape[0] * count
    blocks = total // BLOCK
    bits = count.bit_length() - 1
    shape = jax.ShapeDtypeStruct((heads, blocks, BLOCK, 128), BF16)
    whole = (count,) + rows.shape
    near = tuple(jax.ShapeDtypeStruct((heads, blocks, size, 128), BF16) for size in (256, 128, 64))
    return pl.pallas_call(
        functools.partial(prepare_kernel, heads, blocks, scale, bits, layer),
        out_shape=(shape, shape) + near + (jax.ShapeDtypeStruct(whole, BF16),),
        in_specs=[pl.BlockSpec(memory_space=pltpu.VMEM if at != 2 else pl.ANY) for at in range(4)],
        out_specs=(pl.BlockSpec(memory_space=pltpu.VMEM),) * 5 + (pl.BlockSpec(memory_space=pl.ANY),),
        scratch_shapes=[
            pltpu.VMEM(whole, BF16),
            pltpu.VMEM((heads, total, 256), BF16),
            pltpu.VMEM((heads, weights.shape[1], 256), BF16),
            pltpu.VMEM(weights.shape[1:], BF16),
            pltpu.SemaphoreType.DMA((2, count - 1)),
            pltpu.SemaphoreType.DMA((2, count - 1)),
            pltpu.SemaphoreType.DMA,
            pltpu.SemaphoreType.DMA,
        ],
        compiler_params=pltpu.CompilerParams(collective_id=1 + layer, has_side_effects=True, vmem_limit_bytes=48 * 2**20),
        name="attention_prepare",
    )(rows, side, weights, kf)


def lower_kernel(q_ref, kv_ref, f0_ref, f1_ref, *refs):
    o_ref = refs[-1]
    step = 256
    for block in range(2):
        own = kv_ref[0, block]
        near = kv_ref[0, 1 - block, :512]
        for at in range(0, BLOCK, step):
            rows = slice(at, at + step)
            base = q_ref[0, block, rows]
            s0 = nt(base + f0_ref[rows], own)
            top = jnp.max(s0, axis=1, keepdims=True)
            if at < 512:
                s1 = nt(base + f1_ref[rows], near)
                top = jnp.maximum(top, jnp.max(s1, axis=1, keepdims=True))
            own_rows = own[rows].astype(F32)
            meet = base.astype(F32) * own_rows
            alone = jnp.sum(meet, axis=1, keepdims=True)
            lane = lanes_of(own_rows.shape)
            bias = jnp.min(jnp.where(lane == BIAS, own_rows, 0.0), axis=1, keepdims=True)
            classes = sum((lax.broadcasted_iota(jnp.int32, (step, 1), 0) + at < edge).astype(F32) for edge in (512, 256, 128, 64))
            alone = jnp.where(bias < 0.0, alone + jnp.log2(classes + 1.0), NEG)
            top = jnp.maximum(top, alone)
            out = nn(jnp.exp2(s0 - top).astype(BF16), own)
            if at < 512:
                out = out + nn(jnp.exp2(s1 - top).astype(BF16), near)
            out = out + jnp.exp2(alone - top) * own_rows
            o_ref[0, block, rows] = jnp.where(lane == 0, top, out)


def part_call(kernel, name, operands, tables, outs, part, parts, base, cost):
    heads, blocks = operands[0].shape[:2]
    count = heads // parts
    spec = pl.BlockSpec((1, 2, BLOCK, 128), lambda h, p: (h + part * count, p, 0, 0))
    whole = lambda a: pl.BlockSpec(a.shape, lambda h, p: (0,) * a.ndim)
    ins = [spec] * len(operands) + [whole(table) for table in tables]
    arrays = list(operands) + list(tables)
    aliases = {}
    if base is not None:
        for at, array in enumerate(base):
            aliases[len(arrays)] = at
            arrays.append(array)
            ins.append(pl.BlockSpec(memory_space=pl.ANY))
    pairs = int(count * blocks * 1.25 * 2**20)
    return pl.pallas_call(
        kernel,
        grid=(count, blocks // 2),
        in_specs=ins,
        out_specs=(spec,) * outs,
        out_shape=(jax.ShapeDtypeStruct(operands[0].shape, F32),) * outs,
        input_output_aliases=aliases,
        compiler_params=pltpu.CompilerParams(vmem_limit_bytes=56 * 2**20),
        cost_estimate=pl.CostEstimate(flops=pairs * 256 * cost, bytes_accessed=operands[0].size * 8 // parts, transcendentals=pairs),
        name=name,
    )(*arrays)


def lower_forward(q, kv, f0, f1, part, parts, base):
    out = part_call(lower_kernel, "attention_lower", (q, kv), (f0, f1), 1, part, parts, None if base is None else (base,), 4)
    return out[0]


UPPER = ((0, 0, 64), (1, 0, 64), (0, 64, 128), (1, 64, 128), (0, 128, 256), (1, 128, 256))


def gather_upper(ref, lead):
    return jnp.concatenate([ref[(*lead, block, slice(low, high))] for block, low, high in UPPER], axis=0)


def upper_kernel(q_ref, o_ref, r2_ref, r3_ref, r4_ref, f2_ref, f3_ref, f4_ref, att_ref, qb_ref):
    merged = {}
    uq = gather_upper(q_ref, (0,))
    ol = gather_upper(o_ref, (0,))
    for low, high in ((0, 128), (128, 256), (256, 512)):
        base = uq[low:high]
        pairs = [(nt(base + f2_ref[low:high], r2_ref[0, 0]), r2_ref[0, 0])]
        if high <= 256:
            pairs.append((nt(base + f3_ref[low:high], r3_ref[0]), r3_ref[0]))
        if high <= 128:
            pairs.append((nt(base + f4_ref[low:high], r4_ref[0]), r4_ref[0]))
        old = ol[low:high]
        lane = lanes_of(old.shape)
        before = old[:, 0:1]
        top = before
        for scores, keys in pairs:
            top = jnp.maximum(top, jnp.max(scores, axis=1, keepdims=True))
        out = old * jnp.exp2(before - top)
        for scores, keys in pairs:
            out = out + nn(jnp.exp2(scores - top).astype(BF16), keys)
        merged[low] = jnp.where(lane == 0, top, out)
    whole = jnp.concatenate([merged[0], merged[128], merged[256]], axis=0)
    place = 0

    def finish(block, low, high, rows):
        lane = lanes_of(rows.shape)
        top = rows[:, 0:1]
        total = rows[:, ONE : ONE + 1]
        att_ref[0, block, low:high] = jnp.where((lane >= VALUE) & (lane < VALUE + 48), rows / total, 0.0)
        lse = top + jnp.log2(total)
        qb_ref[0, block, low:high] = place3(q_ref[0, block, low:high].astype(F32), -lse).astype(BF16)

    for block, low, high in UPPER:
        finish(block, low, high, whole[place : place + high - low])
        place += high - low
    for block in range(2):
        for low in (256, 512, 768):
            finish(block, low, low + 256, o_ref[0, block, low : low + 256])


def upper_forward(q, o, r2, r3, r4, f2, f3, f4):
    heads, blocks = q.shape[:2]
    spec = pl.BlockSpec((1, 2, BLOCK, 128), lambda h, p: (h, p, 0, 0))
    two = pl.BlockSpec((1, 1, 512, 128), lambda h, p: (h, p, 0, 0))
    far = pl.BlockSpec((1, 512, 128), lambda h, p: (h, 0, 0))
    whole = lambda a: pl.BlockSpec(a.shape, lambda h, p: (0,) * a.ndim)
    return pl.pallas_call(
        upper_kernel,
        grid=(heads, blocks // 2),
        in_specs=[spec, spec, two, far, far, whole(f2), whole(f3), whole(f4)],
        out_specs=(spec, spec),
        out_shape=(jax.ShapeDtypeStruct(q.shape, F32), jax.ShapeDtypeStruct(q.shape, BF16)),
        compiler_params=pltpu.CompilerParams(vmem_limit_bytes=48 * 2**20),
        name="attention_upper",
    )(q, o, r2, r3, r4, f2, f3, f4)


def chunk_place(head, residue, part):
    turn = lax.rem(residue - head + 32, 16)
    position = 8 * lax.rem(turn, 2) + 4 * lax.rem(turn // 2, 2) + 2 * lax.rem(turn // 4, 2) + turn // 8
    return pl.multiple_of(position * 64 + part * CHUNK, CHUNK)


def exchange_rows(bits, make, out_ref, sent, land, send_sem, recv_sem, out_sem):
    me = lax.axis_index("branch")
    count = 1 << bits

    def away(mask):
        place = me
        for bit in range(bits):
            if mask >> bit & 1:
                place = place + (1 << bit) * (1 - 2 * lax.rem(me // (1 << bit), 2))
        return place

    barrier = pltpu.get_barrier_semaphore()
    for mask in range(1, count):
        pl.semaphore_signal(barrier, inc=1, device_id={"branch": away(mask)}, device_id_type=pl.DeviceIdType.MESH)
    copies = []
    for mask in range(count - 1, 0, -1):
        sent[mask - 1] = make(away(mask))
        if not copies:
            pl.semaphore_wait(barrier, count - 1)
        copy = pltpu.make_async_remote_copy(
            src_ref=sent.at[mask - 1],
            dst_ref=land.at[me],
            send_sem=send_sem.at[mask - 1],
            recv_sem=recv_sem.at[mask - 1],
            device_id={"branch": away(mask)},
            device_id_type=pl.DeviceIdType.MESH,
        )
        copy.start()
        copies.append(copy)
    land[pl.ds(me, 1)] = make(me)[None]
    for copy in copies:
        copy.wait_recv()
    kept = pltpu.make_async_copy(land, out_ref, out_sem)
    kept.start()
    kept.wait()
    for copy in copies:
        copy.wait_send()


def exchange_scratch(count, shape):
    return [
        pltpu.VMEM((count - 1,) + shape, BF16),
        pltpu.VMEM((count,) + shape, BF16),
        pltpu.SemaphoreType.DMA((count - 1,)),
        pltpu.SemaphoreType.DMA((count - 1,)),
        pltpu.SemaphoreType.DMA,
    ]


def rows_kernel(heads, bits, a_ref, place_ref, out_ref, work, *exchange):
    me = lax.axis_index("branch")

    def make(position):
        block, part = position // 2, lax.rem(position, 2)
        value = None
        for head in range(heads):
            for residue in range(16):
                at = chunk_place(me * heads + head, residue, part)
                work[head, residue * CHUNK : (residue + 1) * CHUNK, :] = a_ref[head, block, pl.ds(at, CHUNK), :].astype(BF16)
            placed = nt(place_ref[head], work[head])
            value = placed if value is None else value + placed
        return value.astype(BF16)

    exchange_rows(bits, make, out_ref, *exchange)


def to_rows(att, place):
    heads, blocks = att.shape[:2]
    shape = (place.shape[1], BLOCK // 2)
    count = 2 * blocks
    return pl.pallas_call(
        functools.partial(rows_kernel, heads, count.bit_length() - 1),
        out_shape=jax.ShapeDtypeStruct((count,) + shape, BF16),
        in_specs=[pl.BlockSpec(memory_space=pltpu.VMEM)] * 2,
        out_specs=pl.BlockSpec(memory_space=pl.ANY),
        scratch_shapes=[pltpu.VMEM((heads, BLOCK // 2, 128), BF16)] + exchange_scratch(count, shape),
        compiler_params=pltpu.CompilerParams(collective_id=8, has_side_effects=True, vmem_limit_bytes=48 * 2**20),
        name="attention_rows",
    )(att, place)


def prepare_back_kernel(heads, blocks, first_ref, x_ref, place_ref, att_ref, g_ref, work):
    for head in range(heads):
        for part in range(x_ref.shape[0]):
            work[part * 512 : part * 512 + 512] = tn(x_ref[part], place_ref[head]).astype(BF16)
        which = first_ref[0] + head
        for position in range(16):
            for block in range(blocks):
                for part in range(2):
                    row = chunk_row(which, block, position, part, 512)
                    at = position * 64 + part * CHUNK
                    g_ref[head, block, at : at + CHUNK, :] = work[pl.ds(row, CHUNK), :]
        for block in range(blocks):
            for at in range(0, BLOCK, 256):
                rows = slice(at, at + 256)
                grad = g_ref[head, block, rows].astype(F32)
                dots = jnp.sum(grad * att_ref[head, block, rows], axis=1, keepdims=True)
                g_ref[head, block, rows] = place3(grad, -dots).astype(BF16)


def prepare_back(first, rows, place, att):
    heads, blocks = att.shape[:2]
    total = blocks * BLOCK
    return pl.pallas_call(
        functools.partial(prepare_back_kernel, heads, blocks),
        out_shape=jax.ShapeDtypeStruct(att.shape, BF16),
        in_specs=[pl.BlockSpec(memory_space=pltpu.SMEM)]
        + [pl.BlockSpec(memory_space=pltpu.VMEM)] * 3,
        out_specs=pl.BlockSpec(memory_space=pltpu.VMEM),
        scratch_shapes=[pltpu.VMEM((total, 128), BF16)],
        compiler_params=pltpu.CompilerParams(vmem_limit_bytes=48 * 2**20),
        name="attention_prepare_back",
    )(first, rows, place, att)


def back_tile(kv, key_t, q_scores, g, q):
    probs = jnp.exp2(nt(kv, q_scores))
    grad_scores = (probs * nt(kv, g)).astype(BF16)
    grad_kv = nn(probs.astype(BF16), g) + nn(grad_scores, q)
    return grad_kv, nn(key_t, grad_scores)


def upper_back_kernel(qb_ref, g_ref, r2_ref, r3_ref, r4_ref, f2_ref, f3_ref, f4_ref, dq_ref, d2_ref, d3_ref, d4_ref):
    uq = gather_upper(qb_ref, (0,))
    ug = gather_upper(g_ref, (0,))
    dq = None
    lane = lanes_of((256, 128))
    for ref, out, f_ref, count in ((r2_ref.at[0], d2_ref.at[0], f2_ref, 512), (r3_ref, d3_ref.at[0], f3_ref, 256), (r4_ref, d4_ref.at[0], f4_ref, 128)):
        q = uq[:count]
        g = ug[:count]
        qs = q + f_ref[...]
        total = None
        for at in range(0, 512, 256):
            kv = ref[0, at : at + 256]
            key_t = kv.astype(F32).T[:48].astype(BF16)
            grad_kv, part = back_tile(kv, key_t, qs, g, q)
            out[0, at : at + 256] = jnp.where(lane < 48, grad_kv * LN2, grad_kv).astype(BF16)
            total = part if total is None else total + part
        rows = total.T
        if count < 512:
            rows = jnp.concatenate([rows, jnp.zeros((512 - count, 48), F32)], axis=0)
        dq = rows if dq is None else dq + rows
    dq_ref[0, 0] = jnp.concatenate([dq, jnp.zeros((512, 80), F32)], axis=1)


def upper_back(qb, g, r2, r3, r4, f2, f3, f4):
    heads, blocks = qb.shape[:2]
    pairs = blocks // 2
    spec = pl.BlockSpec((1, 2, BLOCK, 128), lambda h, p: (h, p, 0, 0))
    two = pl.BlockSpec((1, 1, 512, 128), lambda h, p: (h, p, 0, 0))
    far = pl.BlockSpec((1, 512, 128), lambda h, p: (h, 0, 0))
    whole = lambda a: pl.BlockSpec(a.shape, lambda h, p: (0,) * a.ndim)
    shape = (heads, pairs, 512, 128)
    return pl.pallas_call(
        upper_back_kernel,
        grid=(heads, pairs),
        in_specs=[spec, spec, two, far, far, whole(f2), whole(f3), whole(f4)],
        out_specs=(two,) * 4,
        out_shape=(jax.ShapeDtypeStruct(shape, F32),) + (jax.ShapeDtypeStruct(shape, BF16),) * 3,
        compiler_params=pltpu.CompilerParams(vmem_limit_bytes=48 * 2**20),
        name="attention_upper_back",
    )(qb, g, r2, r3, r4, f2, f3, f4)


def lower_back_kernel(qb_ref, g_ref, kv_ref, f0_ref, f1_ref, *refs):
    dq_ref, dkv_ref = refs[-2:]
    step = 256
    lane = lanes_of((step, 128))
    totals = [None, None]
    for block in range(2):
        q = qb_ref[0, block]
        g = g_ref[0, block]
        q0 = q + f0_ref[...]
        far_q = qb_ref[0, 1 - block, :512]
        far_g = g_ref[0, 1 - block, :512]
        far_q1 = far_q + f1_ref[...]
        for at in range(0, BLOCK, step):
            rows = slice(at, at + step)
            kv = kv_ref[0, block, rows]
            key_t = kv.astype(F32).T[:48].astype(BF16)
            grad_kv, part = back_tile(kv, key_t, q0, g, q)
            totals[block] = part if totals[block] is None else totals[block] + part
            if at < 512:
                more_kv, part = back_tile(kv, key_t, far_q1, far_g, far_q)
                grad_kv = grad_kv + more_kv
                part = jnp.concatenate([part, jnp.zeros((48, 512), F32)], axis=1)
                totals[1 - block] = part if totals[1 - block] is None else totals[1 - block] + part
            kv_rows = kv.astype(F32)
            q_rows = q[rows].astype(F32)
            g_rows = g[rows].astype(F32)
            bias = jnp.min(jnp.where(lane == BIAS, kv_rows, 0.0), axis=1, keepdims=True)
            classes = sum((lax.broadcasted_iota(jnp.int32, (step, 1), 0) + at < edge).astype(F32) for edge in (512, 256, 128, 64))
            met = jnp.where(lane < ONE + 3, q_rows * kv_rows, 0.0)
            score = jnp.sum(met, axis=1, keepdims=True) + jnp.log2(classes + 1.0)
            prob = jnp.where(bias < 0.0, jnp.exp2(jnp.where(bias < 0.0, score, NEG)), 0.0)
            grad_score = prob * jnp.sum(jnp.where((lane >= ONE) & (lane != BIAS), g_rows * kv_rows, 0.0), axis=1, keepdims=True)
            grad_kv = grad_kv + prob * g_rows + grad_score * q_rows
            dkv_ref[0, block, rows] = jnp.where(lane < 48, grad_kv * LN2, grad_kv)
            dq_ref[0, block, rows] = grad_score * kv_rows
    for block in range(2):
        for at in range(0, BLOCK, step):
            rows = slice(at, at + step)
            value = totals[block][:, rows].T
            value = jnp.concatenate([value, jnp.zeros((step, 80), F32)], axis=1)
            dq_ref[0, block, rows] = dq_ref[0, block, rows] + value


def lower_back(qb, g, kv, f0, f1, part, parts, base):
    return part_call(lower_back_kernel, "attention_lower_back", (qb, g, kv), (f0, f1), 2, part, parts, base, 10)


def rows_back_kernel(heads, blocks, scale, first_ref, dq_ref, du_ref, dkv_ref, x2_ref, place_ref, out_ref, work, sum_q, sum_kv):
    for head in range(heads):
        for block in range(blocks):
            start = 0
            for ub, low, high in UPPER:
                if ub == block % 2:
                    sum_q[head, block, low:high] = dq_ref[head, block, low:high] + du_ref[head, block // 2, start : start + high - low]
                start += high - low
            sum_q[head, block, 256:] = dq_ref[head, block, 256:]
            sum_kv[head, block, :256] = dkv_ref[head, block, :256] + x2_ref[head, block].astype(F32)
            sum_kv[head, block, 256:] = dkv_ref[head, block, 256:]
        which = first_ref[0] + head
        for residue in range(16):
            for block in range(blocks):
                for part in range(2):
                    row = (2 * block + part) * 512 + residue * CHUNK
                    at = chunk_place(which, residue, part)
                    grad_q = sum_q[head, block, pl.ds(at, CHUNK), :]
                    grad_kv = sum_kv[head, block, pl.ds(at, CHUNK), :]
                    lane = lanes_of(grad_q.shape)
                    work[head, row : row + CHUNK, :128] = jnp.where(lane < 48, grad_q * scale, 0.0).astype(BF16)
                    keep = (lane < 48) | ((lane >= VALUE) & (lane < VALUE + 48))
                    work[head, row : row + CHUNK, 128:] = jnp.where(keep, grad_kv, 0.0).astype(BF16)
        for part in range(out_ref.shape[0]):
            value = nt(place_ref[head], work[head, part * 512 : part * 512 + 512]).astype(BF16)
            out_ref[part] = value if head == 0 else out_ref[part] + value


def to_rows_back(first, dq, du, dkv, x2, place, scale):
    heads, blocks = dq.shape[:2]
    total = blocks * BLOCK
    return pl.pallas_call(
        functools.partial(rows_back_kernel, heads, blocks, scale),
        out_shape=jax.ShapeDtypeStruct((total // 512, place.shape[1], 512), BF16),
        in_specs=[pl.BlockSpec(memory_space=pltpu.SMEM)]
        + [pl.BlockSpec(memory_space=pltpu.VMEM)] * 5,
        out_specs=pl.BlockSpec(memory_space=pltpu.VMEM),
        scratch_shapes=[pltpu.VMEM((heads, total, 256), BF16)] + [pltpu.VMEM(dq.shape, F32)] * 2,
        compiler_params=pltpu.CompilerParams(vmem_limit_bytes=56 * 2**20),
        name="attention_rows_back",
    )(first, dq, du, dkv, x2, place)


def placements(heads):
    full = np.zeros((heads, heads * 144, 256), np.float32)
    narrow = np.zeros((heads, heads * 48, 128), np.float32)
    for head in range(heads):
        for at in range(48):
            full[head, head * 144 + at, at] = 1.0
            full[head, head * 144 + 48 + at, 128 + at] = 1.0
            full[head, head * 144 + 96 + at, 128 + VALUE + at] = 1.0
            narrow[head, head * 48 + at, VALUE + at] = 1.0
    return full.astype(jnp.bfloat16), narrow.astype(jnp.bfloat16)


H = 16
SIZE = 48
eps_norm = 1e-05


def exchange(value, axis, bit):
    count = lax.axis_size(axis)
    return lax.ppermute(value, axis, [(at, at ^ (1 << bit)) for at in range(count)])


def to_major(x):
    rows, width = x.shape
    return x.reshape(rows // 16, 16, width).swapaxes(0, 1).reshape(rows, width)


def from_major(x):
    rows, width = x.shape
    return x.reshape(16, rows // 16, width).swapaxes(0, 1).reshape(rows, width)


def normalize(stream):
    centered = stream - jnp.mean(stream, axis=-1, keepdims=True)
    spread = jnp.mean(centered * centered, axis=-1, keepdims=True)
    scale = lax.rsqrt(spread + eps_norm)
    return centered * scale, scale


def normalize_back(stream, gain, e):
    xhat, scale = normalize(stream)
    dxh = e * gain
    back = scale * (dxh - jnp.mean(dxh, axis=-1, keepdims=True) - xhat * jnp.mean(dxh * xhat, axis=-1, keepdims=True))
    return back, jnp.sum(e * xhat, axis=0), jnp.sum(e, axis=0)


class Task:
    def __init__(self, steps):
        self.steps = steps
        self.pending, self.result, self.done = None, None, False
        self.advance(None)

    def advance(self, value):
        try:
            self.pending = self.steps.send(value)
        except StopIteration as stop:
            self.result, self.pending, self.done = stop.value, None, True


def start(tasks, ins):
    tasks = [task for task in tasks if not task.done]
    operands = [task.pending[0] for task in tasks]
    operands, ins = lax.optimization_barrier((operands, ins))
    flights = [(task, jax.tree.map(lambda v: exchange(v, *task.pending[1:]), operand)) for task, operand in zip(tasks, operands)]
    return flights, ins


def land(flights, outs):
    if flights:
        values, _ = lax.optimization_barrier(([value for _, value in flights], outs))
        for (task, _), value in zip(flights, values):
            task.advance(value)


def gather_far(own2, own3, own4, geometry):
    blocks, same = geometry["blocks"], geometry["same"]
    heads = own2.shape[0]
    if blocks == 2:
        a3 = yield own3, "seq", 1
        a4 = yield jnp.concatenate([own4, a3[:, :, :64]], axis=1), "seq", 2
        r2, b3, b4 = yield (own2, a3, a4), "seq", 0
        r3 = jnp.concatenate([a3, b3], axis=1)
        r4 = jnp.concatenate([a4[:, :2], b4[:, :2], a4[:, 2:], b4[:, 2:]], axis=1)
    else:
        r2 = jnp.concatenate([own2[:, 2:], own2[:, :2]], axis=1)
        r3 = yield own3, "seq", 0
        r4 = yield jnp.concatenate([own4, r3[:, :, :64]], axis=1), "seq", 1
    bias_lane = lanes_of((1, 1, 1, 128)) == BIAS
    r3 = jnp.where(bias_lane & ~same[1], jnp.asarray(NEG, BF16), r3)
    alike = jnp.repeat(jnp.stack([same[2], same[3]]), 4)[None, :, None, None]
    r4 = jnp.where(bias_lane & ~alike, jnp.asarray(NEG, BF16), r4)
    return (
        r2.reshape(heads, blocks // 2, 512, 128),
        r3.reshape(heads, 512, 128),
        r4.reshape(heads, 512, 128),
    )


def return_far(d2, d3, d4, geometry):
    blocks = geometry["blocks"]
    heads = d2.shape[0]

    def fold(d):
        return d[:, 0] if d.shape[1] == 1 else jnp.sum(d.astype(F32), axis=1).astype(BF16)

    def add(a, b):
        return (a.astype(F32) + b.astype(F32)).astype(BF16)

    def grow(d):
        return jnp.concatenate([d, jnp.zeros_like(d)], axis=2)

    d4 = fold(d4).reshape(heads, 8, 64, 128)
    d3 = fold(d3).reshape(heads, 4, 128, 128)
    d2 = d2.reshape(heads, blocks, 256, 128)
    if blocks == 2:
        b4 = jnp.concatenate([d4[:, 2:4], d4[:, 6:8]], axis=1)
        a4 = jnp.concatenate([d4[:, 0:2], d4[:, 4:6]], axis=1)
        x2, y3, y4 = yield (d2, d3[:, 2:], b4), "seq", 0
        x4 = yield add(a4, y4), "seq", 2
        x3 = yield add(add(d3[:, :2], y3), grow(x4[:, 2:])), "seq", 1
        return add(x2, grow(add(x3, grow(x4[:, :2]))))
    x4 = yield d4, "seq", 1
    x3 = yield add(d3, grow(x4[:, 4:])), "seq", 0
    x3 = add(x3, grow(x4[:, :4]))
    x2 = jnp.concatenate([d2[:, 2:], d2[:, :2]], axis=1)
    return add(x2, grow(x3))


def split_groups(value, count):
    return value.reshape(count, -1, value.shape[1])


def join_groups(value):
    return value.reshape(-1, value.shape[2])


def pin(first, then):
    return lax.optimization_barrier((first, then))[1]


def swap(value):
    return lax.all_to_all(value, "branch", split_axis=0, concat_axis=0, tiled=True)


def dot(spec, a, b):
    return jnp.einsum(spec, a, b, preferred_element_type=F32)


def axis_bit(axis, bit):
    return (lax.axis_index(axis) >> bit) & 1


def half(value, axis, which):
    size = value.shape[axis] // 2
    return lax.dynamic_slice_in_dim(value, which * size, size, axis)


def bits_of(axis, low=0):
    return [(axis, bit) for bit in range(low, lax.axis_size(axis).bit_length() - 1)]


def halving_order():
    return bits_of("branch") + bits_of("seq", 1)


def flipped_order():
    return bits_of("branch")[::-1] + bits_of("seq", 1)


def doubling_order(flip, branch_first=False):
    branch = bits_of("branch") if flip else bits_of("branch")[::-1]
    seq = bits_of("seq", 1)[::-1]
    return (branch + seq if branch_first else seq + branch) + [("seq", 0)]


def reduce_product(a, b, order, parts=1):
    core = axis_bit("seq", 0)
    side = axis_bit(*order[0])
    came = yield dot("tm,tn->mn", a, half(b, 1, 1 - core)).astype(BF16), "seq", 0
    mine = half(b, 1, core)
    other = dot("tm,tn->mn", half(a, 1, 1 - side), mine) + half(came, 0, 1 - side)
    size = other.shape[0] // parts
    firsts = []
    for at in range(parts):
        came_part = yield other[at * size : (at + 1) * size].astype(BF16), *order[0]
        firsts.append(came_part)
    first = jnp.concatenate(firsts, axis=0)
    part = dot("tm,tn->mn", half(a, 1, side), mine) + half(came, 0, side) + first
    for axis, bit in order[1:]:
        which = axis_bit(axis, bit)
        came = yield half(part, 0, 1 - which).astype(BF16), axis, bit
        part = half(part, 0, which) + came
    return part.astype(BF16)


def product_halves(a, b, halving):
    core = axis_bit("seq", 0)
    blocks = 1 << len(halving)

    def part(which):
        value = dot("tm,tn->mn", a, half(b, 1, which)).astype(BF16)
        return value.reshape(blocks, -1, value.shape[1])

    return part(1 - core), part(core)


def own_halves(a, b, halving):
    core = axis_bit("seq", 0)
    blocks = 1 << len(halving)

    def part(which):
        value = dot("ktm,knt->mn", half(a, 2, which), b).astype(BF16)
        return value.reshape(blocks, -1, value.shape[1])

    return part(1 - core), part(core)


def reduce_own(a, b, bits):
    core = axis_bit("seq", 0)
    came = yield dot("ktm,knt->mn", half(a, 2, 1 - core), b).astype(BF16), "seq", 0
    part = dot("ktm,knt->mn", half(a, 2, core), b) + came
    for bit in bits:
        which = axis_bit("seq", bit)
        came = yield half(part, 0, 1 - which).astype(BF16), "seq", bit
        part = half(part, 0, which) + came
    return part.astype(BF16)


def finish_kernel(halvings, rounds, done, turns, sizes, *refs):
    fresh, count = len(halvings), len(rounds)
    stages = len(rounds[0])
    steps = [len(halving) for halving in halvings]
    at = 2 * fresh + count - fresh
    sents, mines, pieces = refs[:fresh], refs[fresh : 2 * fresh], refs[2 * fresh : at]
    outs, scratch = refs[at : at + count], list(refs[at + count :])
    own_sem, half_send, half_recv, send_sem, recv_sem = scratch[:5]
    scratch = scratch[5:]
    buffers = []
    for flow in range(fresh):
        first, total, piece = scratch[:3]
        pairs = [(scratch[3 + 2 * step], scratch[4 + 2 * step]) for step in range(steps[flow] - 1)]
        scratch = scratch[1 + 2 * steps[flow] :]
        buffers.append((first, total, piece, pairs))
    index = {axis: lax.axis_index(axis) for axis in sizes}

    def bit_of(axis, bit):
        return lax.rem(index[axis] // (1 << bit), 2)

    def partner(axis, bit):
        return {axis: index[axis] + (1 << bit) * (1 - 2 * bit_of(axis, bit))}

    barrier = pltpu.get_barrier_semaphore()
    for axis, bit in rounds[0]:
        pl.semaphore_signal(barrier, inc=1, device_id=partner(axis, bit), device_id_type=pl.DeviceIdType.MESH)
    slots = []
    for flow in range(count):
        slot = 0
        for stage, (axis, bit) in enumerate(rounds[flow]):
            slot = slot + bit_of(axis, bit) * (1 << stage)
        slots.append(slot)

    def region(flow, stage):
        size = 1 << stage
        return outs[flow].at[pl.ds(slots[flow] // size * size, size)]

    def own(flow, source):
        return pltpu.make_async_copy(source, region(flow, done[flow]), own_sem.at[flow])

    def send(source, target, send, recv, stage):
        copy = pltpu.make_async_remote_copy(
            src_ref=source, dst_ref=target, send_sem=send, recv_sem=recv, device_id=partner(*stage), device_id_type=pl.DeviceIdType.MESH
        )
        copy.start()
        return copy

    owns = {flow: own(flow, pieces[flow - fresh]) for flow in range(fresh, count)}
    for copy in owns.values():
        copy.start()
    pl.semaphore_wait(barrier, stages)
    halves, copies = {}, {}
    place = [0] * fresh

    def reduce_step(flow, step):
        first, total, piece, pairs = buffers[flow]
        if step == 0:
            halves[flow, 0] = send(sents[flow], first, half_send.at[flow, 0], half_recv.at[flow, 0], halvings[flow][0])
            return
        halves[flow, step - 1].wait_recv()
        if step == 1:
            total[...] = mines[flow][...].astype(F32) + first[...].astype(F32)
        else:
            size = pairs[step - 2][1].shape[0]
            kept = pl.ds(place[flow], size)
            total[kept] = total[kept] + pairs[step - 2][1][...].astype(F32)
        if step < steps[flow]:
            sent, came = pairs[step - 1]
            size = sent.shape[0]
            side = bit_of(*halvings[flow][step])
            sent[...] = total[pl.ds(place[flow] + (1 - side) * size, size)].astype(BF16)
            place[flow] = place[flow] + side * size
            halves[flow, step] = send(sent, came, half_send.at[flow, step], half_recv.at[flow, step], halvings[flow][step])
        else:
            piece[...] = total[pl.ds(place[flow], 1)].astype(BF16)
            owns[flow] = own(flow, piece)
            owns[flow].start()

    def gather_step(flow, step):
        stage = done[flow] + step
        if step == 0:
            owns[flow].wait()
        else:
            copies[flow, stage - 1].wait_recv()
        if stage < stages:
            here = region(flow, stage)
            copies[flow, stage] = send(here, here, send_sem.at[flow, stage], recv_sem.at[flow, stage], rounds[flow][stage])

    for turn in range(max(steps) + stages + 1):
        for flow in range(count):
            if flow < fresh:
                if turn <= steps[flow]:
                    reduce_step(flow, turn)
                if 0 <= turn - steps[flow] <= stages:
                    gather_step(flow, turn - steps[flow])
            elif turn in turns:
                gather_step(flow, turns.index(turn))
    for copy in list(halves.values()) + list(copies.values()):
        copy.wait_send()


def finish_everywhere(sents, mines, halvings, pieces, rounds):
    stages = len(rounds[0])
    fresh, count = len(sents), len(rounds)
    shapes = [sent.shape[1:] for sent in sents] + [piece.shape[1:] for piece in pieces]
    kinds = [BF16] * fresh + [piece.dtype for piece in pieces]
    done = [0] * fresh + [piece.shape[0].bit_length() - 1 for piece in pieces]
    branch = len([stage for stage in rounds[0] if stage[0] == "branch"])
    seq = stages - 1 - branch
    turns = list(range(seq + 1)) + [seq + 1 + 2 * at for at in range(1, branch)]
    turns = turns + [max(turns) + 3, max(turns) + 4]
    buffers = []
    for sent, halving in zip(sents, halvings):
        blocks, rows, columns = sent.shape
        buffers += [pltpu.VMEM(sent.shape, BF16), pltpu.VMEM(sent.shape, F32), pltpu.VMEM((1, rows, columns), BF16)]
        for step in range(1, len(halving)):
            buffers += [pltpu.VMEM((blocks >> step, rows, columns), BF16)] * 2
    most = max(len(halving) for halving in halvings)
    return pl.pallas_call(
        functools.partial(finish_kernel, halvings, rounds, done, turns, ("branch", "seq")),
        out_shape=tuple(jax.ShapeDtypeStruct((1 << stages,) + shape, kind) for shape, kind in zip(shapes, kinds)),
        in_specs=[pl.BlockSpec(memory_space=pltpu.VMEM)] * (2 * fresh + len(pieces)),
        out_specs=(pl.BlockSpec(memory_space=pl.ANY),) * count,
        scratch_shapes=[
            pltpu.SemaphoreType.DMA((count,)),
            pltpu.SemaphoreType.DMA((fresh, most)),
            pltpu.SemaphoreType.DMA((fresh, most)),
            pltpu.SemaphoreType.DMA((count, stages)),
            pltpu.SemaphoreType.DMA((count, stages)),
        ]
        + buffers,
        compiler_params=pltpu.CompilerParams(collective_id=0, has_side_effects=True, vmem_limit_bytes=60 * 2**20),
        name="gradient_finish",
    )(*sents, *mines, *pieces)


def columns_kernel(pieces_ref, *refs):
    out_ref = refs[-1]
    count, rows, columns = pieces_ref.shape[2:]
    for core in range(2):
        for at in range(count):
            out_ref[0, at * rows : (at + 1) * rows, core * columns : (core + 1) * columns] = pieces_ref[core, 0, at].astype(F32)


def groups_kernel(groups, branch_first, pieces_ref, *refs):
    out_ref = refs[-1]
    rows, columns = pieces_ref.shape[3:]
    depth = pieces_ref.shape[1 if branch_first else 2]
    for place, group in enumerate(groups):
        for at in range(depth):
            piece = pieces_ref[0, at, place] if branch_first else pieces_ref[0, place, at]
            out_ref[0, at * rows : (at + 1) * rows, group * columns : (group + 1) * columns] = piece.astype(F32)


def write_layer(kernel, name, gathered, block, index, steps, shape, layer, layers, base):
    rows, width = shape
    ins = [pl.BlockSpec(block, index)]
    operands = [gathered]
    aliases = {}
    if base is not None:
        ins.append(pl.BlockSpec(memory_space=pl.ANY))
        operands.append(base)
        aliases = {1: 0}
    return pl.pallas_call(
        kernel,
        grid=(steps,),
        in_specs=ins,
        out_specs=pl.BlockSpec((1, rows // steps, width), lambda at: (layer, at, 0)),
        out_shape=jax.ShapeDtypeStruct((layers, rows, width), F32),
        input_output_aliases=aliases,
        compiler_params=pltpu.CompilerParams(vmem_limit_bytes=48 * 2**20),
        name=name,
    )(*operands)


def branch_places(order):
    stages = [stage for stage in order if stage[0] == "branch"]
    return [stages.index(("branch", bit)) for bit in range(len(stages))]


def write_columns(gathered, order, halving, layer, layers, base):
    pieces, rows, columns = gathered.shape
    places = branch_places(order)
    branch = 1 << len(places)
    seq = pieces // (2 * branch)

    def index(at):
        slot = 0
        for rank, (_, bit) in enumerate(halving[: len(places)]):
            slot = slot + (at // (1 << (len(places) - 1 - rank))) % 2 * (1 << places[bit])
        return 0, slot, 0, 0, 0

    gathered = gathered.reshape(2, branch, seq, rows, columns)
    shape = (branch * seq * rows, 2 * columns)
    return write_layer(columns_kernel, "gradient_columns", gathered, (2, 1, seq, rows, columns), index, branch, shape, layer, layers, base)


def write_groups(gathered, order, layer, layers, base):
    pieces, rows, columns = gathered.shape
    places = branch_places(order)
    branch = 1 << len(places)
    seq = pieces // (2 * branch)
    groups = [sum(((at >> place) & 1) << bit for bit, place in enumerate(places)) for at in range(branch)]
    branch_first = order[0][0] == "branch"
    split = (seq, branch) if branch_first else (branch, seq)
    gathered = gathered.reshape((2,) + split + (rows, columns))
    kernel = functools.partial(groups_kernel, groups, branch_first)
    shape = (2 * seq * rows, branch * columns)
    return write_layer(kernel, "gradient_groups", gathered, (1,) + split + (rows, columns), lambda at: (at, 0, 0, 0, 0), 2, shape, layer, layers, base)


def layer_forward(stream, layer, weights, gain, shift, side, tables, geometry):
    w_in, w_out, w_up, w_down = weights
    first = geometry["first"]
    xhat, _ = normalize(stream)
    normed = (xhat * gain[0] + shift[0]).astype(BF16)
    q, kv, own2, own3, own4, normed_all = prepare(normed, side, geometry["attention_in"], layer, tables["kf"], LOG2E * SIZE**-0.5, geometry["branch"])
    far = Task(gather_far(own2, own3, own4, geometry))
    lower = None
    for part in range(2):
        flights, q = start([far], q)
        lower = lower_forward(q, kv, tables["f0"], tables["f1"], part, 2, lower)
        land(flights, lower)
    while not far.done:
        flights, lower = start([far], lower)
        land(flights, lower)
    r2, r3, r4 = far.result
    att, qb = upper_forward(q, lower, r2, r3, r4, tables["f2"], tables["f3"], tables["f4"])
    saved_parts = (kv, r2, r3, r4, qb, att)
    att_rows = join_groups(to_rows(att, tables["narrow"]))
    midway = stream + dot("ct,cd->td", att_rows, w_out)
    xhat, _ = normalize(midway)
    second = (xhat * gain[1] + shift[1]).astype(BF16)
    pre_act = dot("td,df->tf", second, w_up)
    hidden = (0.5 * pre_act * (1.0 + lax.erf(pre_act * np.float32(2**-0.5)))).astype(BF16)
    result = midway + dot("tf,fd->td", hidden, w_down)
    return result, (stream, normed_all, saved_parts, att_rows, midway, second, pre_act, hidden)


def layer_backward(gradient, saved, weights, gain, shift, tables, geometry, old, flights, last):
    w_in, w_out, w_up, w_down = weights
    stream, normed_all, parts, att_rows, midway, second, pre_act, hidden = saved
    kv, r2, r3, r4, qb, att = parts
    first = geometry["first"]
    halving = halving_order()
    seq_bits = [bit for _, bit in bits_of("seq", 1)]

    down_in = gradient.astype(BF16)
    new, ahead = [], []
    if not last:
        down = Task(reduce_product(hidden, down_in, halving))
        ahead, down_in = start([down], down_in)
    grad_hidden = dot("td,fd->tf", down_in, w_down)
    cdf = 0.5 * (1.0 + lax.erf(pre_act * np.float32(2**-0.5)))
    density = jnp.exp(-0.5 * pre_act * pre_act) * np.float32((2 * np.pi) ** -0.5)
    grad_pre = (grad_hidden * (cdf + pre_act * density)).astype(BF16)
    grad_second = dot("tf,mf->tm", grad_pre, w_up)
    back, gain_two, shift_two = normalize_back(midway, gain[1], grad_second)
    grad_midway = gradient + back
    out_in = grad_midway.astype(BF16)
    grad_rows = split_groups(dot("cd,td->ct", w_out, out_in).astype(BF16), geometry["branch"])
    land(flights + ahead, grad_rows)
    grad_rows, second, att_rows = lax.optimization_barrier((grad_rows, second, att_rows))
    if not last:
        ahead, grad_rows = start([down], grad_rows)
    waiting, grad_rows = start(old, grad_rows)
    rows = swap(grad_rows)
    if last:
        new = [
            product_halves(hidden, down_in, flipped_order()),
            product_halves(second, grad_pre, halving),
            product_halves(att_rows.T, out_in, halving),
        ]
        rows = pin(new, rows)
        ours = []
    else:
        up = Task(reduce_product(second, grad_pre, halving, 2))
        out = Task(reduce_product(att_rows.T, out_in, halving))
        rows = pin([up.pending[0], out.pending[0]], rows)
        new = [down, up, out]
        ours = new
    flights, rows = start(ours[1:], rows)
    g = prepare_back(first, rows, tables["narrow"], att)
    du, d2, d3, d4 = upper_back(qb, g, r2, r3, r4, tables["f2"], tables["f3"], tables["f4"])
    far = Task(return_far(d2, d3, d4, geometry))
    short, _ = start([far], d2)
    land(flights + ahead + waiting, du)
    land(short, d2)
    grads = None
    for part in range(2):
        moving = [task for task in ours + old if part or task is not ours[-1]] if ours else old
        flights, qb = start([far] + moving, qb)
        grads = lower_back(qb, g, kv, tables["f0"], tables["f1"], part, 2, grads)
        land(flights, grads)
    dq, dkv = grads
    flights, dq = start(ours + old, dq)
    back_rows = to_rows_back(first, dq, du, dkv, far.result, tables["full"], SIZE**-0.5)
    returned = swap(back_rows)
    normed_all, back_rows = lax.optimization_barrier((normed_all, back_rows))
    if last:
        enter = own_halves(normed_all, back_rows, bits_of("seq", 1))
        returned = pin(enter, returned)
    else:
        enter = Task(reduce_own(normed_all, back_rows, seq_bits))
        returned = pin(enter.pending[0], returned)
        extra, returned = start([enter], returned)
        flights = flights + extra
    projected = join_groups(returned)
    grad_first = dot("ct,dc->td", projected, w_in)
    back, gain_one, shift_one = normalize_back(stream, gain[0], grad_first)
    vectors = jnp.stack([gain_one, gain_two, shift_one, shift_two])
    return grad_midway + back, vectors, new + [enter], flights


def local(tile_embeddings, tile_valid, slide_bounds, norm_gain, norm_bias, attention_in, attention_out, hidden_up, hidden_down, cotangent):
    branch = lax.axis_size("branch")
    seq = lax.axis_size("seq")
    heads = H // branch
    rows, width = tile_embeddings.shape
    shard = rows * branch
    blocks = shard // BLOCK
    seq_at = lax.axis_index("seq")
    origin = seq_at * shard
    bit = 1 if blocks == 2 else 0

    def slide_at(place):
        return jnp.sum((place >= slide_bounds[1:-1]).astype(jnp.int32))

    def same(mask):
        return slide_at((seq_at ^ mask) * shard) == slide_at(origin)

    low, high = 1 << bit, 2 << bit
    geometry = dict(
        attention_in=attention_in,
        branch=branch,
        blocks=blocks,
        bit=bit,
        first=(lax.axis_index("branch") * heads).astype(jnp.int32).reshape(1),
        same=(None, same(low), same(high), same(high | low)),
    )
    full, narrow = placements(heads)
    tables = dict(
        full=jnp.asarray(full),
        narrow=jnp.asarray(narrow),
        kf=jnp.asarray(key_features()),
        f0=jnp.asarray(query_features(block_classes, 0)),
        f1=jnp.asarray(query_features(block_classes[:512], 1)),
        f2=jnp.asarray(query_features(upper_classes, 2)),
        f3=jnp.asarray(query_features(upper_classes[:256], 3)),
        f4=jnp.asarray(query_features(upper_classes[:128], 4)),
    )
    valid = lax.dynamic_slice_in_dim(tile_valid, origin, shard)
    valid = valid.reshape(branch, rows // 16, 16).swapaxes(1, 2).reshape(shard, 1)
    side = jnp.where((lanes_of((1, 128)) == BIAS) & (valid != 1), NEG, 0.0).astype(BF16)

    layers = attention_in.shape[0]
    weights = [(attention_in[at], attention_out[at], hidden_up[at], hidden_down[at]) for at in range(layers)]
    stream = to_major(tile_embeddings).astype(F32)
    outputs, saved_all = [], []
    for layer in range(layers):
        stream, saved = layer_forward(stream, layer, weights[layer], norm_gain[layer], norm_bias[layer], side, tables, geometry)
        outputs.append(from_major(stream.astype(BF16)))
        saved_all.append(saved)
    gradient = to_major(cotangent).astype(F32)
    vectors = [None] * layers
    tasks, flights = [], []
    first_round, flipped = doubling_order(False), doubling_order(True)
    rounds = [[flipped, first_round, first_round, first_round] for _ in range(layers)]
    rounds[0][3] = doubling_order(True, branch_first=True)
    for layer in reversed(range(layers)):
        gradient, vectors[layer], new, flights = layer_backward(
            gradient, saved_all[layer], weights[layer], norm_gain[layer], norm_bias[layer], tables, geometry, tasks, flights, layer == 0
        )
        if layer:
            tasks = tasks + new
    land(flights, gradient)
    for task in tasks:
        while not task.done:
            task.advance(jax.tree.map(lambda v: exchange(v, *task.pending[1:]), task.pending[0]))
    core = [("seq", 0)]
    halving = halving_order()
    halvings = [core + flipped_order(), core + halving, core + halving, core + bits_of("seq", 1)]
    pieces = [task.result[None] for task in tasks] + [jnp.stack(vectors).reshape(1, -1, width)]
    order = rounds[0] + [order for layer in reversed(range(1, layers)) for order in rounds[layer]] + [first_round]
    gathered = finish_everywhere([sent for sent, _ in new], [mine for _, mine in new], halvings, pieces, order)
    places = [(0, member) for member in range(4)] + [(layer, member) for layer in reversed(range(1, layers)) for member in range(4)]
    vectors = jnp.sum(gathered[-1], axis=0).reshape(layers, 2, 2, width)
    sums = [None] * 4
    for (layer, member), whole in zip(places, gathered[:-1]):
        if member == 3:
            sums[member] = write_groups(whole, rounds[layer][member], layer, layers, sums[member])
        else:
            follows = halvings[member][1:] if layer == 0 else halving
            sums[member] = write_columns(whole, rounds[layer][member], follows, layer, layers, sums[member])
    down, up, out, enter = sums
    return (jnp.stack(outputs), from_major(gradient), vectors[:, 0], vectors[:, 1], enter, out, up, down)


def solution(mesh):
    split = P(("seq", "branch"), None)
    in_specs = (split,) + (P(),) * 8 + (split,)
    out_specs = (P(None, ("seq", "branch"), None), split) + (P(),) * 6
    return jax.shard_map(local, mesh=mesh, in_specs=in_specs, out_specs=out_specs, check_vma=False)
```

```python
import functools
import numpy as np
import jax
import jax.numpy as jnp
from jax import lax
from jax.experimental import pallas as pl
from jax.experimental.pallas import tpu as pltpu
from jax.sharding import PartitionSpec as P

BLOCK = 1024
CHUNK = 32
ORDER = (0, 8, 4, 12, 2, 10, 6, 14, 1, 9, 5, 13, 3, 11, 7, 15)
ONE, BIAS, HIGH, LOW, VALUE = 48, 51, 52, 57, 64
NEG = -1e30
LOG2E = 1.4426950408889634
LN2 = 0.6931471805599453
F32, BF16 = jnp.float32, jnp.bfloat16


def low_np(x):
    return np.asarray(x, np.float32).astype(jnp.bfloat16).astype(np.float32)


def query_features(classes, level):
    table = np.zeros((len(classes), 128), np.float32)
    table[:, BIAS] = 1.0
    for at, mine in enumerate(classes):
        for theirs in range(5):
            met = min(mine, theirs) - level + 1
            value = np.log2(met) if met > 0 else NEG
            high = low_np(value)
            table[at, HIGH + theirs] = high
            table[at, LOW + theirs] = low_np(value - high) if met > 0 else 0.0
    return table.astype(jnp.bfloat16)


block_classes = [4] * 64 + [3] * 64 + [2] * 128 + [1] * 256 + [0] * 512
upper_classes = [4] * 128 + [3] * 128 + [2] * 256


def key_features():
    table = np.zeros((BLOCK, 128), np.float32)
    table[:, ONE : ONE + 3] = 1.0
    for at, mine in enumerate(block_classes):
        table[at, HIGH + mine] = 1.0
        table[at, LOW + mine] = 1.0
    return table.astype(jnp.bfloat16)


def nt(a, b):
    return lax.dot_general(a, b, (((1,), (1,)), ((), ())), preferred_element_type=F32)


def tn(a, b):
    return lax.dot_general(a, b, (((0,), (0,)), ((), ())), preferred_element_type=F32)


def nn(a, b):
    return lax.dot_general(a, b, (((1,), (0,)), ((), ())), preferred_element_type=F32)


def lanes_of(shape):
    return lax.broadcasted_iota(jnp.int32, shape, len(shape) - 1)


def split3(column):
    high = column.astype(BF16)
    rest = column - high.astype(F32)
    mid = rest.astype(BF16)
    last = (rest - mid.astype(F32)).astype(BF16)
    return high, mid, last


def place3(base, column):
    high, mid, last = split3(column)
    lane = lanes_of(base.shape)
    out = jnp.where(lane == ONE, high.astype(F32), base)
    out = jnp.where(lane == ONE + 1, mid.astype(F32), out)
    return jnp.where(lane == ONE + 2, last.astype(F32), out)


def chunk_row(head, block, position, part, per_dev):
    residue = lax.rem(ORDER[position] + head, 16)
    return pl.multiple_of((2 * block + part) * per_dev + residue * CHUNK, CHUNK)


def prepare_kernel(heads, blocks, scale, bits, layer, x_ref, side_ref, weights_ref, kf_ref, q_ref, kv_ref, *refs):
    near_refs, (all_ref, rows_all, work, placed, weight_ref, send_sem, recv_sem, in_sem, out_sem) = refs[:3], refs[3:]
    weight = pltpu.make_async_copy(weights_ref.at[layer], weight_ref, in_sem)
    weight.start()
    me = lax.axis_index("branch")
    count, rows = rows_all.shape[:2]

    def away(mask):
        place = me
        for bit in range(bits):
            if mask >> bit & 1:
                place = place + (1 << bit) * (1 - 2 * lax.rem(me // (1 << bit), 2))
        return place

    def place_weight(head):
        shape = (weight_ref.shape[1], 256)
        lane = lax.broadcasted_iota(jnp.int32, shape, 1)
        column = lax.broadcasted_iota(jnp.int32, shape, 0) - (me * heads + head) * 144
        query = (lane < 48) & (column == lane)
        key = (lane >= 128) & (lane < 176) & (column == lane - 80)
        value = (lane >= 128 + VALUE) & (lane < 128 + VALUE + 48) & (column == lane - (32 + VALUE))
        chosen = (query | key | value).astype(F32).astype(BF16)
        placed[head] = nn(weight_ref[...], chosen).astype(BF16)

    barrier = pltpu.get_barrier_semaphore()
    for bit in range(bits):
        pl.semaphore_signal(barrier, inc=1, device_id={"branch": away(1 << bit)}, device_id_type=pl.DeviceIdType.MESH)
    rows_all[pl.ds(me, 1)] = x_ref[...][None]
    pl.semaphore_wait(barrier, bits)
    orders = (list(range(bits)), list(range(bits))[::-1])
    size = rows // 2
    copies = {}

    def begin(flow, stage):
        order = orders[flow]
        masks = [0]
        for bit in order[:stage]:
            masks = masks + [mask | 1 << bit for mask in masks]
        for number, mask in enumerate(masks):
            place = (1 << stage) - 1 + number
            here = rows_all.at[away(mask), pl.ds(flow * size, size)]
            copy = pltpu.make_async_remote_copy(
                src_ref=here,
                dst_ref=here,
                send_sem=send_sem.at[flow, place],
                recv_sem=recv_sem.at[flow, place],
                device_id={"branch": away(1 << order[stage])},
                device_id_type=pl.DeviceIdType.MESH,
            )
            copy.start()
            copies.setdefault((flow, stage), []).append(copy)

    def project(mask):
        place = away(mask)
        at = pl.multiple_of(place * rows, rows)
        source = rows_all[place]
        for head in range(heads):
            value = nn(source, placed[head])
            work[head, pl.ds(at, rows), :128] = (value[:, :128] * scale).astype(BF16)
            work[head, pl.ds(at, rows), 128:] = value[:, 128:].astype(BF16)

    for stage in range(bits):
        for flow in range(2):
            if stage > 0:
                for copy in copies[flow, stage - 1]:
                    copy.wait_recv()
            begin(flow, stage)
        if stage == 0:
            weight.wait()
            for head in range(heads):
                place_weight(head)
            project(0)
    for flow in range(2):
        for copy in copies[flow, bits - 1]:
            copy.wait_recv()
    kept = pltpu.make_async_copy(rows_all, all_ref, out_sem)
    kept.start()
    for mask in range(1, count):
        project(mask)
    kf = kf_ref[...]
    for head in range(heads):
        which = me * heads + head
        for position in range(16):
            features = kf[position * 64 : position * 64 + CHUNK]
            for block in range(blocks):
                for part in range(2):
                    row = chunk_row(which, block, position, part, rows)
                    at = position * 64 + part * CHUNK
                    source = work[head, pl.ds(row, CHUNK), :]
                    q_ref[head, block, at : at + CHUNK, :] = source[:, :128]
                    key_value = source[:, 128:] + features + side_ref[pl.ds(row, CHUNK), :]
                    kv_ref[head, block, at : at + CHUNK, :] = key_value
                    for near_ref in near_refs:
                        if at < near_ref.shape[2]:
                            near_ref[head, block, at : at + CHUNK, :] = key_value
    kept.wait()
    for group in copies.values():
        for copy in group:
            copy.wait_send()


def prepare(rows, side, weights, layer, kf, scale, count):
    heads = weights.shape[2] // (144 * count)
    total = rows.shape[0] * count
    blocks = total // BLOCK
    bits = count.bit_length() - 1
    shape = jax.ShapeDtypeStruct((heads, blocks, BLOCK, 128), BF16)
    whole = (count,) + rows.shape
    near = tuple(jax.ShapeDtypeStruct((heads, blocks, size, 128), BF16) for size in (256, 128, 64))
    return pl.pallas_call(
        functools.partial(prepare_kernel, heads, blocks, scale, bits, layer),
        out_shape=(shape, shape) + near + (jax.ShapeDtypeStruct(whole, BF16),),
        in_specs=[pl.BlockSpec(memory_space=pltpu.VMEM if at != 2 else pl.ANY) for at in range(4)],
        out_specs=(pl.BlockSpec(memory_space=pltpu.VMEM),) * 5 + (pl.BlockSpec(memory_space=pl.ANY),),
        scratch_shapes=[
            pltpu.VMEM(whole, BF16),
            pltpu.VMEM((heads, total, 256), BF16),
            pltpu.VMEM((heads, weights.shape[1], 256), BF16),
            pltpu.VMEM(weights.shape[1:], BF16),
            pltpu.SemaphoreType.DMA((2, count - 1)),
            pltpu.SemaphoreType.DMA((2, count - 1)),
            pltpu.SemaphoreType.DMA,
            pltpu.SemaphoreType.DMA,
        ],
        compiler_params=pltpu.CompilerParams(collective_id=1 + layer, has_side_effects=True, vmem_limit_bytes=48 * 2**20),
        name="attention_prepare",
    )(rows, side, weights, kf)


def lower_kernel(q_ref, kv_ref, f0_ref, f1_ref, *refs):
    o_ref = refs[-1]
    step = 256
    for block in range(2):
        own = kv_ref[0, block]
        near = kv_ref[0, 1 - block, :512]
        for at in range(0, BLOCK, step):
            rows = slice(at, at + step)
            base = q_ref[0, block, rows]
            s0 = nt(base + f0_ref[rows], own)
            top = jnp.max(s0, axis=1, keepdims=True)
            if at < 512:
                s1 = nt(base + f1_ref[rows], near)
                top = jnp.maximum(top, jnp.max(s1, axis=1, keepdims=True))
            own_rows = own[rows].astype(F32)
            meet = base.astype(F32) * own_rows
            alone = jnp.sum(meet, axis=1, keepdims=True)
            lane = lanes_of(own_rows.shape)
            bias = jnp.min(jnp.where(lane == BIAS, own_rows, 0.0), axis=1, keepdims=True)
            classes = sum((lax.broadcasted_iota(jnp.int32, (step, 1), 0) + at < edge).astype(F32) for edge in (512, 256, 128, 64))
            alone = jnp.where(bias < 0.0, alone + jnp.log2(classes + 1.0), NEG)
            top = jnp.maximum(top, alone)
            out = nn(jnp.exp2(s0 - top).astype(BF16), own)
            if at < 512:
                out = out + nn(jnp.exp2(s1 - top).astype(BF16), near)
            out = out + jnp.exp2(alone - top) * own_rows
            o_ref[0, block, rows] = jnp.where(lane == 0, top, out)


def part_call(kernel, name, operands, tables, outs, part, parts, base, cost):
    heads, blocks = operands[0].shape[:2]
    count = heads // parts
    spec = pl.BlockSpec((1, 2, BLOCK, 128), lambda h, p: (h + part * count, p, 0, 0))
    whole = lambda a: pl.BlockSpec(a.shape, lambda h, p: (0,) * a.ndim)
    ins = [spec] * len(operands) + [whole(table) for table in tables]
    arrays = list(operands) + list(tables)
    aliases = {}
    if base is not None:
        for at, array in enumerate(base):
            aliases[len(arrays)] = at
            arrays.append(array)
            ins.append(pl.BlockSpec(memory_space=pl.ANY))
    pairs = int(count * blocks * 1.25 * 2**20)
    return pl.pallas_call(
        kernel,
        grid=(count, blocks // 2),
        in_specs=ins,
        out_specs=(spec,) * outs,
        out_shape=(jax.ShapeDtypeStruct(operands[0].shape, F32),) * outs,
        input_output_aliases=aliases,
        compiler_params=pltpu.CompilerParams(vmem_limit_bytes=56 * 2**20),
        cost_estimate=pl.CostEstimate(flops=pairs * 256 * cost, bytes_accessed=operands[0].size * 8 // parts, transcendentals=pairs),
        name=name,
    )(*arrays)


def lower_forward(q, kv, f0, f1, part, parts, base):
    out = part_call(lower_kernel, "attention_lower", (q, kv), (f0, f1), 1, part, parts, None if base is None else (base,), 4)
    return out[0]


UPPER = ((0, 0, 64), (1, 0, 64), (0, 64, 128), (1, 64, 128), (0, 128, 256), (1, 128, 256))


def gather_upper(ref, lead):
    return jnp.concatenate([ref[(*lead, block, slice(low, high))] for block, low, high in UPPER], axis=0)


def upper_kernel(q_ref, o_ref, r2_ref, r3_ref, r4_ref, f2_ref, f3_ref, f4_ref, att_ref, qb_ref):
    merged = {}
    uq = gather_upper(q_ref, (0,))
    ol = gather_upper(o_ref, (0,))
    for low, high in ((0, 128), (128, 256), (256, 512)):
        base = uq[low:high]
        pairs = [(nt(base + f2_ref[low:high], r2_ref[0, 0]), r2_ref[0, 0])]
        if high <= 256:
            pairs.append((nt(base + f3_ref[low:high], r3_ref[0]), r3_ref[0]))
        if high <= 128:
            pairs.append((nt(base + f4_ref[low:high], r4_ref[0]), r4_ref[0]))
        old = ol[low:high]
        lane = lanes_of(old.shape)
        before = old[:, 0:1]
        top = before
        for scores, keys in pairs:
            top = jnp.maximum(top, jnp.max(scores, axis=1, keepdims=True))
        out = old * jnp.exp2(before - top)
        for scores, keys in pairs:
            out = out + nn(jnp.exp2(scores - top).astype(BF16), keys)
        merged[low] = jnp.where(lane == 0, top, out)
    whole = jnp.concatenate([merged[0], merged[128], merged[256]], axis=0)
    place = 0

    def finish(block, low, high, rows):
        lane = lanes_of(rows.shape)
        top = rows[:, 0:1]
        total = rows[:, ONE : ONE + 1]
        att_ref[0, block, low:high] = jnp.where((lane >= VALUE) & (lane < VALUE + 48), rows / total, 0.0)
        lse = top + jnp.log2(total)
        qb_ref[0, block, low:high] = place3(q_ref[0, block, low:high].astype(F32), -lse).astype(BF16)

    for block, low, high in UPPER:
        finish(block, low, high, whole[place : place + high - low])
        place += high - low
    for block in range(2):
        for low in (256, 512, 768):
            finish(block, low, low + 256, o_ref[0, block, low : low + 256])


def upper_forward(q, o, r2, r3, r4, f2, f3, f4):
    heads, blocks = q.shape[:2]
    spec = pl.BlockSpec((1, 2, BLOCK, 128), lambda h, p: (h, p, 0, 0))
    two = pl.BlockSpec((1, 1, 512, 128), lambda h, p: (h, p, 0, 0))
    far = pl.BlockSpec((1, 512, 128), lambda h, p: (h, 0, 0))
    whole = lambda a: pl.BlockSpec(a.shape, lambda h, p: (0,) * a.ndim)
    return pl.pallas_call(
        upper_kernel,
        grid=(heads, blocks // 2),
        in_specs=[spec, spec, two, far, far, whole(f2), whole(f3), whole(f4)],
        out_specs=(spec, spec),
        out_shape=(jax.ShapeDtypeStruct(q.shape, F32), jax.ShapeDtypeStruct(q.shape, BF16)),
        compiler_params=pltpu.CompilerParams(vmem_limit_bytes=48 * 2**20),
        name="attention_upper",
    )(q, o, r2, r3, r4, f2, f3, f4)


def chunk_place(head, residue, part):
    turn = lax.rem(residue - head + 32, 16)
    position = 8 * lax.rem(turn, 2) + 4 * lax.rem(turn // 2, 2) + 2 * lax.rem(turn // 4, 2) + turn // 8
    return pl.multiple_of(position * 64 + part * CHUNK, CHUNK)


def exchange_rows(bits, make, out_ref, sent, land, send_sem, recv_sem, out_sem):
    me = lax.axis_index("branch")
    count = 1 << bits

    def away(mask):
        place = me
        for bit in range(bits):
            if mask >> bit & 1:
                place = place + (1 << bit) * (1 - 2 * lax.rem(me // (1 << bit), 2))
        return place

    barrier = pltpu.get_barrier_semaphore()
    for mask in range(1, count):
        pl.semaphore_signal(barrier, inc=1, device_id={"branch": away(mask)}, device_id_type=pl.DeviceIdType.MESH)
    copies = []
    for mask in range(count - 1, 0, -1):
        sent[mask - 1] = make(away(mask))
        if not copies:
            pl.semaphore_wait(barrier, count - 1)
        copy = pltpu.make_async_remote_copy(
            src_ref=sent.at[mask - 1],
            dst_ref=land.at[me],
            send_sem=send_sem.at[mask - 1],
            recv_sem=recv_sem.at[mask - 1],
            device_id={"branch": away(mask)},
            device_id_type=pl.DeviceIdType.MESH,
        )
        copy.start()
        copies.append(copy)
    land[pl.ds(me, 1)] = make(me)[None]
    for copy in copies:
        copy.wait_recv()
    kept = pltpu.make_async_copy(land, out_ref, out_sem)
    kept.start()
    kept.wait()
    for copy in copies:
        copy.wait_send()


def exchange_scratch(count, shape):
    return [
        pltpu.VMEM((count - 1,) + shape, BF16),
        pltpu.VMEM((count,) + shape, BF16),
        pltpu.SemaphoreType.DMA((count - 1,)),
        pltpu.SemaphoreType.DMA((count - 1,)),
        pltpu.SemaphoreType.DMA,
    ]


def rows_kernel(heads, bits, a_ref, place_ref, out_ref, work, *exchange):
    me = lax.axis_index("branch")

    def make(position):
        block, part = position // 2, lax.rem(position, 2)
        value = None
        for head in range(heads):
            for residue in range(16):
                at = chunk_place(me * heads + head, residue, part)
                work[head, residue * CHUNK : (residue + 1) * CHUNK, :] = a_ref[head, block, pl.ds(at, CHUNK), :].astype(BF16)
            placed = nt(place_ref[head], work[head])
            value = placed if value is None else value + placed
        return value.astype(BF16)

    exchange_rows(bits, make, out_ref, *exchange)


def to_rows(att, place):
    heads, blocks = att.shape[:2]
    shape = (place.shape[1], BLOCK // 2)
    count = 2 * blocks
    return pl.pallas_call(
        functools.partial(rows_kernel, heads, count.bit_length() - 1),
        out_shape=jax.ShapeDtypeStruct((count,) + shape, BF16),
        in_specs=[pl.BlockSpec(memory_space=pltpu.VMEM)] * 2,
        out_specs=pl.BlockSpec(memory_space=pl.ANY),
        scratch_shapes=[pltpu.VMEM((heads, BLOCK // 2, 128), BF16)] + exchange_scratch(count, shape),
        compiler_params=pltpu.CompilerParams(collective_id=8, has_side_effects=True, vmem_limit_bytes=48 * 2**20),
        name="attention_rows",
    )(att, place)


def prepare_back_kernel(heads, blocks, first_ref, x_ref, place_ref, att_ref, g_ref, work):
    for head in range(heads):
        for part in range(x_ref.shape[0]):
            work[part * 512 : part * 512 + 512] = tn(x_ref[part], place_ref[head]).astype(BF16)
        which = first_ref[0] + head
        for position in range(16):
            for block in range(blocks):
                for part in range(2):
                    row = chunk_row(which, block, position, part, 512)
                    at = position * 64 + part * CHUNK
                    g_ref[head, block, at : at + CHUNK, :] = work[pl.ds(row, CHUNK), :]
        for block in range(blocks):
            for at in range(0, BLOCK, 256):
                rows = slice(at, at + 256)
                grad = g_ref[head, block, rows].astype(F32)
                dots = jnp.sum(grad * att_ref[head, block, rows], axis=1, keepdims=True)
                g_ref[head, block, rows] = place3(grad, -dots).astype(BF16)


def prepare_back(first, rows, place, att):
    heads, blocks = att.shape[:2]
    total = blocks * BLOCK
    return pl.pallas_call(
        functools.partial(prepare_back_kernel, heads, blocks),
        out_shape=jax.ShapeDtypeStruct(att.shape, BF16),
        in_specs=[pl.BlockSpec(memory_space=pltpu.SMEM)]
        + [pl.BlockSpec(memory_space=pltpu.VMEM)] * 3,
        out_specs=pl.BlockSpec(memory_space=pltpu.VMEM),
        scratch_shapes=[pltpu.VMEM((total, 128), BF16)],
        compiler_params=pltpu.CompilerParams(vmem_limit_bytes=48 * 2**20),
        name="attention_prepare_back",
    )(first, rows, place, att)


def back_tile(kv, key_t, q_scores, g, q):
    probs = jnp.exp2(nt(kv, q_scores))
    grad_scores = (probs * nt(kv, g)).astype(BF16)
    grad_kv = nn(probs.astype(BF16), g) + nn(grad_scores, q)
    return grad_kv, nn(key_t, grad_scores)


def upper_back_kernel(qb_ref, g_ref, r2_ref, r3_ref, r4_ref, f2_ref, f3_ref, f4_ref, dq_ref, d2_ref, d3_ref, d4_ref):
    uq = gather_upper(qb_ref, (0,))
    ug = gather_upper(g_ref, (0,))
    dq = None
    lane = lanes_of((256, 128))
    for ref, out, f_ref, count in ((r2_ref.at[0], d2_ref.at[0], f2_ref, 512), (r3_ref, d3_ref.at[0], f3_ref, 256), (r4_ref, d4_ref.at[0], f4_ref, 128)):
        q = uq[:count]
        g = ug[:count]
        qs = q + f_ref[...]
        total = None
        for at in range(0, 512, 256):
            kv = ref[0, at : at + 256]
            key_t = kv.astype(F32).T[:48].astype(BF16)
            grad_kv, part = back_tile(kv, key_t, qs, g, q)
            out[0, at : at + 256] = jnp.where(lane < 48, grad_kv * LN2, grad_kv).astype(BF16)
            total = part if total is None else total + part
        rows = total.T
        if count < 512:
            rows = jnp.concatenate([rows, jnp.zeros((512 - count, 48), F32)], axis=0)
        dq = rows if dq is None else dq + rows
    dq_ref[0, 0] = jnp.concatenate([dq, jnp.zeros((512, 80), F32)], axis=1)


def upper_back(qb, g, r2, r3, r4, f2, f3, f4):
    heads, blocks = qb.shape[:2]
    pairs = blocks // 2
    spec = pl.BlockSpec((1, 2, BLOCK, 128), lambda h, p: (h, p, 0, 0))
    two = pl.BlockSpec((1, 1, 512, 128), lambda h, p: (h, p, 0, 0))
    far = pl.BlockSpec((1, 512, 128), lambda h, p: (h, 0, 0))
    whole = lambda a: pl.BlockSpec(a.shape, lambda h, p: (0,) * a.ndim)
    shape = (heads, pairs, 512, 128)
    return pl.pallas_call(
        upper_back_kernel,
        grid=(heads, pairs),
        in_specs=[spec, spec, two, far, far, whole(f2), whole(f3), whole(f4)],
        out_specs=(two,) * 4,
        out_shape=(jax.ShapeDtypeStruct(shape, F32),) + (jax.ShapeDtypeStruct(shape, BF16),) * 3,
        compiler_params=pltpu.CompilerParams(vmem_limit_bytes=48 * 2**20),
        name="attention_upper_back",
    )(qb, g, r2, r3, r4, f2, f3, f4)


def lower_back_kernel(qb_ref, g_ref, kv_ref, f0_ref, f1_ref, *refs):
    dq_ref, dkv_ref = refs[-2:]
    step = 256
    lane = lanes_of((step, 128))
    totals = [None, None]
    for block in range(2):
        q = qb_ref[0, block]
        g = g_ref[0, block]
        q0 = q + f0_ref[...]
        far_q = qb_ref[0, 1 - block, :512]
        far_g = g_ref[0, 1 - block, :512]
        far_q1 = far_q + f1_ref[...]
        for at in range(0, BLOCK, step):
            rows = slice(at, at + step)
            kv = kv_ref[0, block, rows]
            key_t = kv.astype(F32).T[:48].astype(BF16)
            grad_kv, part = back_tile(kv, key_t, q0, g, q)
            totals[block] = part if totals[block] is None else totals[block] + part
            if at < 512:
                more_kv, part = back_tile(kv, key_t, far_q1, far_g, far_q)
                grad_kv = grad_kv + more_kv
                part = jnp.concatenate([part, jnp.zeros((48, 512), F32)], axis=1)
                totals[1 - block] = part if totals[1 - block] is None else totals[1 - block] + part
            kv_rows = kv.astype(F32)
            q_rows = q[rows].astype(F32)
            g_rows = g[rows].astype(F32)
            bias = jnp.min(jnp.where(lane == BIAS, kv_rows, 0.0), axis=1, keepdims=True)
            classes = sum((lax.broadcasted_iota(jnp.int32, (step, 1), 0) + at < edge).astype(F32) for edge in (512, 256, 128, 64))
            met = jnp.where(lane < ONE + 3, q_rows * kv_rows, 0.0)
            score = jnp.sum(met, axis=1, keepdims=True) + jnp.log2(classes + 1.0)
            prob = jnp.where(bias < 0.0, jnp.exp2(jnp.where(bias < 0.0, score, NEG)), 0.0)
            grad_score = prob * jnp.sum(jnp.where((lane >= ONE) & (lane != BIAS), g_rows * kv_rows, 0.0), axis=1, keepdims=True)
            grad_kv = grad_kv + prob * g_rows + grad_score * q_rows
            dkv_ref[0, block, rows] = jnp.where(lane < 48, grad_kv * LN2, grad_kv)
            dq_ref[0, block, rows] = grad_score * kv_rows
    for block in range(2):
        for at in range(0, BLOCK, step):
            rows = slice(at, at + step)
            value = totals[block][:, rows].T
            value = jnp.concatenate([value, jnp.zeros((step, 80), F32)], axis=1)
            dq_ref[0, block, rows] = dq_ref[0, block, rows] + value


def lower_back(qb, g, kv, f0, f1, part, parts, base):
    return part_call(lower_back_kernel, "attention_lower_back", (qb, g, kv), (f0, f1), 2, part, parts, base, 10)


def rows_back_kernel(heads, blocks, scale, first_ref, dq_ref, du_ref, dkv_ref, x2_ref, place_ref, out_ref, work, sum_q, sum_kv):
    for head in range(heads):
        for block in range(blocks):
            start = 0
            for ub, low, high in UPPER:
                if ub == block % 2:
                    sum_q[head, block, low:high] = dq_ref[head, block, low:high] + du_ref[head, block // 2, start : start + high - low]
                start += high - low
            sum_q[head, block, 256:] = dq_ref[head, block, 256:]
            sum_kv[head, block, :256] = dkv_ref[head, block, :256] + x2_ref[head, block].astype(F32)
            sum_kv[head, block, 256:] = dkv_ref[head, block, 256:]
        which = first_ref[0] + head
        for residue in range(16):
            for block in range(blocks):
                for part in range(2):
                    row = (2 * block + part) * 512 + residue * CHUNK
                    at = chunk_place(which, residue, part)
                    grad_q = sum_q[head, block, pl.ds(at, CHUNK), :]
                    grad_kv = sum_kv[head, block, pl.ds(at, CHUNK), :]
                    lane = lanes_of(grad_q.shape)
                    work[head, row : row + CHUNK, :128] = jnp.where(lane < 48, grad_q * scale, 0.0).astype(BF16)
                    keep = (lane < 48) | ((lane >= VALUE) & (lane < VALUE + 48))
                    work[head, row : row + CHUNK, 128:] = jnp.where(keep, grad_kv, 0.0).astype(BF16)
        for part in range(out_ref.shape[0]):
            value = nt(place_ref[head], work[head, part * 512 : part * 512 + 512]).astype(BF16)
            out_ref[part] = value if head == 0 else out_ref[part] + value


def to_rows_back(first, dq, du, dkv, x2, place, scale):
    heads, blocks = dq.shape[:2]
    total = blocks * BLOCK
    return pl.pallas_call(
        functools.partial(rows_back_kernel, heads, blocks, scale),
        out_shape=jax.ShapeDtypeStruct((total // 512, place.shape[1], 512), BF16),
        in_specs=[pl.BlockSpec(memory_space=pltpu.SMEM)]
        + [pl.BlockSpec(memory_space=pltpu.VMEM)] * 5,
        out_specs=pl.BlockSpec(memory_space=pltpu.VMEM),
        scratch_shapes=[pltpu.VMEM((heads, total, 256), BF16)] + [pltpu.VMEM(dq.shape, F32)] * 2,
        compiler_params=pltpu.CompilerParams(vmem_limit_bytes=56 * 2**20),
        name="attention_rows_back",
    )(first, dq, du, dkv, x2, place)


def placements(heads):
    full = np.zeros((heads, heads * 144, 256), np.float32)
    narrow = np.zeros((heads, heads * 48, 128), np.float32)
    for head in range(heads):
        for at in range(48):
            full[head, head * 144 + at, at] = 1.0
            full[head, head * 144 + 48 + at, 128 + at] = 1.0
            full[head, head * 144 + 96 + at, 128 + VALUE + at] = 1.0
            narrow[head, head * 48 + at, VALUE + at] = 1.0
    return full.astype(jnp.bfloat16), narrow.astype(jnp.bfloat16)


H = 16
SIZE = 48
eps_norm = 1e-05


def exchange(value, axis, bit):
    count = lax.axis_size(axis)
    return lax.ppermute(value, axis, [(at, at ^ (1 << bit)) for at in range(count)])


def to_major(x):
    rows, width = x.shape
    return x.reshape(rows // 16, 16, width).swapaxes(0, 1).reshape(rows, width)


def from_major(x):
    rows, width = x.shape
    return x.reshape(16, rows // 16, width).swapaxes(0, 1).reshape(rows, width)


def normalize(stream):
    centered = stream - jnp.mean(stream, axis=-1, keepdims=True)
    spread = jnp.mean(centered * centered, axis=-1, keepdims=True)
    scale = lax.rsqrt(spread + eps_norm)
    return centered * scale, scale


def normalize_back(stream, gain, e):
    xhat, scale = normalize(stream)
    dxh = e * gain
    back = scale * (dxh - jnp.mean(dxh, axis=-1, keepdims=True) - xhat * jnp.mean(dxh * xhat, axis=-1, keepdims=True))
    return back, jnp.sum(e * xhat, axis=0), jnp.sum(e, axis=0)


class Task:
    def __init__(self, steps):
        self.steps = steps
        self.pending, self.result, self.done = None, None, False
        self.advance(None)

    def advance(self, value):
        try:
            self.pending = self.steps.send(value)
        except StopIteration as stop:
            self.result, self.pending, self.done = stop.value, None, True


def start(tasks, ins):
    tasks = [task for task in tasks if not task.done]
    operands = [task.pending[0] for task in tasks]
    operands, ins = lax.optimization_barrier((operands, ins))
    flights = [(task, jax.tree.map(lambda v: exchange(v, *task.pending[1:]), operand)) for task, operand in zip(tasks, operands)]
    return flights, ins


def land(flights, outs):
    if flights:
        values, _ = lax.optimization_barrier(([value for _, value in flights], outs))
        for (task, _), value in zip(flights, values):
            task.advance(value)


def gather_far(own2, own3, own4, geometry):
    blocks, same = geometry["blocks"], geometry["same"]
    heads = own2.shape[0]
    if blocks == 2:
        a3 = yield own3, "seq", 1
        a4 = yield jnp.concatenate([own4, a3[:, :, :64]], axis=1), "seq", 2
        r2, b3, b4 = yield (own2, a3, a4), "seq", 0
        r3 = jnp.concatenate([a3, b3], axis=1)
        r4 = jnp.concatenate([a4[:, :2], b4[:, :2], a4[:, 2:], b4[:, 2:]], axis=1)
    else:
        r2 = jnp.concatenate([own2[:, 2:], own2[:, :2]], axis=1)
        r3 = yield own3, "seq", 0
        r4 = yield jnp.concatenate([own4, r3[:, :, :64]], axis=1), "seq", 1
    bias_lane = lanes_of((1, 1, 1, 128)) == BIAS
    r3 = jnp.where(bias_lane & ~same[1], jnp.asarray(NEG, BF16), r3)
    alike = jnp.repeat(jnp.stack([same[2], same[3]]), 4)[None, :, None, None]
    r4 = jnp.where(bias_lane & ~alike, jnp.asarray(NEG, BF16), r4)
    return (
        r2.reshape(heads, blocks // 2, 512, 128),
        r3.reshape(heads, 512, 128),
        r4.reshape(heads, 512, 128),
    )


def return_far(d2, d3, d4, geometry):
    blocks = geometry["blocks"]
    heads = d2.shape[0]

    def fold(d):
        return d[:, 0] if d.shape[1] == 1 else jnp.sum(d.astype(F32), axis=1).astype(BF16)

    def add(a, b):
        return (a.astype(F32) + b.astype(F32)).astype(BF16)

    def grow(d):
        return jnp.concatenate([d, jnp.zeros_like(d)], axis=2)

    d4 = fold(d4).reshape(heads, 8, 64, 128)
    d3 = fold(d3).reshape(heads, 4, 128, 128)
    d2 = d2.reshape(heads, blocks, 256, 128)
    if blocks == 2:
        b4 = jnp.concatenate([d4[:, 2:4], d4[:, 6:8]], axis=1)
        a4 = jnp.concatenate([d4[:, 0:2], d4[:, 4:6]], axis=1)
        x2, y3, y4 = yield (d2, d3[:, 2:], b4), "seq", 0
        x4 = yield add(a4, y4), "seq", 2
        x3 = yield add(add(d3[:, :2], y3), grow(x4[:, 2:])), "seq", 1
        return add(x2, grow(add(x3, grow(x4[:, :2]))))
    x4 = yield d4, "seq", 1
    x3 = yield add(d3, grow(x4[:, 4:])), "seq", 0
    x3 = add(x3, grow(x4[:, :4]))
    x2 = jnp.concatenate([d2[:, 2:], d2[:, :2]], axis=1)
    return add(x2, grow(x3))


def split_groups(value, count):
    return value.reshape(count, -1, value.shape[1])


def join_groups(value):
    return value.reshape(-1, value.shape[2])


def pin(first, then):
    return lax.optimization_barrier((first, then))[1]


def swap(value):
    return lax.all_to_all(value, "branch", split_axis=0, concat_axis=0, tiled=True)


def dot(spec, a, b):
    return jnp.einsum(spec, a, b, preferred_element_type=F32)


def axis_bit(axis, bit):
    return (lax.axis_index(axis) >> bit) & 1


def half(value, axis, which):
    size = value.shape[axis] // 2
    return lax.dynamic_slice_in_dim(value, which * size, size, axis)


def bits_of(axis, low=0):
    return [(axis, bit) for bit in range(low, lax.axis_size(axis).bit_length() - 1)]


def halving_order():
    return bits_of("branch") + bits_of("seq", 1)


def flipped_order():
    return bits_of("branch")[::-1] + bits_of("seq", 1)


def doubling_order(flip, branch_first=False):
    branch = bits_of("branch") if flip else bits_of("branch")[::-1]
    seq = bits_of("seq", 1)[::-1]
    return (branch + seq if branch_first else seq + branch) + [("seq", 0)]


def reduce_product(a, b, order, parts=1):
    core = axis_bit("seq", 0)
    side = axis_bit(*order[0])
    came = yield dot("tm,tn->mn", a, half(b, 1, 1 - core)).astype(BF16), "seq", 0
    mine = half(b, 1, core)
    other = dot("tm,tn->mn", half(a, 1, 1 - side), mine) + half(came, 0, 1 - side)
    size = other.shape[0] // parts
    firsts = []
    for at in range(parts):
        came_part = yield other[at * size : (at + 1) * size].astype(BF16), *order[0]
        firsts.append(came_part)
    first = jnp.concatenate(firsts, axis=0)
    part = dot("tm,tn->mn", half(a, 1, side), mine) + half(came, 0, side) + first
    for axis, bit in order[1:]:
        which = axis_bit(axis, bit)
        came = yield half(part, 0, 1 - which).astype(BF16), axis, bit
        part = half(part, 0, which) + came
    return part.astype(BF16)


def product_halves(a, b, halving):
    core = axis_bit("seq", 0)
    blocks = 1 << len(halving)

    def part(which):
        value = dot("tm,tn->mn", a, half(b, 1, which)).astype(BF16)
        return value.reshape(blocks, -1, value.shape[1])

    return part(1 - core), part(core)


def own_halves(a, b, halving):
    core = axis_bit("seq", 0)
    blocks = 1 << len(halving)

    def part(which):
        value = dot("ktm,knt->mn", half(a, 2, which), b).astype(BF16)
        return value.reshape(blocks, -1, value.shape[1])

    return part(1 - core), part(core)


def reduce_own(a, b, bits):
    core = axis_bit("seq", 0)
    came = yield dot("ktm,knt->mn", half(a, 2, 1 - core), b).astype(BF16), "seq", 0
    part = dot("ktm,knt->mn", half(a, 2, core), b) + came
    for bit in bits:
        which = axis_bit("seq", bit)
        came = yield half(part, 0, 1 - which).astype(BF16), "seq", bit
        part = half(part, 0, which) + came
    return part.astype(BF16)


def finish_kernel(halvings, rounds, done, turns, sizes, *refs):
    fresh, count = len(halvings), len(rounds)
    stages = len(rounds[0])
    steps = [len(halving) for halving in halvings]
    at = 2 * fresh + count - fresh
    sents, mines, pieces = refs[:fresh], refs[fresh : 2 * fresh], refs[2 * fresh : at]
    outs, scratch = refs[at : at + count], list(refs[at + count :])
    own_sem, half_send, half_recv, send_sem, recv_sem = scratch[:5]
    scratch = scratch[5:]
    buffers = []
    for flow in range(fresh):
        first, total, piece = scratch[:3]
        pairs = [(scratch[3 + 2 * step], scratch[4 + 2 * step]) for step in range(steps[flow] - 1)]
        scratch = scratch[1 + 2 * steps[flow] :]
        buffers.append((first, total, piece, pairs))
    index = {axis: lax.axis_index(axis) for axis in sizes}

    def bit_of(axis, bit):
        return lax.rem(index[axis] // (1 << bit), 2)

    def partner(axis, bit):
        return {axis: index[axis] + (1 << bit) * (1 - 2 * bit_of(axis, bit))}

    barrier = pltpu.get_barrier_semaphore()
    for axis, bit in rounds[0]:
        pl.semaphore_signal(barrier, inc=1, device_id=partner(axis, bit), device_id_type=pl.DeviceIdType.MESH)
    slots = []
    for flow in range(count):
        slot = 0
        for stage, (axis, bit) in enumerate(rounds[flow]):
            slot = slot + bit_of(axis, bit) * (1 << stage)
        slots.append(slot)

    def region(flow, stage):
        size = 1 << stage
        return outs[flow].at[pl.ds(slots[flow] // size * size, size)]

    def own(flow, source):
        return pltpu.make_async_copy(source, region(flow, done[flow]), own_sem.at[flow])

    def send(source, target, send, recv, stage):
        copy = pltpu.make_async_remote_copy(
            src_ref=source, dst_ref=target, send_sem=send, recv_sem=recv, device_id=partner(*stage), device_id_type=pl.DeviceIdType.MESH
        )
        copy.start()
        return copy

    owns = {flow: own(flow, pieces[flow - fresh]) for flow in range(fresh, count)}
    for copy in owns.values():
        copy.start()
    pl.semaphore_wait(barrier, stages)
    halves, copies = {}, {}
    place = [0] * fresh

    def reduce_step(flow, step):
        first, total, piece, pairs = buffers[flow]
        if step == 0:
            halves[flow, 0] = send(sents[flow], first, half_send.at[flow, 0], half_recv.at[flow, 0], halvings[flow][0])
            return
        halves[flow, step - 1].wait_recv()
        if step == 1:
            total[...] = mines[flow][...].astype(F32) + first[...].astype(F32)
        else:
            size = pairs[step - 2][1].shape[0]
            kept = pl.ds(place[flow], size)
            total[kept] = total[kept] + pairs[step - 2][1][...].astype(F32)
        if step < steps[flow]:
            sent, came = pairs[step - 1]
            size = sent.shape[0]
            side = bit_of(*halvings[flow][step])
            sent[...] = total[pl.ds(place[flow] + (1 - side) * size, size)].astype(BF16)
            place[flow] = place[flow] + side * size
            halves[flow, step] = send(sent, came, half_send.at[flow, step], half_recv.at[flow, step], halvings[flow][step])
        else:
            piece[...] = total[pl.ds(place[flow], 1)].astype(BF16)
            owns[flow] = own(flow, piece)
            owns[flow].start()

    def gather_step(flow, step):
        stage = done[flow] + step
        if step == 0:
            owns[flow].wait()
        else:
            copies[flow, stage - 1].wait_recv()
        if stage < stages:
            here = region(flow, stage)
            copies[flow, stage] = send(here, here, send_sem.at[flow, stage], recv_sem.at[flow, stage], rounds[flow][stage])

    for turn in range(max(steps) + stages + 1):
        for flow in range(count):
            if flow < fresh:
                if turn <= steps[flow]:
                    reduce_step(flow, turn)
                if 0 <= turn - steps[flow] <= stages:
                    gather_step(flow, turn - steps[flow])
            elif turn in turns:
                gather_step(flow, turns.index(turn))
    for copy in list(halves.values()) + list(copies.values()):
        copy.wait_send()


def finish_everywhere(sents, mines, halvings, pieces, rounds):
    stages = len(rounds[0])
    fresh, count = len(sents), len(rounds)
    shapes = [sent.shape[1:] for sent in sents] + [piece.shape[1:] for piece in pieces]
    kinds = [BF16] * fresh + [piece.dtype for piece in pieces]
    done = [0] * fresh + [piece.shape[0].bit_length() - 1 for piece in pieces]
    branch = len([stage for stage in rounds[0] if stage[0] == "branch"])
    seq = stages - 1 - branch
    turns = list(range(seq + 1)) + [seq + 1 + 2 * at for at in range(1, branch)]
    turns = turns + [max(turns) + 3, max(turns) + 4]
    buffers = []
    for sent, halving in zip(sents, halvings):
        blocks, rows, columns = sent.shape
        buffers += [pltpu.VMEM(sent.shape, BF16), pltpu.VMEM(sent.shape, F32), pltpu.VMEM((1, rows, columns), BF16)]
        for step in range(1, len(halving)):
            buffers += [pltpu.VMEM((blocks >> step, rows, columns), BF16)] * 2
    most = max(len(halving) for halving in halvings)
    return pl.pallas_call(
        functools.partial(finish_kernel, halvings, rounds, done, turns, ("branch", "seq")),
        out_shape=tuple(jax.ShapeDtypeStruct((1 << stages,) + shape, kind) for shape, kind in zip(shapes, kinds)),
        in_specs=[pl.BlockSpec(memory_space=pltpu.VMEM)] * (2 * fresh + len(pieces)),
        out_specs=(pl.BlockSpec(memory_space=pl.ANY),) * count,
        scratch_shapes=[
            pltpu.SemaphoreType.DMA((count,)),
            pltpu.SemaphoreType.DMA((fresh, most)),
            pltpu.SemaphoreType.DMA((fresh, most)),
            pltpu.SemaphoreType.DMA((count, stages)),
            pltpu.SemaphoreType.DMA((count, stages)),
        ]
        + buffers,
        compiler_params=pltpu.CompilerParams(collective_id=0, has_side_effects=True, vmem_limit_bytes=60 * 2**20),
        name="gradient_finish",
    )(*sents, *mines, *pieces)


def columns_kernel(pieces_ref, *refs):
    out_ref = refs[-1]
    count, rows, columns = pieces_ref.shape[2:]
    for core in range(2):
        for at in range(count):
            out_ref[0, at * rows : (at + 1) * rows, core * columns : (core + 1) * columns] = pieces_ref[core, 0, at].astype(F32)


def groups_kernel(groups, branch_first, pieces_ref, *refs):
    out_ref = refs[-1]
    rows, columns = pieces_ref.shape[3:]
    depth = pieces_ref.shape[1 if branch_first else 2]
    for place, group in enumerate(groups):
        for at in range(depth):
            piece = pieces_ref[0, at, place] if branch_first else pieces_ref[0, place, at]
            out_ref[0, at * rows : (at + 1) * rows, group * columns : (group + 1) * columns] = piece.astype(F32)


def write_layer(kernel, name, gathered, block, index, steps, shape, layer, layers, base):
    rows, width = shape
    ins = [pl.BlockSpec(block, index)]
    operands = [gathered]
    aliases = {}
    if base is not None:
        ins.append(pl.BlockSpec(memory_space=pl.ANY))
        operands.append(base)
        aliases = {1: 0}
    return pl.pallas_call(
        kernel,
        grid=(steps,),
        in_specs=ins,
        out_specs=pl.BlockSpec((1, rows // steps, width), lambda at: (layer, at, 0)),
        out_shape=jax.ShapeDtypeStruct((layers, rows, width), F32),
        input_output_aliases=aliases,
        compiler_params=pltpu.CompilerParams(vmem_limit_bytes=48 * 2**20),
        name=name,
    )(*operands)


def branch_places(order):
    stages = [stage for stage in order if stage[0] == "branch"]
    return [stages.index(("branch", bit)) for bit in range(len(stages))]


def write_columns(gathered, order, halving, layer, layers, base):
    pieces, rows, columns = gathered.shape
    places = branch_places(order)
    branch = 1 << len(places)
    seq = pieces // (2 * branch)

    def index(at):
        slot = 0
        for rank, (_, bit) in enumerate(halving[: len(places)]):
            slot = slot + (at // (1 << (len(places) - 1 - rank))) % 2 * (1 << places[bit])
        return 0, slot, 0, 0, 0

    gathered = gathered.reshape(2, branch, seq, rows, columns)
    shape = (branch * seq * rows, 2 * columns)
    return write_layer(columns_kernel, "gradient_columns", gathered, (2, 1, seq, rows, columns), index, branch, shape, layer, layers, base)


def write_groups(gathered, order, layer, layers, base):
    pieces, rows, columns = gathered.shape
    places = branch_places(order)
    branch = 1 << len(places)
    seq = pieces // (2 * branch)
    groups = [sum(((at >> place) & 1) << bit for bit, place in enumerate(places)) for at in range(branch)]
    branch_first = order[0][0] == "branch"
    split = (seq, branch) if branch_first else (branch, seq)
    gathered = gathered.reshape((2,) + split + (rows, columns))
    kernel = functools.partial(groups_kernel, groups, branch_first)
    shape = (2 * seq * rows, branch * columns)
    return write_layer(kernel, "gradient_groups", gathered, (1,) + split + (rows, columns), lambda at: (at, 0, 0, 0, 0), 2, shape, layer, layers, base)


def layer_forward(stream, layer, weights, gain, shift, side, tables, geometry):
    w_in, w_out, w_up, w_down = weights
    first = geometry["first"]
    xhat, _ = normalize(stream)
    normed = (xhat * gain[0] + shift[0]).astype(BF16)
    q, kv, own2, own3, own4, normed_all = prepare(normed, side, geometry["attention_in"], layer, tables["kf"], LOG2E * SIZE**-0.5, geometry["branch"])
    far = Task(gather_far(own2, own3, own4, geometry))
    lower = None
    for part in range(2):
        flights, q = start([far], q)
        lower = lower_forward(q, kv, tables["f0"], tables["f1"], part, 2, lower)
        land(flights, lower)
    while not far.done:
        flights, lower = start([far], lower)
        land(flights, lower)
    r2, r3, r4 = far.result
    att, qb = upper_forward(q, lower, r2, r3, r4, tables["f2"], tables["f3"], tables["f4"])
    saved_parts = (kv, r2, r3, r4, qb, att)
    att_rows = join_groups(to_rows(att, tables["narrow"]))
    midway = stream + dot("ct,cd->td", att_rows, w_out)
    xhat, _ = normalize(midway)
    second = (xhat * gain[1] + shift[1]).astype(BF16)
    pre_act = dot("td,df->tf", second, w_up)
    hidden = (0.5 * pre_act * (1.0 + lax.erf(pre_act * np.float32(2**-0.5)))).astype(BF16)
    result = midway + dot("tf,fd->td", hidden, w_down)
    return result, (stream, normed_all, saved_parts, att_rows, midway, second, pre_act, hidden)


def layer_backward(gradient, saved, weights, gain, shift, tables, geometry, old, flights, last):
    w_in, w_out, w_up, w_down = weights
    stream, normed_all, parts, att_rows, midway, second, pre_act, hidden = saved
    kv, r2, r3, r4, qb, att = parts
    first = geometry["first"]
    halving = halving_order()
    seq_bits = [bit for _, bit in bits_of("seq", 1)]

    down_in = gradient.astype(BF16)
    new, ahead = [], []
    if not last:
        down = Task(reduce_product(hidden, down_in, halving))
        ahead, down_in = start([down], down_in)
    grad_hidden = dot("td,fd->tf", down_in, w_down)
    cdf = 0.5 * (1.0 + lax.erf(pre_act * np.float32(2**-0.5)))
    density = jnp.exp(-0.5 * pre_act * pre_act) * np.float32((2 * np.pi) ** -0.5)
    grad_pre = (grad_hidden * (cdf + pre_act * density)).astype(BF16)
    grad_second = dot("tf,mf->tm", grad_pre, w_up)
    back, gain_two, shift_two = normalize_back(midway, gain[1], grad_second)
    grad_midway = gradient + back
    out_in = grad_midway.astype(BF16)
    grad_rows = split_groups(dot("cd,td->ct", w_out, out_in).astype(BF16), geometry["branch"])
    land(flights + ahead, grad_rows)
    grad_rows, second, att_rows = lax.optimization_barrier((grad_rows, second, att_rows))
    if not last:
        ahead, grad_rows = start([down], grad_rows)
    waiting, grad_rows = start(old, grad_rows)
    rows = swap(grad_rows)
    if last:
        new = [
            product_halves(hidden, down_in, flipped_order()),
            product_halves(second, grad_pre, halving),
            product_halves(att_rows.T, out_in, halving),
        ]
        rows = pin(new, rows)
        ours = []
    else:
        up = Task(reduce_product(second, grad_pre, halving, 2))
        out = Task(reduce_product(att_rows.T, out_in, halving))
        rows = pin([up.pending[0], out.pending[0]], rows)
        new = [down, up, out]
        ours = new
    flights, rows = start(ours[1:], rows)
    g = prepare_back(first, rows, tables["narrow"], att)
    du, d2, d3, d4 = upper_back(qb, g, r2, r3, r4, tables["f2"], tables["f3"], tables["f4"])
    far = Task(return_far(d2, d3, d4, geometry))
    short, _ = start([far], d2)
    land(flights + ahead + waiting, du)
    land(short, d2)
    grads = None
    for part in range(2):
        moving = [task for task in ours + old if part or task is not ours[-1]] if ours else old
        flights, qb = start([far] + moving, qb)
        grads = lower_back(qb, g, kv, tables["f0"], tables["f1"], part, 2, grads)
        land(flights, grads)
    dq, dkv = grads
    flights, dq = start(ours + old, dq)
    back_rows = to_rows_back(first, dq, du, dkv, far.result, tables["full"], SIZE**-0.5)
    returned = swap(back_rows)
    normed_all, back_rows = lax.optimization_barrier((normed_all, back_rows))
    if last:
        enter = own_halves(normed_all, back_rows, bits_of("seq", 1))
        returned = pin(enter, returned)
    else:
        enter = Task(reduce_own(normed_all, back_rows, seq_bits))
        returned = pin(enter.pending[0], returned)
        extra, returned = start([enter], returned)
        flights = flights + extra
    projected = join_groups(returned)
    grad_first = dot("ct,dc->td", projected, w_in)
    back, gain_one, shift_one = normalize_back(stream, gain[0], grad_first)
    vectors = jnp.stack([gain_one, gain_two, shift_one, shift_two])
    return grad_midway + back, vectors, new + [enter], flights


def local(tile_embeddings, tile_valid, slide_bounds, norm_gain, norm_bias, attention_in, attention_out, hidden_up, hidden_down, cotangent):
    branch = lax.axis_size("branch")
    seq = lax.axis_size("seq")
    heads = H // branch
    rows, width = tile_embeddings.shape
    shard = rows * branch
    blocks = shard // BLOCK
    seq_at = lax.axis_index("seq")
    origin = seq_at * shard
    bit = 1 if blocks == 2 else 0

    def slide_at(place):
        return jnp.sum((place >= slide_bounds[1:-1]).astype(jnp.int32))

    def same(mask):
        return slide_at((seq_at ^ mask) * shard) == slide_at(origin)

    low, high = 1 << bit, 2 << bit
    geometry = dict(
        attention_in=attention_in,
        branch=branch,
        blocks=blocks,
        bit=bit,
        first=(lax.axis_index("branch") * heads).astype(jnp.int32).reshape(1),
        same=(None, same(low), same(high), same(high | low)),
    )
    full, narrow = placements(heads)
    tables = dict(
        full=jnp.asarray(full),
        narrow=jnp.asarray(narrow),
        kf=jnp.asarray(key_features()),
        f0=jnp.asarray(query_features(block_classes, 0)),
        f1=jnp.asarray(query_features(block_classes[:512], 1)),
        f2=jnp.asarray(query_features(upper_classes, 2)),
        f3=jnp.asarray(query_features(upper_classes[:256], 3)),
        f4=jnp.asarray(query_features(upper_classes[:128], 4)),
    )
    valid = lax.dynamic_slice_in_dim(tile_valid, origin, shard)
    valid = valid.reshape(branch, rows // 16, 16).swapaxes(1, 2).reshape(shard, 1)
    side = jnp.where((lanes_of((1, 128)) == BIAS) & (valid != 1), NEG, 0.0).astype(BF16)

    layers = attention_in.shape[0]
    weights = [(attention_in[at], attention_out[at], hidden_up[at], hidden_down[at]) for at in range(layers)]
    stream = to_major(tile_embeddings).astype(F32)
    outputs, saved_all = [], []
    for layer in range(layers):
        stream, saved = layer_forward(stream, layer, weights[layer], norm_gain[layer], norm_bias[layer], side, tables, geometry)
        outputs.append(from_major(stream.astype(BF16)))
        saved_all.append(saved)
    gradient = to_major(cotangent).astype(F32)
    vectors = [None] * layers
    tasks, flights = [], []
    first_round, flipped = doubling_order(False), doubling_order(True)
    rounds = [[flipped, first_round, first_round, first_round] for _ in range(layers)]
    rounds[0][3] = flipped
    for layer in reversed(range(layers)):
        gradient, vectors[layer], new, flights = layer_backward(
            gradient, saved_all[layer], weights[layer], norm_gain[layer], norm_bias[layer], tables, geometry, tasks, flights, layer == 0
        )
        if layer:
            tasks = tasks + new
    land(flights, gradient)
    for task in tasks:
        while not task.done:
            task.advance(jax.tree.map(lambda v: exchange(v, *task.pending[1:]), task.pending[0]))
    core = [("seq", 0)]
    halving = halving_order()
    halvings = [core + flipped_order(), core + halving, core + halving, core + bits_of("seq", 1)]
    pieces = [task.result[None] for task in tasks] + [jnp.stack(vectors).reshape(1, -1, width)]
    order = rounds[0] + [order for layer in reversed(range(1, layers)) for order in rounds[layer]] + [first_round]
    gathered = finish_everywhere([sent for sent, _ in new], [mine for _, mine in new], halvings, pieces, order)
    places = [(0, member) for member in range(4)] + [(layer, member) for layer in reversed(range(1, layers)) for member in range(4)]
    vectors = jnp.sum(gathered[-1], axis=0).reshape(layers, 2, 2, width)
    sums = [None] * 4
    for (layer, member), whole in zip(places, gathered[:-1]):
        if member == 3:
            sums[member] = write_groups(whole, rounds[layer][member], layer, layers, sums[member])
        else:
            follows = halvings[member][1:] if layer == 0 else halving
            sums[member] = write_columns(whole, rounds[layer][member], follows, layer, layers, sums[member])
    down, up, out, enter = sums
    return (jnp.stack(outputs), from_major(gradient), vectors[:, 0], vectors[:, 1], enter, out, up, down)


def solution(mesh):
    split = P(("seq", "branch"), None)
    in_specs = (split,) + (P(),) * 8 + (split,)
    out_specs = (P(None, ("seq", "branch"), None), split) + (P(),) * 6
    return jax.shard_map(local, mesh=mesh, in_specs=in_specs, out_specs=out_specs, check_vma=False)
```
